32 devices in a mesh: frame: 8 (over y, x, core), video: 4 (over z).
Axes of the slice: x: 2, y: 2, z: 4, core: 2. Of those that a mesh axis runs over, the one named last changes fastest.
Arguments:
- tokens: bfloat16 [12, 16, 197, 768], P('video', 'frame'), may hold values from -6 to 6
- cotangent: bfloat16 [12, 16, 197, 768], P('video', 'frame'), may hold values from -6 to 6
- msg_weight: bfloat16 [768, 768], replicated, may hold values from -0.21875 to 0.21875
- msg_bias: bfloat16 [768], replicated, may hold values from -1.75 to 1.75
- msg_norm_gain: bfloat16 [768], replicated, may hold values from 0.5 to 1.5
- msg_norm_shift: bfloat16 [768], replicated, may hold values from -1.75 to 1.75
- msg_in_weight: bfloat16 [768, 2304], replicated, may hold values from -0.21875 to 0.21875
- msg_in_bias: bfloat16 [1536], replicated, may hold values from -1.75 to 1.75
- msg_out_weight: bfloat16 [768, 768], replicated, may hold values from -0.4375 to 0.4375
- msg_out_bias: bfloat16 [768], replicated, may hold values from -1.75 to 1.75
- norm1_gain: bfloat16 [768], replicated, may hold values from 0.5 to 1.5
- norm1_shift: bfloat16 [768], replicated, may hold values from -1.75 to 1.75
- attn_in_weight: bfloat16 [768, 2304], replicated, may hold values from -0.21875 to 0.21875
- attn_in_bias: bfloat16 [1536], replicated, may hold values from -1.75 to 1.75
- attn_out_weight: bfloat16 [768, 768], replicated, may hold values from -1.25 to 1.25
- attn_out_bias: bfloat16 [768], replicated, may hold values from -1.75 to 1.75
- norm2_gain: bfloat16 [768], replicated, may hold values from 0.5 to 1.5
- norm2_shift: bfloat16 [768], replicated, may hold values from -1.75 to 1.75
- fc_weight: bfloat16 [768, 3072], replicated, may hold values from -0.21875 to 0.21875
- fc_bias: bfloat16 [3072], replicated, may hold values from -1.75 to 1.75
- proj_weight: bfloat16 [3072, 768], replicated, may hold values from -0.109375 to 0.109375
- proj_bias: bfloat16 [768], replicated, may hold values from -1.75 to 1.75
Outputs:
- output: bfloat16 [12, 16, 197, 768], P('video', 'frame')
- tokens_grad: float32 [12, 16, 197, 768], P('video', 'frame')
- msg_weight_grad: float32 [768, 768], P('frame', 'video')
- msg_bias_grad: float32 [768], P('frame')
- msg_norm_gain_grad: float32 [768], P('frame')
- msg_norm_shift_grad: float32 [768], P('frame')
- msg_in_weight_grad: float32 [768, 2304], P('frame', 'video')
- msg_in_bias_grad: float32 [1536], P('frame')
- msg_out_weight_grad: float32 [768, 768], P('frame', 'video')
- msg_out_bias_grad: float32 [768], P('frame')
- norm1_gain_grad: float32 [768], P('frame')
- norm1_shift_grad: float32 [768], P('frame')
- attn_in_weight_grad: float32 [768, 2304], P('frame', 'video')
- attn_in_bias_grad: float32 [1536], P('frame')
- attn_out_weight_grad: float32 [768, 768], P('frame', 'video')
- attn_out_bias_grad: float32 [768], P('frame')
- norm2_gain_grad: float32 [768], P('frame')
- norm2_shift_grad: float32 [768], P('frame')
- fc_weight_grad: float32 [768, 3072], P('frame', 'video')
- fc_bias_grad: float32 [3072], P('frame')
- proj_weight_grad: float32 [3072, 768], P('frame', 'video')
- proj_bias_grad: float32 [768], P('frame')
The draws below stay inside these ranges and needn't reach their ends.
All inputs are finite; a program needn't handle non-finite values.
Results may differ from the reference program's by a relative error of at most 0.025.
Values may be sent and summed in bfloat16 or wider, within the bound.
A program may use at most 192 MiB of HBM per device.

```python
import jax
import jax.numpy as jnp
from jax import lax

D = 768
HEADS = 12
HEAD_DIM = 64
FF = 3072
PATCHES = 197
FRAMES = 16
VIDEOS = 12


def shard_levels(own_key, dims, split, least, largest):
    loudness, own = 1.0, jax.random.fold_in(own_key, 6)
    for axis_at, shards_of in split:
        draws = jnp.exp(jax.random.uniform(jax.random.fold_in(own, axis_at), (shards_of,), jnp.float32, least / len(split), largest / len(split)))
        loudness = loudness * jnp.repeat(draws, dims[axis_at] // shards_of).reshape([-1 if axis == axis_at else 1 for axis in range(len(dims))])
    return loudness


def noise(own_key, dims, deviation, most, shards=(), held_as=jnp.bfloat16):
    values = jax.random.normal(own_key, dims, jnp.float32) * deviation
    if len(shards) > 0:
        values = shard_levels(own_key, dims, shards, -0.22, 0.18) * values
    return jnp.clip(values, min=-most, max=most).astype(held_as)


def setup_inputs(seed: int = 0) -> dict:
    keys = jax.random.split(jax.random.key(seed), 23)
    return {
        "tokens": noise(keys[0], (VIDEOS, FRAMES, PATCHES, D), 1.0, 6.0, ((0, 4), (1, 8))),
        "cotangent": noise(keys[1], (VIDEOS, FRAMES, PATCHES, D), 1.0, 6.0, ((0, 4), (1, 8))),
        "msg_weight": noise(keys[2], (D, D), D ** -0.5, 0.21875),
        "msg_bias": noise(keys[3], (D,), 0.3, 1.75),
        "msg_norm_gain": jnp.clip(1.0 + 0.1 * jax.random.normal(keys[4], (D,), jnp.float32), 0.5, 1.5).astype(jnp.bfloat16),
        "msg_norm_shift": noise(keys[5], (D,), 0.3, 1.75),
        "msg_in_weight": noise(keys[6], (D, 3 * D), D ** -0.5, 0.21875),
        "msg_in_bias": noise(keys[7], (2 * D,), 0.3, 1.75),
        "msg_out_weight": noise(keys[8], (D, D), (D // 4) ** -0.5, 0.4375),
        "msg_out_bias": noise(keys[9], (D,), 0.3, 1.75),
        "norm1_gain": jnp.clip(1.0 + 0.1 * jax.random.normal(keys[10], (D,), jnp.float32), 0.5, 1.5).astype(jnp.bfloat16),
        "norm1_shift": noise(keys[11], (D,), 0.3, 1.75),
        "attn_in_weight": noise(keys[12], (D, 3 * D), D ** -0.5, 0.21875),
        "attn_in_bias": noise(keys[13], (2 * D,), 0.3, 1.75),
        "attn_out_weight": noise(keys[14], (D, D), (D // 32) ** -0.5, 1.25),
        "attn_out_bias": noise(keys[15], (D,), 0.3, 1.75),
        "norm2_gain": jnp.clip(1.0 + 0.1 * jax.random.normal(keys[16], (D,), jnp.float32), 0.5, 1.5).astype(jnp.bfloat16),
        "norm2_shift": noise(keys[17], (D,), 0.3, 1.75),
        "fc_weight": noise(keys[18], (D, FF), D ** -0.5, 0.21875),
        "fc_bias": noise(keys[19], (FF,), 0.3, 1.75),
        "proj_weight": noise(keys[20], (FF, D), FF ** -0.5, 0.109375),
        "proj_bias": noise(keys[21], (D,), 0.3, 1.75),
    }


@jax.custom_vjp
def low(v):
    return lax.optimization_barrier(v.astype(jnp.bfloat16)).astype(jnp.float32)

@jax.custom_vjp
def low_back(v):
    return v

def low_keep(v):
    return (low(v), None)

def low_pass(kept, grad):
    return (grad,)

def back_keep(v):
    return (v, None)

def back_low(kept, grad):
    return (low(grad),)
low.defvjp(low_keep, low_pass)
low_back.defvjp(back_keep, back_low)

def layer_norm(values, norm_gain, norm_shift):
    centre = values - lax.optimization_barrier(jnp.mean(values, axis=-1, keepdims=True))
    spread = lax.optimization_barrier(jnp.mean(centre * centre, axis=-1, keepdims=True))
    return centre * lax.rsqrt(spread + 1e-05) * norm_gain + norm_shift

def project(values, weight):
    return jnp.einsum('...i,ij->...j', values, weight, precision=lax.Precision.HIGHEST)

def split_heads(values):
    return values.reshape(values.shape[:-1] + (HEADS, HEAD_DIM))

def attend(queries, key_rows, value_rows):
    scaling = HEAD_DIM ** (-0.5)
    scores = jnp.einsum('...qhd,...khd->...hqk', split_heads(queries), split_heads(key_rows), precision=lax.Precision.HIGHEST) * scaling
    scores = low_back(scores)
    attn_probs = jax.nn.softmax(scores, axis=-1)
    mixed_rows = jnp.einsum('...hqk,...khd->...qhd', low(attn_probs), split_heads(value_rows), precision=lax.Precision.HIGHEST)
    return mixed_rows.reshape(queries.shape)

def in_project(normed, weight, biases):
    lowered = low(normed)
    queries = low(low_back(project(lowered, weight[:, :D]) + biases[:D]))
    key_rows = low(low_back(project(lowered, weight[:, D:2 * D])))
    value_rows = low(low_back(project(lowered, weight[:, 2 * D:]) + biases[D:]))
    return (queries, key_rows, value_rows)

def out_project(mixed_rows, weight, biases):
    return low_back(project(low(low_back(mixed_rows)), weight) + biases)

def video_forward(video_rows, params):
    msg_weight, msg_bias, msg_norm_gain, msg_norm_shift, msg_in_weight, msg_in_bias, msg_out_weight, msg_out_bias, norm1_gain, norm1_shift, attn_in_weight, attn_in_bias, attn_out_weight, attn_out_bias, norm2_gain, norm2_shift, fc_weight, fc_bias, proj_weight, proj_bias = params
    message = low_back(project(video_rows[:, 0, :], msg_weight) + msg_bias)
    queries, key_rows, value_rows = in_project(layer_norm(message, msg_norm_gain, msg_norm_shift), msg_in_weight, msg_in_bias)
    message = message + out_project(attend(queries, key_rows, value_rows), msg_out_weight, msg_out_bias)
    joined = jnp.concatenate([video_rows, message[:, None, :]], axis=1)
    queries, key_rows, value_rows = in_project(layer_norm(joined, norm1_gain, norm1_shift), attn_in_weight, attn_in_bias)
    joined = joined + out_project(attend(queries, key_rows, value_rows), attn_out_weight, attn_out_bias)
    kept_rows = joined[:, :PATCHES]
    hidden = low_back(project(low(layer_norm(kept_rows, norm2_gain, norm2_shift)), fc_weight) + fc_bias)
    active = hidden * jax.nn.sigmoid(1.702 * hidden)
    return kept_rows + low_back(project(low(active), proj_weight) + proj_bias)

def reference(tokens, cotangent, msg_weight, msg_bias, msg_norm_gain, msg_norm_shift, msg_in_weight, msg_in_bias, msg_out_weight, msg_out_bias, norm1_gain, norm1_shift, attn_in_weight, attn_in_bias, attn_out_weight, attn_out_bias, norm2_gain, norm2_shift, fc_weight, fc_bias, proj_weight, proj_bias):
    params = tuple((item.astype(jnp.float32) for item in (msg_weight, msg_bias, msg_norm_gain, msg_norm_shift, msg_in_weight, msg_in_bias, msg_out_weight, msg_out_bias, norm1_gain, norm1_shift, attn_in_weight, attn_in_bias, attn_out_weight, attn_out_bias, norm2_gain, norm2_shift, fc_weight, fc_bias, proj_weight, proj_bias)))

    def per_video(totals, video_pair):
        video_rows, grad_rows = video_pair
        result, pullback = jax.vjp(video_forward, video_rows.astype(jnp.float32), params)
        video_grad, param_grads = pullback(grad_rows.astype(jnp.float32))
        totals = jax.tree.map(jnp.add, totals, param_grads)
        return (totals, (result.astype(jnp.bfloat16), video_grad))
    zero_grads = jax.tree.map(jnp.zeros_like, params)
    totals, (output, tokens_grad) = lax.scan(per_video, zero_grads, (tokens, cotangent))
    return (output, tokens_grad, totals[0], totals[1], totals[2], totals[3], totals[4], totals[5], totals[6], totals[7], totals[8], totals[9], totals[10], totals[11], totals[12], totals[13], totals[14], totals[15], totals[16], totals[17], totals[18], totals[19])
```

```python
import functools
import math

import jax
import jax.numpy as jnp
from jax import lax
from jax.experimental import pallas as pl
from jax.experimental.pallas import tpu as pltpu
from jax.sharding import PartitionSpec as P

D = 768
HEADS = 12
PAIRS = 6
FF = 3072
PATCHES = 197
JOINED = 198
ROWS = 208
KEYS = 256
FRAMES = 16
BLOCK = 192
UNITS = 3
BF = jnp.bfloat16
F32 = jnp.float32
MIB = 1 << 20
MESH = pl.DeviceIdType.MESH


def vec(ref, at=0):
    return ref[...].astype(F32).reshape(1, ref.shape[0])[:, at * D : at * D + D]


def dims(a, b, ca, cb):
    return lax.dot_general(a, b, (((ca,), (cb,)), ((), ())), preferred_element_type=F32)


def column_sum(x):
    return jnp.sum(x, axis=0, keepdims=True)


def norm_fwd(x, gain, shift):
    centre = x - jnp.mean(x, axis=-1, keepdims=True)
    inv = lax.rsqrt(jnp.mean(centre * centre, axis=-1, keepdims=True) + 1e-05)
    unit = centre * inv
    return unit * gain + shift, unit, inv


def norm_back(grad, unit, inv, gain):
    scaled = grad * gain
    return inv * (
        scaled
        - jnp.mean(scaled, axis=-1, keepdims=True)
        - unit * jnp.mean(scaled * unit, axis=-1, keepdims=True)
    )


def low_half():
    return lax.broadcasted_iota(jnp.int32, (1, 128), 1) < 64


def half(low, head, value, other):
    return jnp.where(low, value, other) if head == 0 else jnp.where(low, other, value)


def pair_fwd(q, k, v, mask_scores, keep):
    low = low_half()
    sums = []
    for head in range(2):
        scores = mask_scores(dims(q, half(low, head, k, jnp.zeros_like(k)), 1, 1))
        top = jnp.max(scores, axis=1, keepdims=True)
        probs = jnp.exp(scores - top).astype(BF)
        keep(head, probs)
        sums.append(dims(probs, half(low, head, v, jnp.ones_like(v)), 1, 0))
    inv = 1.0 / pltpu.roll(jnp.where(low, sums[1], sums[0]), 64, 1)
    return jnp.where(low, sums[0], sums[1]) * inv, inv


def pair_back(q, k, v, grad, mixed, inv, probs):
    low = low_half()
    scaled = grad * inv
    scaled_low = scaled.astype(BF)
    both = mixed.astype(F32) * scaled
    zero = jnp.zeros_like(both)
    totals = None
    for head in range(2):
        p = probs(head)
        grad_p = dims(scaled_low, half(low, head, v, jnp.zeros_like(v)), 1, 1)
        delta = jnp.sum(half(low, head, both, zero), axis=1, keepdims=True)
        grad_s = (p.astype(F32) * (grad_p - delta)).astype(BF)
        terms = (
            dims(grad_s, half(low, head, k, jnp.zeros_like(k)), 1, 0),
            dims(grad_s, half(low, head, q, jnp.zeros_like(q)), 0, 0),
            dims(p, half(low, head, scaled_low, jnp.zeros_like(scaled_low)), 0, 0),
        )
        totals = terms if totals is None else tuple(a + b for a, b in zip(totals, terms))
    return totals[0] * 0.125, totals[1], totals[2]


def lanes(pair):
    return slice(pair * 128, pair * 128 + 128)


def msg_mask(rows):
    row = lax.broadcasted_iota(jnp.int32, (rows, rows), 0) // FRAMES
    col = lax.broadcasted_iota(jnp.int32, (rows, rows), 1) // FRAMES
    same = row == col
    return lambda scores: jnp.where(same, scores, -1e30)


def msg_forward(cls, biases, w_msg, w_in, w_out):
    bias, gain, shift, in_bias, _ = biases
    message = dims(cls, w_msg[...], 1, 0) + vec(bias)
    normed, unit, inv_std = norm_fwd(message, vec(gain), vec(shift))
    normed = normed.astype(BF)
    qkv = dims(normed, w_in[...], 1, 0)
    q = ((qkv[:, :D] + vec(in_bias)) * 0.125).astype(BF)
    k = qkv[:, D : 2 * D].astype(BF)
    v = (qkv[:, 2 * D :] + vec(in_bias, 1)).astype(BF)
    mask = msg_mask(cls.shape[0])
    mixed, invs, probs = [], [], {}
    for pair in range(PAIRS):
        sl = lanes(pair)

        def keep(head, p, pair=pair):
            probs[pair, head] = p

        out, inv = pair_fwd(q[:, sl], k[:, sl], v[:, sl], mask, keep)
        mixed.append(out.astype(BF))
        invs.append(inv)
    mixed_all = jnp.concatenate(mixed, axis=1)
    return dict(
        message=message, normed=normed, unit=unit, inv_std=inv_std, q=q, k=k, v=v,
        mixed=mixed, invs=invs, probs=probs, mixed_all=mixed_all,
    )


class Place:
    def __init__(self, frame_size, video_size):
        self.F, self.V = frame_size, video_size
        self.f, self.v = lax.axis_index("frame"), lax.axis_index("video")
        self.core = lax.rem(self.f, 2)
        self.bits = [lax.rem(lax.div(self.f, 1 << i), 2) for i in range(int(math.log2(frame_size)))]

    def frame_peer(self, step):
        return {"frame": lax.rem(self.f + step, self.F)}

    def video_peer(self, step):
        return {"video": lax.rem(self.v + step, self.V)}

    def greet(self):
        barrier = pltpu.get_barrier_semaphore()
        for step in range(1, self.F):
            pl.semaphore_signal(barrier, inc=1, device_id=self.frame_peer(step), device_id_type=MESH)
        for step in range(1, self.V):
            pl.semaphore_signal(barrier, inc=1, device_id=self.video_peer(step), device_id_type=MESH)
        pl.semaphore_wait(barrier, self.F + self.V - 2)


def remote(src, dst, send, recv, peer):
    return pltpu.make_async_remote_copy(
        src_ref=src, dst_ref=dst, send_sem=send, recv_sem=recv, device_id=peer, device_id_type=MESH
    )


class Gather:
    def __init__(self, place, own, rows, send, recv):
        self.place, self.own, self.rows, self.send, self.recv = place, own, rows, send, recv

    def near_copy(self, step, arriving):
        place = self.place
        frame = lax.rem(place.f + place.F - step, place.F) if arriving else place.f
        return remote(
            self.own, self.rows.at[place.v, :, frame], self.send.at[0, step], self.recv.at[0, step], place.frame_peer(step)
        )

    def far_copy(self, hop, arriving):
        place = self.place
        video = lax.rem(place.v + place.V - hop, place.V) if arriving else place.v
        slot = place.F - 1 + hop
        return remote(
            self.own, self.rows.at[video, :, place.f], self.send.at[0, slot], self.recv.at[0, slot], place.video_peer(hop)
        )

    def passed_copy(self, hop, step, arriving):
        place = self.place
        video = lax.rem(place.v + place.V - hop, place.V)
        frame = lax.rem(place.f + place.F - step, place.F) if arriving else place.f
        part = self.rows.at[video, :, frame]
        return remote(part, part, self.send.at[hop, step], self.recv.at[hop, step], place.frame_peer(step))

    def start(self):
        for step in range(1, self.place.F):
            self.near_copy(step, False).start()
        for hop in range(1, self.place.V):
            self.far_copy(hop, False).start()

    def near(self):
        for step in range(1, self.place.F):
            self.near_copy(step, True).wait_recv()

    def forward(self):
        for hop in range(1, self.place.V):
            self.far_copy(hop, True).wait_recv()
            for step in range(1, self.place.F):
                self.passed_copy(hop, step, False).start()

    def finish(self):
        for hop in range(1, self.place.V):
            for step in range(1, self.place.F):
                self.passed_copy(hop, step, True).wait_recv()
        for step in range(1, self.place.F):
            self.near_copy(step, False).wait_send()
        for hop in range(1, self.place.V):
            self.far_copy(hop, False).wait_send()
            for step in range(1, self.place.F):
                self.passed_copy(hop, step, False).wait_send()


def msg_fwd_kernel(
    frame_size, video_size, frames_here, videos_here,
    x_hbm, bias, gain, shift, in_bias, out_bias, w_msg_hbm, w_in_hbm, w_out_hbm,
    out_ref, cls_ref,
    own, rows, wide, mixed_out, w_msg, w_in, w_out, send, recv, local,
):
    place = Place(frame_size, video_size)
    loads = [
        pltpu.make_async_copy(x_hbm.at[:, 0], own, local.at[0]),
        pltpu.make_async_copy(x_hbm.at[:, 0], rows.at[place.v, :, place.f], local.at[1]),
        pltpu.make_async_copy(w_msg_hbm, w_msg, local.at[2]),
        pltpu.make_async_copy(w_in_hbm, w_in, local.at[3]),
        pltpu.make_async_copy(w_out_hbm, w_out, local.at[4]),
    ]
    for load in loads:
        load.start()
    place.greet()
    gather = Gather(place, own, rows, send, recv)
    loads[0].wait()
    gather.start()
    loads[1].wait()
    gather.near()
    gather.forward()
    count = videos_here * FRAMES

    def unpack(video):
        for i in range(videos_here):
            for f in range(frame_size):
                at = (i * frame_size + f) * frames_here
                wide[at : at + frames_here, :] = rows[video, i, f].astype(F32)

    unpack(place.v)
    for load in loads[2:]:
        load.wait()
    biases = (bias, gain, shift, in_bias, out_bias)
    state = msg_forward(wide[...].astype(BF), biases, w_msg, w_in, w_out)
    mixed_out[...] = state["message"] + dims(state["mixed_all"], w_out[...], 1, 0) + vec(out_bias)
    for i in range(videos_here):
        for j in range(frames_here):
            out_ref[i * frames_here + j] = mixed_out[pl.ds(i * FRAMES + place.f * frames_here + j, 1), :]
    gather.finish()
    for video in range(video_size):
        unpack(video)
        cls_ref[video * count : video * count + count, :] = wide[...].astype(BF)


def attn_fwd_kernel(
    frames_here,
    x_ref, msg_ref, gain, shift, in_bias, out_bias, w_in, w_out,
    q_ref, k_ref, v_ref, p_ref, inv_ref, mixed_ref, kept_ref, normed_ref,
    joined,
):
    x = x_ref[0].astype(F32)
    for j in range(frames_here):
        joined[j, 0:PATCHES, :] = x[:, j, :]
        joined[j, PATCHES:ROWS, :] = jnp.zeros((ROWS - PATCHES, D), F32)
        joined[j, PATCHES : PATCHES + 1, :] = msg_ref[j]
    valid = lax.broadcasted_iota(jnp.int32, (1, KEYS - 128), 1) < JOINED - 128

    def mask(scores):
        return jnp.concatenate([scores[:, :128], jnp.where(valid, scores[:, 128:], -1e30)], axis=1)

    @pl.loop(0, frames_here)
    def _(j):
        normed, _, _ = norm_fwd(joined[j], vec(gain), vec(shift))
        normed_ref[j] = normed.astype(BF)
        normed = normed_ref[j]
        pad = jnp.zeros((KEYS - ROWS, 128), BF)
        q = ((dims(normed, w_in[:, :D], 1, 0) + vec(in_bias)) * 0.125).astype(BF)
        k = dims(normed, w_in[:, D : 2 * D], 1, 0).astype(BF)
        v = (dims(normed, w_in[:, 2 * D :], 1, 0) + vec(in_bias, 1)).astype(BF)
        for pair in range(PAIRS):
            sl = lanes(pair)
            q_ref[j, pair] = q[:, sl]
            k_ref[j, pair, 0:ROWS] = k[:, sl]
            k_ref[j, pair, ROWS:KEYS] = pad
            v_ref[j, pair, 0:ROWS] = v[:, sl]
            v_ref[j, pair, ROWS:KEYS] = pad
        for pair in range(PAIRS):

            def keep(head, p, pair=pair):
                p_ref[j, pair, :, head * KEYS : head * KEYS + KEYS] = p

            out, inv = pair_fwd(q_ref[j, pair], k_ref[j, pair], v_ref[j, pair], mask, keep)
            inv_ref[j, pair] = inv
            mixed_ref[j, :, lanes(pair)] = out.astype(BF)
        kept_ref[j] = joined[j] + dims(mixed_ref[j], w_out[...], 1, 0) + vec(out_bias)


def mlp_kernel(
    frame_size, videos_here, frames_here,
    kept_ref, cot_ref, gain, shift, fc_bias, proj_bias, fc, proj,
    out_ref, grad_ref, fc_grad, proj_grad, sums,
    wide, normed2, cot2, act, grad_h, out_acc, grad_acc, bias_rows,
):
    chunk = pl.program_id(0)
    frames = videos_here * frames_here

    def rows_of(b):
        return pl.ds(pl.multiple_of(b * ROWS, ROWS), ROWS)

    @pl.when(chunk == 0)
    def _():
        sums[...] = jnp.zeros_like(sums)
        wide[:, PATCHES:ROWS, :] = jnp.zeros((frames_here, ROWS - PATCHES, D), F32)
        for part in range(FF // D):
            bias_rows[part : part + 1, :] = vec(fc_bias, part)

        @pl.loop(0, videos_here)
        def _(i):
            cot = cot_ref[i].astype(F32)
            for j in range(frames_here):
                wide[j, 0:PATCHES, :] = cot[:, j, :]
            for j in range(frames_here):
                b = i * frames_here + j
                cot_j = wide[j]
                cot2[rows_of(b), :] = cot_j.astype(BF)
                sums[6:7, :] += column_sum(cot_j)
                normed, _, _ = norm_fwd(kept_ref[b], vec(gain), vec(shift))
                normed2[rows_of(b), :] = normed.astype(BF)
                out_acc[rows_of(b), :] = kept_ref[b] + vec(proj_bias)
                grad_acc[rows_of(b), :] = jnp.zeros((ROWS, D), F32)

    bias = bias_rows[pl.ds(chunk, 1), :]

    @pl.loop(0, frames)
    def _(b):
        rows = rows_of(b)
        hidden = dims(normed2[rows, :], fc[...], 1, 0) + bias
        grad_a = dims(cot2[rows, :], proj[...], 1, 1)
        gate = 0.5 * jnp.tanh(0.851 * hidden) + 0.5
        active = hidden * gate
        grad = (grad_a * (gate + 1.702 * active * (1.0 - gate))).astype(BF)
        active = active.astype(BF)
        act[rows, :] = active
        grad_h[rows, :] = grad
        sums[pl.ds(2 + chunk, 1), :] += column_sum(grad.astype(F32))
        out_acc[rows, :] += dims(active, proj[...], 1, 0)
        grad_acc[rows, :] += dims(grad, fc[...], 1, 1)

    step = D // frame_size // UNITS
    grad = dims(act[...], cot2[...], 0, 0).astype(BF).reshape(frame_size // 8, 2, UNITS, 4, step, D)
    for u in range(UNITS):
        for part in range(4):
            proj_grad[u, :, :, :, part * D : part * D + D] = grad[:, :, u, part]
    grad = dims(normed2[...], grad_h[...], 0, 0).astype(BF).reshape(frame_size // 2, 2, UNITS, step, D)
    for u in range(UNITS):
        fc_grad[u] = grad[:, :, u]

    @pl.when(chunk == pl.num_programs(0) - 1)
    def _():
        @pl.loop(0, videos_here)
        def _(i):
            outs = [out_acc[rows_of(i * frames_here + j), :][:PATCHES] for j in range(frames_here)]
            out_ref[i] = jnp.stack(outs, axis=1).astype(BF)

        @pl.loop(0, frames)
        def _(b):
            rows = rows_of(b)
            _, unit, inv = norm_fwd(kept_ref[b], vec(gain), vec(shift))
            grad = grad_acc[rows, :]
            sums[0:1, :] += column_sum(grad * unit)
            sums[1:2, :] += column_sum(grad)
            grad_ref[b] = norm_back(grad, unit, inv, vec(gain)) + cot2[rows, :].astype(F32)


class Scatter:
    def __init__(self, place, step, acc, recv0, recv_bits, send3, recv3, result, sems):
        self.place, self.step, self.acc = place, step, acc
        self.recv0, self.recv_bits, self.send3, self.recv3, self.result = recv0, recv_bits, send3, recv3, result
        self.sems = sems
        self.n_bits = len(place.bits) - 1

    def other_core(self):
        return {"frame": self.place.f + 1 - 2 * self.place.core}

    def exchange0(self, unit, source):
        return remote(source, self.recv0.at[unit], self.sems["send0"].at[unit], self.sems["recv0"].at[unit], self.other_core())

    def order(self, core, stage):
        return stage if core == 0 else self.n_bits - 1 - stage

    def blocks(self, stage, flip):
        place, n = self.place, self.n_bits
        free = n - 1 - stage
        out = []
        for i in range(1 << free):
            both = []
            for core in range(2):
                done = [self.order(core, s) for s in range(stage)]
                now = self.order(core, stage)
                rest = [bit for bit in range(n) if bit not in done and bit != now]
                at = 0
                for bit in done:
                    at = at + place.bits[bit + 1] * (1 << bit)
                own = place.bits[now + 1]
                at = at + ((1 - own) if flip else own) * (1 << now)
                for index, bit in enumerate(rest):
                    at = at + ((i >> index) & 1) * (1 << bit)
                both.append(at)
            out.append((1 - place.core) * both[0] + place.core * both[1])
        return out

    def partner(self, stage):
        place = self.place
        moves = []
        for core in range(2):
            bit = self.order(core, stage) + 1
            moves.append((1 - 2 * place.bits[bit]) * (1 << bit))
        return {"frame": place.f + (1 - place.core) * moves[0] + place.core * moves[1]}

    def exchange(self, unit, stage, i, block):
        sems = self.sems
        return remote(
            self.acc(unit, block), self.recv_bits[stage].at[unit, i],
            sems["send_bits"].at[unit, stage, i], sems["recv_bits"].at[unit, stage, i], self.partner(stage),
        )

    def add(self, unit, block, came):
        target = self.acc(unit, block)
        target[...] = (target[...].astype(F32) + came.astype(F32)).astype(BF)

    def stage(self, unit, stage):
        if stage == 0:
            self.exchange0(unit, self.recv0.at[unit]).wait_recv()
            came = lambda position, block: self.recv0[unit, block]
        else:
            for i in range(1 << (self.n_bits - stage)):
                self.exchange(unit, stage - 1, i, 0).wait_recv()
            came = lambda position, block: self.recv_bits[stage - 1][unit, position]
        if stage == self.n_bits:
            block = self.own_block()
            self.add(unit, block, came(0, block))
            return
        sending, staying = self.blocks(stage, True), self.blocks(stage, False)
        where = self.positions(stage)
        for i, block in enumerate(sending):
            self.add(unit, block, came(where[1][i], block))
            self.exchange(unit, stage, i, block).start()
        for i, block in enumerate(staying):
            self.add(unit, block, came(where[0][i], block))

    def positions(self, stage):
        place, n = self.place, self.n_bits
        if stage == 0:
            return [[None] * (1 << (n - 1))] * 2
        out = [[], []]
        for flip in range(2):
            for i in range(1 << (n - 1 - stage)):
                both = []
                for core in range(2):
                    done = [self.order(core, s) for s in range(stage)]
                    now = self.order(core, stage)
                    rest_before = [bit for bit in range(n) if bit not in done]
                    rest = [bit for bit in rest_before if bit != now]
                    own = place.bits[now + 1]
                    at = 0
                    for index, bit in enumerate(rest_before):
                        if bit == now:
                            at = at + ((1 - own) if flip else own) * (1 << index)
                        else:
                            at = at + ((i >> rest.index(bit)) & 1) * (1 << index)
                    both.append(at)
                out[flip].append((1 - place.core) * both[0] + place.core * both[1])
        return out

    def own_block(self):
        return lax.div(self.place.f, 2)

    def parts(self, kind, x, w):
        V = self.place.V
        if kind == 0:
            size = FF // V
            return x[:, w * size : w * size + size]
        if kind == 1:
            size = D // V
            return jnp.concatenate([x[:, q * D + w * size : q * D + w * size + size] for q in range(4)], axis=1)
        size, last = 3 * D // V, D // V
        return jnp.concatenate(
            [x[:, w * size : w * size + size], x[:, 3 * D + w * last : 3 * D + w * last + last]], axis=1
        )

    def across(self, unit, hop):
        place, sems = self.place, self.sems
        to = lax.rem(place.v + hop, place.V)
        return remote(
            self.send3.at[unit, to], self.recv3.at[unit, hop],
            sems["send3"].at[unit, hop], sems["recv3"].at[unit, hop], place.video_peer(hop),
        )

    def stage_video(self, unit, kinds):
        self.stage(unit, self.n_bits)
        x = self.acc(unit, self.own_block())

        def fill(kind):
            value = x[...].astype(F32)
            for w in range(self.place.V):
                self.send3[unit, w] = self.parts(kind, value, w).astype(BF)

        if isinstance(kinds, int):
            fill(kinds)
        else:
            for kind, condition in kinds:
                pl.when(condition)(functools.partial(fill, kind))
        for hop in range(1, self.place.V):
            self.across(unit, hop).start()

    def finish(self, unit):
        total = self.send3[unit, self.place.v].astype(F32)
        for hop in range(1, self.place.V):
            self.across(unit, hop).wait_recv()
            total = total + self.recv3[unit, hop].astype(F32)
        self.result[unit] = total

    def drain(self, unit, source):
        self.exchange0(unit, source).wait_send()
        for stage in range(self.n_bits):
            for i in range(1 << (self.n_bits - 1 - stage)):
                self.exchange(unit, stage, i, 0).wait_send()
        for hop in range(1, self.place.V):
            self.across(unit, hop).wait_send()


class Totals:
    def __init__(self, place, which, own, near, middle, far, result, sems):
        self.place, self.which, self.own, self.near_buf, self.middle = place, which, own, near, middle
        self.far_buf, self.result, self.sems = far, result, sems

    def near(self, step):
        sems = self.sems
        return remote(
            self.own, self.near_buf.at[self.which, step], sems["vec_send"].at[self.which, 0, step],
            sems["vec_recv"].at[self.which, 0, step], self.place.frame_peer(step),
        )

    def far(self, hop):
        sems = self.sems
        return remote(
            self.middle.at[self.which], self.far_buf.at[self.which, hop], sems["vec_send"].at[self.which, 1, hop],
            sems["vec_recv"].at[self.which, 1, hop], self.place.video_peer(hop),
        )

    def start(self):
        for step in range(1, self.place.F):
            self.near(step).start()

    def forward(self):
        total = self.own[...]
        for step in range(1, self.place.F):
            self.near(step).wait_recv()
            total = total + self.near_buf[self.which, step]
        self.middle[self.which] = total
        for hop in range(1, self.place.V):
            self.far(hop).start()

    def finish(self):
        total = self.middle[self.which]
        for hop in range(1, self.place.V):
            self.far(hop).wait_recv()
            total = total + self.far_buf[self.which, hop]
        self.result[self.which] = total
        for step in range(1, self.place.F):
            self.near(step).wait_send()
        for hop in range(1, self.place.V):
            self.far(hop).wait_send()


def attn_back_kernel(
    frame_size, video_size, videos_here, frames_here,
    x_ref, msg_ref, gk_ref, gain, shift, w_in, w_out, mlp_sums, fc_grad, proj_grad,
    q_ref, k_ref, v_ref, p_ref, inv_ref, mixed_ref, normed_ref,
    tg_ref, gm_ref, reduced_ref, totals_ref,
    joined, staged, gqkv_all, sums, gm_wide, gm_own, gm_rows, wide,
    acc_mlp, acc_attn, recv0, recv_a, recv_b, recv_c, send3, recv3,
    vec_near, vec_mid, vec_far,
    s_local, s_staged, s_send0, s_recv0, s_sendb, s_recvb, s_send3, s_recv3, s_vsend, s_vrecv, s_gsend, s_grecv,
):
    frames = videos_here * frames_here
    b = pl.program_id(0)
    place = Place(frame_size, video_size)
    step = D // frame_size // UNITS
    sems = dict(
        send0=s_send0, recv0=s_recv0, send_bits=s_sendb, recv_bits=s_recvb, send3=s_send3, recv3=s_recv3,
        vec_send=s_vsend, vec_recv=s_vrecv,
    )

    def acc(unit, block):
        if isinstance(unit, int) and unit >= 2 * UNITS:
            return acc_attn.at[0, unit - 2 * UNITS, block]
        return acc_mlp.at[unit, block]

    scatter = Scatter(place, step, acc, recv0, [recv_a, recv_b, recv_c], send3, recv3, reduced_ref, sems)
    early = Totals(place, 0, mlp_sums, vec_near, vec_mid, vec_far, totals_ref, sems)
    late = Totals(place, 1, sums, vec_near, vec_mid, vec_far, totals_ref, sems)
    gather = Gather(place, gm_own, gm_rows, s_gsend, s_grecv)

    def mlp_source(unit, core):
        return (fc_grad if unit < UNITS else proj_grad).at[unit % UNITS, :, core]

    def local(unit, source=None):
        source = recv0.at[unit] if source is None else source
        return pltpu.make_async_copy(source, acc_mlp.at[unit], s_local.at[unit])

    def begin(unit):
        local(unit).wait()
        scatter.stage(unit, 0)

    @pl.when(b == 0)
    def _():
        place.greet()
        sums[...] = jnp.zeros_like(sums)
        for unit in range(2 * UNITS):
            scatter.exchange0(unit, mlp_source(unit, 1 - place.core)).start()
            local(unit, mlp_source(unit, place.core)).start()
        early.start()

    rows = pl.ds(pl.multiple_of(b * ROWS, ROWS), ROWS)
    gk_low = gk_ref[b].astype(BF)
    sums[0:1, :] += column_sum(gk_low.astype(F32))
    grad_mixed = dims(gk_low, w_out[...], 1, 1)

    def run_pairs(pairs):
        for pair in pairs:
            grads = pair_back(
                q_ref[0, pair], k_ref[0, pair], v_ref[0, pair], grad_mixed[:, lanes(pair)],
                mixed_ref[b, :, lanes(pair)], inv_ref[0, pair],
                lambda head, pair=pair: p_ref[0, pair, :, head * KEYS : head * KEYS + KEYS],
            )
            for kind in range(3):
                gqkv_all[rows, kind * D + pair * 128 : kind * D + pair * 128 + 128] = grads[kind][:ROWS].astype(BF)

    n_bits = scatter.n_bits
    units = 2 * UNITS

    def kinds(unit):
        return unit // UNITS if isinstance(unit, int) else ((0, unit < UNITS), (1, unit >= UNITS))

    def actions(at, first):
        if first:
            return [(at, begin)]
        due = []
        for stage in range(1, n_bits):
            due.append((at - stage, lambda unit, stage=stage: scatter.stage(unit, stage)))
        due.append((at - n_bits, lambda unit: scatter.stage_video(unit, kinds(unit))))
        due.append((at - n_bits - 1, scatter.finish))
        return due

    def tick(at, first):
        for unit, call in actions(at, first):
            if isinstance(unit, int):
                if 0 <= unit < units:
                    call(unit)
            else:
                pl.when(jnp.logical_and(unit >= 0, unit < units))(functools.partial(call, unit))

    tick(b, True)
    run_pairs(range(PAIRS // 2))
    tick(b, False)
    run_pairs(range(PAIRS // 2, PAIRS))
    gqkv = gqkv_all[rows, :]
    sums[1:2, :] += column_sum(gqkv[:, :D].astype(F32))
    sums[2:3, :] += column_sum(gqkv[:, 2 * D :].astype(F32))

    @pl.when(b == frames - 1)
    def _():
        last = 16
        at = JOINED - 1 - (JOINED - 1) % 16
        gm_grad = []
        for c in range(frames):
            piece = dims(gqkv_all[c * ROWS + at : c * ROWS + at + last, :], w_in[...], 1, 1)
            gm_grad.append(piece[PATCHES - at : PATCHES - at + 1])
        for c in range(frames):
            gm_wide[c : c + 1, :] = gm_grad[c]
        for c in range(frames):
            joined[c : c + 1, :] = msg_ref[c]
        msg = joined[0:frames, :]
        grad = gm_wide[0:frames, :]
        _, unit, inv = norm_fwd(msg, vec(gain), vec(shift))
        gm_wide[0:frames, :] = norm_back(grad, unit, inv, vec(gain))
        for i in range(videos_here):
            gm_own[i] = gm_wide[i * frames_here : i * frames_here + frames_here, :].astype(BF)
            gm_rows[place.v, i, place.f] = gm_own[i]
        gather.start()
        early.forward()

        def attn_unit(value, lo, hi):
            value = value.astype(BF).reshape(frame_size // 2, 2, UNITS, step, hi - lo)
            for u in range(UNITS):
                for core in range(2):
                    acc_attn[lax.rem(core + place.core, 2), u, :, :, lo:hi] = value[:, core, u]

        gk_low = jnp.concatenate([gk_ref[c].astype(BF) for c in range(frames)], axis=0)
        attn_unit(dims(mixed_ref[...].reshape(frames * ROWS, D), gk_low, 0, 0), 3 * D, 4 * D)
        gather.forward()
        at = frames
        for kind in range(3):
            tick(at, True)
            tick(at, False)
            at += 1
            attn_unit(dims(normed_ref[...].reshape(frames * ROWS, D), gqkv_all[:, kind * D : kind * D + D], 0, 0), kind * D, kind * D + D)
        for u in range(UNITS):
            scatter.exchange0(2 * UNITS + u, acc_attn.at[1, u]).start()
        while at < units + n_bits + 1:
            tick(at, True)
            tick(at, False)
            at += 1
        early.finish()

        def put(i, j):
            return pltpu.make_async_copy(staged.at[j], tg_ref.at[i, :, j], s_staged.at[j])

        def norm_frames(lo, hi):
            @pl.loop(lo, hi)
            def _(i):
                x = x_ref[i].astype(F32)
                for j in range(frames_here):
                    c = i * frames_here + j
                    joined[0:PATCHES, :] = x[:, j, :]
                    joined[PATCHES:ROWS, :] = jnp.zeros((ROWS - PATCHES, D), F32)
                    joined[PATCHES : PATCHES + 1, :] = msg_ref[c]
                    _, unit, inv = norm_fwd(joined[...], vec(gain), vec(shift))
                    rows = pl.ds(pl.multiple_of(c * ROWS, ROWS), ROWS)
                    grad = dims(gqkv_all[rows, :], w_in[...], 1, 1)
                    sums[3:4, :] += column_sum(grad * unit)
                    sums[4:5, :] += column_sum(grad)
                    pl.when(i > 0)(lambda j=j: put(i - 1, j).wait())
                    staged[j] = (gk_ref[c] + norm_back(grad, unit, inv, vec(gain)))[:PATCHES]
                    put(i, j).start()

        attn_units = range(2 * UNITS, 3 * UNITS)
        norm_frames(0, 1)
        for unit in attn_units:
            scatter.stage(unit, 0)
        norm_frames(1, videos_here)
        late.start()
        gather.near()
        for stage in range(1, n_bits):
            for unit in attn_units:
                scatter.stage(unit, stage)
        late.forward()
        for unit in attn_units:
            scatter.stage_video(unit, 2)
        gather.finish()
        for video in range(video_size):
            for i in range(videos_here):
                for f in range(frame_size):
                    at_row = (i * frame_size + f) * frames_here
                    wide[at_row : at_row + frames_here, :] = gm_rows[video, i, f].astype(F32)
            count = videos_here * FRAMES
            gm_ref[video * count : video * count + count, :] = wide[...].astype(BF)
        late.finish()
        for j in range(frames_here):
            put(videos_here - 1, j).wait()
        for unit in attn_units:
            scatter.finish(unit)
        for unit in range(2 * UNITS):
            scatter.drain(unit, mlp_source(unit, 1 - place.core))
        for unit in attn_units:
            scatter.drain(unit, acc_attn.at[1, unit - 2 * UNITS])


def msg_back_kernel(
    frame_size, video_size, videos_here, frames_here,
    cls_ref, gm_ref, bias, gain, shift, in_bias, out_bias, w_msg, w_in, w_out, reduced, totals, tg_hbm,
    tokens_grad, msg_grad, in_grad, out_grad, *rest,
):
    (
        msg_bias_g, msg_gain_g, msg_shift_g, msg_in_bias_g, msg_out_bias_g, gain1_g, shift1_g,
        attn_in_g, attn_in_bias_g, attn_out_g, attn_out_bias_g, gain2_g, shift2_g, fc_g, fc_bias_g, proj_g, proj_bias_g,
        tg, cls_grad, acc_msg, acc_in, acc_out, sums, sem,
    ) = rest
    block = pl.program_id(0)
    f, v = lax.axis_index("frame"), lax.axis_index("video")
    own_rows = D // frame_size
    padded = -(-own_rows // 128) * 128

    def load():
        return pltpu.make_async_copy(tg_hbm, tg, sem.at[0])

    def store():
        return pltpu.make_async_copy(tg, tokens_grad, sem.at[1])

    @pl.when(block == 0)
    def _():
        load().start()
        for ref in (sums, acc_msg, acc_in, acc_out):
            ref[...] = jnp.zeros_like(ref)

    def own_columns(x):
        return pltpu.roll(x.astype(F32), lax.rem(D - f * own_rows, D), 1)[:, :padded].astype(BF)

    biases = (bias, gain, shift, in_bias, out_bias)
    cls = cls_ref[...]
    gm = gm_ref[...]
    state = msg_forward(cls, biases, w_msg, w_in, w_out)
    acc_out[...] += dims(own_columns(state["mixed_all"]), gm, 0, 0)
    sums[5:6, :] += column_sum(gm.astype(F32))
    grad_mixed = dims(gm, w_out[...], 1, 1)
    parts = ([], [], [])
    for pair in range(PAIRS):
        sl = lanes(pair)
        grads = pair_back(
            state["q"][:, sl], state["k"][:, sl], state["v"][:, sl], grad_mixed[:, sl],
            state["mixed"][pair], state["invs"][pair],
            lambda head, pair=pair: state["probs"][pair, head],
        )
        for kind in range(3):
            parts[kind].append(grads[kind].astype(BF))
    gqkv = jnp.concatenate(parts[0] + parts[1] + parts[2], axis=1)
    acc_in[...] += dims(own_columns(state["normed"]), gqkv, 0, 0)
    sums[3:4, :] += column_sum(gqkv[:, :D].astype(F32))
    sums[4:5, :] += column_sum(gqkv[:, 2 * D :].astype(F32))
    grad = dims(gqkv, w_in[...], 1, 1)
    sums[1:2, :] += column_sum(grad * state["unit"])
    sums[2:3, :] += column_sum(grad)
    grad_message = norm_back(grad, state["unit"], state["inv_std"], vec(gain)) + gm.astype(F32)
    grad_message = grad_message.astype(BF)
    acc_msg[...] += dims(own_columns(cls), grad_message, 0, 0)
    sums[0:1, :] += column_sum(grad_message.astype(F32))
    cls_grad[pl.ds(pl.multiple_of(block * BLOCK, BLOCK), BLOCK), :] = dims(grad_message, w_msg[...], 1, 1)

    @pl.when(block == pl.num_programs(0) - 1)
    def _():
        load().wait()
        for i in range(videos_here):
            base = (v * videos_here + i) * FRAMES + f * frames_here
            added = [cls_grad[pl.ds(base + j, 1), :] for j in range(frames_here)]
            tg[i, 0] = tg[i, 0] + jnp.concatenate(added, axis=0)
        store().start()

        def own_matrix(target, x):
            size = x.shape[1] // video_size
            target[...] = pltpu.roll(x[:own_rows], lax.rem(x.shape[1] - v * size, x.shape[1]), 1)[:, :size]

        own_matrix(msg_grad, acc_msg[...])
        own_matrix(in_grad, acc_in[...])
        own_matrix(out_grad, acc_out[...])

        def own_vector(target, ref, first, count):
            size = count * D // frame_size
            per_row = frame_size // count
            row = first + lax.div(f, per_row)
            x = ref[pl.ds(row, 1), :]
            x = pltpu.roll(jnp.broadcast_to(x, (8, D)), lax.rem(D - lax.rem(f, per_row) * size, D), 1)
            target[...] = x[0:1, :size].reshape(size)

        for target, first, count in (
            (msg_bias_g, 0, 1), (msg_gain_g, 1, 1), (msg_shift_g, 2, 1), (msg_in_bias_g, 3, 2), (msg_out_bias_g, 5, 1),
        ):
            own_vector(target, sums, first, count)
        mlp_sums, attn_sums = totals.at[0], totals.at[1]
        for target, ref, first, count in (
            (gain1_g, attn_sums, 3, 1), (shift1_g, attn_sums, 4, 1), (attn_in_bias_g, attn_sums, 1, 2),
            (attn_out_bias_g, attn_sums, 0, 1), (gain2_g, mlp_sums, 0, 1), (shift2_g, mlp_sums, 1, 1),
            (fc_bias_g, mlp_sums, 2, 4), (proj_bias_g, mlp_sums, 6, 1),
        ):
            own_vector(target, ref, first, count)
        step = own_rows // UNITS
        columns = D // video_size
        for u in range(UNITS):
            rows = slice(u * step, u * step + step)
            fc_g[rows, :] = reduced[u]
            attn_in_g[rows, :] = reduced[2 * UNITS + u][:, : 3 * columns]
            attn_out_g[rows, :] = reduced[2 * UNITS + u][:, 3 * columns :]
        proj = [reduced[UNITS + u][:, q * columns : q * columns + columns] for u in range(UNITS) for q in range(4)]
        proj_g[...] = jnp.concatenate(proj, axis=0).T
        store().wait()


def shaped(shape, dtype):
    return jax.ShapeDtypeStruct(shape, dtype)


def whole(array):
    shape = array.shape
    return pl.BlockSpec(shape, lambda *_: (0,) * len(shape), pipeline_mode=pl.Buffered(1))


def wholes(*arrays):
    return [whole(array) for array in arrays]


def in_hbm():
    return pl.BlockSpec(memory_space=pl.ANY)


def in_vmem():
    return pl.BlockSpec(memory_space=pltpu.VMEM)


def per_step(count, shape):
    return pl.BlockSpec((count,) + shape, lambda b: (b,) + (0,) * len(shape))


def params(mib, **more):
    return pltpu.CompilerParams(vmem_limit_bytes=mib * MIB, **more)


def on_device(frame_size, video_size, *args):
    (
        tokens, cotangent, msg_weight, msg_bias, msg_norm_gain, msg_norm_shift, msg_in_weight,
        msg_in_bias, msg_out_weight, msg_out_bias, norm1_gain, norm1_shift, attn_in_weight,
        attn_in_bias, attn_out_weight, attn_out_bias, norm2_gain, norm2_shift, fc_weight, fc_bias,
        proj_weight, proj_bias,
    ) = args
    videos_here, frames_here = tokens.shape[:2]
    frames = videos_here * frames_here
    msgs = videos_here * video_size * FRAMES
    group = videos_here * FRAMES
    total = frames * ROWS
    F, V = frame_size, video_size
    step = D // F // UNITS
    n_bits = int(math.log2(F)) - 1
    x = tokens.transpose(0, 2, 1, 3)
    cot = cotangent.transpose(0, 2, 1, 3)
    msg_vectors = (msg_bias, msg_norm_gain, msg_norm_shift, msg_in_bias, msg_out_bias)
    DMA = pltpu.SemaphoreType.DMA

    msg_out, cls = pl.pallas_call(
        functools.partial(msg_fwd_kernel, F, V, frames_here, videos_here),
        in_specs=[in_hbm()] + [in_vmem()] * 5 + [in_hbm()] * 3,
        out_specs=[in_vmem()] * 2,
        out_shape=[shaped((frames, 1, D), F32), shaped((msgs, D), BF)],
        scratch_shapes=[
            pltpu.VMEM((videos_here, frames_here, D), BF),
            pltpu.VMEM((V, videos_here, F, frames_here, D), BF),
            pltpu.VMEM((group, D), F32), pltpu.VMEM((group, D), F32),
            pltpu.VMEM((D, D), BF), pltpu.VMEM((D, 3 * D), BF), pltpu.VMEM((D, D), BF),
            DMA((V, F + V)), DMA((V, F + V)), DMA((5,)),
        ],
        compiler_params=params(40, collective_id=1, has_side_effects=True),
        name="msg_fwd",
    )(x, *msg_vectors, msg_weight, msg_in_weight, msg_out_weight)

    q, k, v, p, inv, mixed, kept, normed = pl.pallas_call(
        functools.partial(attn_fwd_kernel, frames_here),
        grid=(videos_here,),
        in_specs=[per_step(1, (PATCHES, frames_here, D)), per_step(frames_here, (1, D))]
        + wholes(norm1_gain, norm1_shift, attn_in_bias, attn_out_bias, attn_in_weight, attn_out_weight),
        out_specs=[
            per_step(frames_here, shape) for shape in (
                (PAIRS, ROWS, 128), (PAIRS, KEYS, 128), (PAIRS, KEYS, 128), (PAIRS, ROWS, 2 * KEYS),
                (PAIRS, ROWS, 128), (ROWS, D), (ROWS, D), (ROWS, D),
            )
        ],
        out_shape=[
            shaped((frames, PAIRS, ROWS, 128), BF), shaped((frames, PAIRS, KEYS, 128), BF),
            shaped((frames, PAIRS, KEYS, 128), BF), shaped((frames, PAIRS, ROWS, 2 * KEYS), BF),
            shaped((frames, PAIRS, ROWS, 128), F32), shaped((frames, ROWS, D), BF),
            shaped((frames, ROWS, D), F32), shaped((frames, ROWS, D), BF),
        ],
        scratch_shapes=[pltpu.VMEM((frames_here, ROWS, D), F32)],
        compiler_params=params(56),
        name="attn_fwd",
    )(x, msg_out, norm1_gain, norm1_shift, attn_in_bias, attn_out_bias, attn_in_weight, attn_out_weight)

    chunks = FF // D
    unit_shape = (UNITS, F // 2, 2, step, FF)
    output, grad_kept, fc_grad, proj_grad, mlp_sums = pl.pallas_call(
        functools.partial(mlp_kernel, F, videos_here, frames_here),
        grid=(chunks,),
        in_specs=wholes(kept, cot, norm2_gain, norm2_shift, fc_bias, proj_bias)
        + [pl.BlockSpec((D, D), lambda c: (0, c)), pl.BlockSpec((D, D), lambda c: (c, 0))],
        out_specs=[
            whole(x), whole(kept),
            pl.BlockSpec((UNITS, F // 2, 2, step, D), lambda c: (0, 0, 0, 0, c)),
            pl.BlockSpec((UNITS, F // 8, 2, step, FF), lambda c: (0, c, 0, 0, 0)),
            pl.BlockSpec((8, D), lambda c: (0, 0)),
        ],
        out_shape=[
            shaped(x.shape, BF), shaped(kept.shape, F32), shaped(unit_shape, BF), shaped(unit_shape, BF), shaped((8, D), F32),
        ],
        scratch_shapes=[
            pltpu.VMEM((frames_here, ROWS, D), F32),
            pltpu.VMEM((total, D), BF), pltpu.VMEM((total, D), BF), pltpu.VMEM((total, D), BF), pltpu.VMEM((total, D), BF),
            pltpu.VMEM((total, D), F32), pltpu.VMEM((total, D), F32), pltpu.VMEM((chunks, D), F32),
        ],
        compiler_params=params(58),
        name="mlp",
    )(kept, cot, norm2_gain, norm2_shift, fc_bias, proj_bias, fc_weight, proj_weight)

    all_units = 3 * UNITS
    tg, gm, reduced, totals = pl.pallas_call(
        functools.partial(attn_back_kernel, F, V, videos_here, frames_here),
        grid=(frames,),
        in_specs=wholes(x, msg_out, grad_kept, norm1_gain, norm1_shift, attn_in_weight, attn_out_weight, mlp_sums)
        + [in_hbm(), in_hbm()]
        + [
            per_step(1, shape) for shape in (
                (PAIRS, ROWS, 128), (PAIRS, KEYS, 128), (PAIRS, KEYS, 128), (PAIRS, ROWS, 2 * KEYS),
                (PAIRS, ROWS, 128),
            )
        ]
        + wholes(mixed, normed),
        out_specs=[in_hbm()] + wholes(
            cls, shaped((all_units, step, FF // V), F32), shaped((2, 8, D), F32),
        ),
        out_shape=[
            shaped(x.shape, F32), shaped((msgs, D), BF), shaped((all_units, step, FF // V), F32), shaped((2, 8, D), F32),
        ],
        scratch_shapes=[
            pltpu.VMEM((ROWS, D), F32), pltpu.VMEM((frames_here, PATCHES, D), F32),
            pltpu.VMEM((total, 3 * D), BF), pltpu.VMEM((8, D), F32), pltpu.VMEM((8, D), F32),
            pltpu.VMEM((videos_here, frames_here, D), BF), pltpu.VMEM((V, videos_here, F, frames_here, D), BF),
            pltpu.VMEM((group, D), F32),
            pltpu.VMEM((2 * UNITS, F // 2, step, FF), BF), pltpu.VMEM((2, UNITS, F // 2, step, FF), BF),
            pltpu.VMEM((all_units, F // 2, step, FF), BF),
        ]
        + [pltpu.VMEM((all_units, max(1, F >> (2 + i)), step, FF), BF) if i < n_bits else pltpu.VMEM((1, 1, 16, 128), BF) for i in range(3)]
        + [
            pltpu.VMEM((all_units, V, step, FF // V), BF), pltpu.VMEM((all_units, V, step, FF // V), BF),
            pltpu.VMEM((2, F, 8, D), F32), pltpu.VMEM((2, 8, D), F32), pltpu.VMEM((2, V, 8, D), F32),
            DMA((2 * UNITS,)), DMA((frames_here,)), DMA((all_units,)), DMA((all_units,)),
            DMA((all_units, n_bits, F // 4)), DMA((all_units, n_bits, F // 4)),
            DMA((all_units, V)), DMA((all_units, V)),
            DMA((2, 2, max(F, V))), DMA((2, 2, max(F, V))), DMA((V, F + V)), DMA((V, F + V)),
        ],
        compiler_params=params(63, collective_id=2, has_side_effects=True),
        name="attn_back",
    )(
        x, msg_out, grad_kept, norm1_gain, norm1_shift, attn_in_weight, attn_out_weight, mlp_sums, fc_grad, proj_grad,
        q, k, v, p, inv, mixed, normed,
    )

    rows_own, columns = D // F, D // V
    out_shapes = [
        (rows_own, columns), (rows_own, 3 * columns), (rows_own, columns),
        (rows_own,), (rows_own,), (rows_own,), (2 * rows_own,), (rows_own,), (rows_own,), (rows_own,),
        (rows_own, 3 * columns), (2 * rows_own,), (rows_own, columns), (rows_own,), (rows_own,), (rows_own,),
        (rows_own, 4 * columns), (4 * rows_own,), (columns, 4 * rows_own), (rows_own,),
    ]
    out_shapes = [shaped(shape, F32) for shape in out_shapes]
    padded = -(-rows_own // 128) * 128
    block = pl.BlockSpec((BLOCK, D), lambda i: (i, 0))
    (
        tokens_grad, msg_grad, msg_in_grad, msg_out_grad,
        msg_bias_g, msg_gain_g, msg_shift_g, msg_in_bias_g, msg_out_bias_g, gain1_g, shift1_g,
        attn_in_g, attn_in_bias_g, attn_out_g, attn_out_bias_g, gain2_g, shift2_g, fc_g, fc_bias_g, proj_g, proj_bias_g,
    ) = pl.pallas_call(
        functools.partial(msg_back_kernel, F, V, videos_here, frames_here),
        grid=(msgs // BLOCK,),
        in_specs=[block, block] + wholes(*msg_vectors, msg_weight, msg_in_weight, msg_out_weight, reduced, totals) + [in_hbm()],
        out_specs=[in_hbm()] + wholes(*out_shapes),
        out_shape=[shaped(x.shape, F32)] + out_shapes,
        scratch_shapes=[
            pltpu.VMEM(x.shape, F32), pltpu.VMEM((msgs, D), F32),
            pltpu.VMEM((padded, D), F32), pltpu.VMEM((padded, 3 * D), F32), pltpu.VMEM((padded, D), F32),
            pltpu.VMEM((8, D), F32), DMA((2,)),
        ],
        compiler_params=params(58),
        name="msg_back",
    )(cls, gm, *msg_vectors, msg_weight, msg_in_weight, msg_out_weight, reduced, totals, tg)

    return (
        output.transpose(0, 2, 1, 3), tokens_grad.transpose(0, 2, 1, 3),
        msg_grad, msg_bias_g, msg_gain_g, msg_shift_g, msg_in_grad, msg_in_bias_g, msg_out_grad, msg_out_bias_g,
        gain1_g, shift1_g, attn_in_g, attn_in_bias_g, attn_out_g, attn_out_bias_g,
        gain2_g, shift2_g, fc_g, fc_bias_g, proj_g.T, proj_bias_g,
    )


def solution(mesh):
    rows = P("video", "frame", None, None)
    matrix, vector = P("frame", "video"), P("frame")
    out_specs = (
        rows, rows,
        matrix, vector, vector, vector, matrix, vector, matrix, vector,
        vector, vector, matrix, vector, matrix, vector,
        vector, vector, matrix, vector, matrix, vector,
    )
    return jax.shard_map(
        functools.partial(on_device, mesh.shape["frame"], mesh.shape["video"]),
        mesh=mesh, in_specs=(rows, rows) + (P(),) * 20, out_specs=out_specs, check_vma=False,
    )
```

```python
import functools
import math

import jax
import jax.numpy as jnp
from jax import lax
from jax.experimental import pallas as pl
from jax.experimental.pallas import tpu as pltpu
from jax.sharding import PartitionSpec as P

D = 768
HEADS = 12
PAIRS = 6
FF = 3072
PATCHES = 197
JOINED = 198
ROWS = 208
KEYS = 256
FRAMES = 16
BLOCK = 192
UNITS = 3
BF = jnp.bfloat16
F32 = jnp.float32
MIB = 1 << 20
MESH = pl.DeviceIdType.MESH


def vec(ref, at=0):
    return ref[...].astype(F32).reshape(1, ref.shape[0])[:, at * D : at * D + D]


def dims(a, b, ca, cb):
    return lax.dot_general(a, b, (((ca,), (cb,)), ((), ())), preferred_element_type=F32)


def column_sum(x):
    return jnp.sum(x, axis=0, keepdims=True)


def norm_fwd(x, gain, shift):
    centre = x - jnp.mean(x, axis=-1, keepdims=True)
    inv = lax.rsqrt(jnp.mean(centre * centre, axis=-1, keepdims=True) + 1e-05)
    unit = centre * inv
    return unit * gain + shift, unit, inv


def norm_back(grad, unit, inv, gain):
    scaled = grad * gain
    return inv * (
        scaled
        - jnp.mean(scaled, axis=-1, keepdims=True)
        - unit * jnp.mean(scaled * unit, axis=-1, keepdims=True)
    )


def low_half():
    return lax.broadcasted_iota(jnp.int32, (1, 128), 1) < 64


def half(low, head, value, other):
    return jnp.where(low, value, other) if head == 0 else jnp.where(low, other, value)


def pair_fwd(q, k, v, mask_scores, keep):
    low = low_half()
    sums = []
    for head in range(2):
        scores = mask_scores(dims(q, half(low, head, k, jnp.zeros_like(k)), 1, 1))
        top = jnp.max(scores, axis=1, keepdims=True)
        probs = jnp.exp(scores - top).astype(BF)
        keep(head, probs)
        sums.append(dims(probs, half(low, head, v, jnp.ones_like(v)), 1, 0))
    inv = 1.0 / pltpu.roll(jnp.where(low, sums[1], sums[0]), 64, 1)
    return jnp.where(low, sums[0], sums[1]) * inv, inv


def pair_back(q, k, v, grad, mixed, inv, probs):
    low = low_half()
    scaled = grad * inv
    scaled_low = scaled.astype(BF)
    both = mixed.astype(F32) * scaled
    zero = jnp.zeros_like(both)
    totals = None
    for head in range(2):
        p = probs(head)
        grad_p = dims(scaled_low, half(low, head, v, jnp.zeros_like(v)), 1, 1)
        delta = jnp.sum(half(low, head, both, zero), axis=1, keepdims=True)
        grad_s = (p.astype(F32) * (grad_p - delta)).astype(BF)
        terms = (
            dims(grad_s, half(low, head, k, jnp.zeros_like(k)), 1, 0),
            dims(grad_s, half(low, head, q, jnp.zeros_like(q)), 0, 0),
            dims(p, half(low, head, scaled_low, jnp.zeros_like(scaled_low)), 0, 0),
        )
        totals = terms if totals is None else tuple(a + b for a, b in zip(totals, terms))
    return totals[0] * 0.125, totals[1], totals[2]


def lanes(pair):
    return slice(pair * 128, pair * 128 + 128)


def msg_mask(rows):
    row = lax.broadcasted_iota(jnp.int32, (rows, rows), 0) // FRAMES
    col = lax.broadcasted_iota(jnp.int32, (rows, rows), 1) // FRAMES
    same = row == col
    return lambda scores: jnp.where(same, scores, -1e30)


def msg_scratch(rows):
    return [
        pltpu.VMEM((rows, 3 * D), BF), pltpu.VMEM((HEADS, rows, rows), BF), pltpu.VMEM((rows, D), F32), pltpu.VMEM((rows, D), BF),
        pltpu.VMEM((rows, D), BF), pltpu.VMEM((rows, D), F32),
    ]


def pair_lanes(pair, kind=0):
    return pl.ds(pl.multiple_of(kind * D + pair * 128, 128), 128)


def msg_forward(cls, biases, w_msg, w_in, w_out, scratch, unroll):
    bias, gain, shift, in_bias, _ = biases
    qkv, probs, invs, mixed, normed_low, message = scratch
    message[...] = dims(cls, w_msg[...], 1, 0) + vec(bias)
    normed, unit, inv_std = norm_fwd(message[...], vec(gain), vec(shift))
    normed_low[...] = normed.astype(BF)

    def project(kind, bias, scale):
        columns = slice(kind * D, kind * D + D)
        qkv[:, columns] = ((dims(normed_low[...], w_in[:, columns], 1, 0) + bias) * scale).astype(BF)

    project(0, vec(in_bias), 0.125)
    project(1, 0.0, 1.0)
    project(2, vec(in_bias, 1), 1.0)
    mask = msg_mask(cls.shape[0])

    @pl.loop(0, PAIRS, unroll=unroll)
    def _(pair):
        def keep(head, p):
            probs[2 * pair + head] = p

        out, inv = pair_fwd(qkv[:, pair_lanes(pair)], qkv[:, pair_lanes(pair, 1)], qkv[:, pair_lanes(pair, 2)], mask, keep)
        mixed[:, pair_lanes(pair)] = out.astype(BF)
        invs[:, pair_lanes(pair)] = inv

    return unit, inv_std


class Place:
    def __init__(self, frame_size, video_size):
        self.F, self.V = frame_size, video_size
        self.f, self.v = lax.axis_index("frame"), lax.axis_index("video")
        self.core = lax.rem(self.f, 2)
        self.bits = [lax.rem(lax.div(self.f, 1 << i), 2) for i in range(int(math.log2(frame_size)))]

    def frame_peer(self, step):
        return {"frame": lax.rem(self.f + step, self.F)}

    def video_peer(self, step):
        return {"video": lax.rem(self.v + step, self.V)}

    def greet(self):
        self.announce()
        self.meet()

    def announce(self):
        barrier = pltpu.get_barrier_semaphore()

        @pl.loop(1, self.F)
        def _(step):
            pl.semaphore_signal(barrier, inc=1, device_id=self.frame_peer(step), device_id_type=MESH)

        @pl.loop(1, self.V)
        def _(step):
            pl.semaphore_signal(barrier, inc=1, device_id=self.video_peer(step), device_id_type=MESH)

    def meet(self):
        pl.semaphore_wait(pltpu.get_barrier_semaphore(), self.F + self.V - 2)


def remote(src, dst, send, recv, peer):
    return pltpu.make_async_remote_copy(
        src_ref=src, dst_ref=dst, send_sem=send, recv_sem=recv, device_id=peer, device_id_type=MESH
    )


class Gather:
    def __init__(self, place, own, rows, send, recv):
        self.place, self.own, self.rows, self.send, self.recv = place, own, rows, send, recv

    def near_copy(self, step, arriving):
        place = self.place
        frame = lax.rem(place.f + place.F - step, place.F) if arriving else place.f
        return remote(
            self.own, self.rows.at[place.v, :, frame], self.send.at[0, step], self.recv.at[0, step], place.frame_peer(step)
        )

    def far_copy(self, hop, arriving):
        place = self.place
        video = lax.rem(place.v + place.V - hop, place.V) if arriving else place.v
        slot = place.F - 1 + hop
        return remote(
            self.own, self.rows.at[video, :, place.f], self.send.at[0, slot], self.recv.at[0, slot], place.video_peer(hop)
        )

    def passed_copy(self, hop, step, arriving):
        place = self.place
        video = lax.rem(place.v + place.V - hop, place.V)
        frame = lax.rem(place.f + place.F - step, place.F) if arriving else place.f
        part = self.rows.at[video, :, frame]
        return remote(part, part, self.send.at[hop, step], self.recv.at[hop, step], place.frame_peer(step))

    def each_frame(self, call):
        pl.loop(1, self.place.F)(call)

    def each_video(self, call):
        pl.loop(1, self.place.V)(call)

    def start(self, far=True):
        self.each_frame(lambda step: self.near_copy(step, False).start())
        self.each_video(lambda hop: self.far_copy(hop, False).start())

    def near(self):
        self.each_frame(lambda step: self.near_copy(step, True).wait_recv())

    def forward(self):
        @pl.loop(1, self.place.V)
        def _(hop):
            self.far_copy(hop, True).wait_recv()
            self.each_frame(lambda step: self.passed_copy(hop, step, False).start())

    def finish(self):
        @pl.loop(1, self.place.V)
        def _(hop):
            def passed(step):
                self.passed_copy(hop, step, True).wait_recv()
                self.passed_copy(hop, step, False).wait_send()

            self.each_frame(passed)
            self.far_copy(hop, False).wait_send()

        self.each_frame(lambda step: self.near_copy(step, False).wait_send())


def msg_fwd_kernel(
    frame_size, video_size, frames_here, videos_here,
    x_hbm, *rest,
):
    operands, (out_ref, cls_ref, own, rows, wide, mixed_out), rest = rest[:8], rest[8:14], rest[14:]
    kept, scratch, (send, recv, local) = rest[:8], rest[8:14], rest[14:]
    bias, gain, shift, in_bias, out_bias, w_msg, w_in, w_out = kept
    place = Place(frame_size, video_size)
    place.announce()
    loads = [
        pltpu.make_async_copy(x_hbm.at[:, 0], own, local.at[0]),
        pltpu.make_async_copy(x_hbm.at[:, 0], rows.at[place.v, :, place.f], local.at[1]),
    ]
    loads += [pltpu.make_async_copy(a, b, local.at[2 + i]) for i, (a, b) in enumerate(zip(operands, kept))]
    for load in loads:
        load.start()
    place.meet()
    gather = Gather(place, own, rows, send, recv)
    loads[0].wait()
    gather.start()
    loads[1].wait()
    gather.near()
    gather.forward()
    count = videos_here * FRAMES

    def unpack(video):
        for i in range(videos_here):
            for f in range(frame_size):
                at = (i * frame_size + f) * frames_here
                wide[at : at + frames_here, :] = rows[video, i, f].astype(F32)

    unpack(place.v)
    for load in loads[2:]:
        load.wait()
    biases = (bias, gain, shift, in_bias, out_bias)
    msg_forward(wide[...].astype(BF), biases, w_msg, w_in, w_out, scratch, PAIRS)
    mixed_out[...] = scratch[5][...] + dims(scratch[3][...], w_out[...], 1, 0) + vec(out_bias)
    for i in range(videos_here):
        for j in range(frames_here):
            out_ref[i * frames_here + j] = mixed_out[pl.ds(i * FRAMES + place.f * frames_here + j, 1), :]
    gather.finish()
    for video in range(video_size):
        unpack(video)
        cls_ref[video * count : video * count + count, :] = wide[...].astype(BF)


def attn_fwd_kernel(
    frames_here,
    x_ref, msg_ref, gain, shift, in_bias, out_bias, w_in, w_out,
    q_ref, k_ref, v_ref, p_ref, inv_ref, mixed_ref, kept_ref, normed_ref,
    joined,
):
    x = x_ref[0].astype(F32)
    for j in range(frames_here):
        joined[j, 0:PATCHES, :] = x[:, j, :]
        joined[j, PATCHES:ROWS, :] = jnp.zeros((ROWS - PATCHES, D), F32)
        joined[j, PATCHES : PATCHES + 1, :] = msg_ref[j]
    valid = lax.broadcasted_iota(jnp.int32, (1, KEYS - 128), 1) < JOINED - 128

    def mask(scores):
        return jnp.concatenate([scores[:, :128], jnp.where(valid, scores[:, 128:], -1e30)], axis=1)

    every = frames_here * ROWS
    normed, _, _ = norm_fwd(joined[...].reshape(every, D), vec(gain), vec(shift))
    normed_ref[...] = normed.astype(BF).reshape(frames_here, ROWS, D)
    normed = normed_ref[...].reshape(every, D)
    pad = jnp.zeros((KEYS - ROWS, 128), BF)
    q = ((dims(normed, w_in[:, :D], 1, 0) + vec(in_bias)) * 0.125).astype(BF)
    k = dims(normed, w_in[:, D : 2 * D], 1, 0).astype(BF)
    v = (dims(normed, w_in[:, 2 * D :], 1, 0) + vec(in_bias, 1)).astype(BF)
    for j in range(frames_here):
        rows = slice(j * ROWS, j * ROWS + ROWS)
        for pair in range(PAIRS):
            sl = lanes(pair)
            q_ref[j, pair] = q[rows, sl]
            k_ref[j, pair, 0:ROWS] = k[rows, sl]
            k_ref[j, pair, ROWS:KEYS] = pad
            v_ref[j, pair, 0:ROWS] = v[rows, sl]
            v_ref[j, pair, ROWS:KEYS] = pad

    @pl.loop(0, frames_here)
    def _(j):
        for pair in range(PAIRS):

            def keep(head, p, pair=pair):
                p_ref[j, pair, :, head * KEYS : head * KEYS + KEYS] = p

            out, inv = pair_fwd(q_ref[j, pair], k_ref[j, pair], v_ref[j, pair], mask, keep)
            inv_ref[j, pair] = inv
            mixed_ref[j, :, lanes(pair)] = out.astype(BF)

    kept = joined[...].reshape(every, D) + dims(mixed_ref[...].reshape(every, D), w_out[...], 1, 0) + vec(out_bias)
    kept_ref[...] = kept.reshape(frames_here, ROWS, D)


class Scatter:
    def __init__(self, place, step, acc, recv0, recv_bits, send3, recv3, result, sems, first=0):
        self.place, self.step, self.acc, self.first = place, step, acc, first
        self.recv0, self.recv_bits, self.send3, self.recv3, self.result = recv0, recv_bits, send3, recv3, result
        self.sems = sems
        self.n_bits = len(place.bits) - 1

    def other_core(self):
        return {"frame": self.place.f + 1 - 2 * self.place.core}

    def exchange0(self, unit, source):
        return remote(source, self.recv0.at[unit - self.first], self.sems["send0"].at[unit], self.sems["recv0"].at[unit], self.other_core())

    def order(self, core, stage):
        return stage if core == 0 else self.n_bits - 1 - stage

    def blocks(self, stage, flip):
        place, n = self.place, self.n_bits
        free = n - 1 - stage
        out = []
        for i in range(1 << free):
            both = []
            for core in range(2):
                done = [self.order(core, s) for s in range(stage)]
                now = self.order(core, stage)
                rest = [bit for bit in range(n) if bit not in done and bit != now]
                at = 0
                for bit in done:
                    at = at + place.bits[bit + 1] * (1 << bit)
                own = place.bits[now + 1]
                at = at + ((1 - own) if flip else own) * (1 << now)
                for index, bit in enumerate(rest):
                    at = at + ((i >> index) & 1) * (1 << bit)
                both.append(at)
            out.append((1 - place.core) * both[0] + place.core * both[1])
        return out

    def partner(self, stage):
        place = self.place
        moves = []
        for core in range(2):
            bit = self.order(core, stage) + 1
            moves.append((1 - 2 * place.bits[bit]) * (1 << bit))
        return {"frame": place.f + (1 - place.core) * moves[0] + place.core * moves[1]}

    def exchange(self, unit, stage, i, block):
        sems = self.sems
        return remote(
            self.acc(unit, block), self.recv_bits[stage].at[unit - self.first, i],
            sems["send_bits"].at[unit, stage, i], sems["recv_bits"].at[unit, stage, i], self.partner(stage),
        )

    def add(self, unit, block, came):
        target = self.acc(unit, block)
        target[...] = (target[...].astype(F32) + came.astype(F32)).astype(BF)

    def stage(self, unit, stage):
        if stage == 0:
            self.exchange0(unit, self.recv0.at[unit - self.first]).wait_recv()
            came = lambda position, block: self.recv0[unit - self.first, block]
        else:
            for i in range(1 << (self.n_bits - stage)):
                self.exchange(unit, stage - 1, i, 0).wait_recv()
            came = lambda position, block: self.recv_bits[stage - 1][unit - self.first, position]
        if stage == self.n_bits:
            block = self.own_block()
            self.add(unit, block, came(0, block))
            return
        sending, staying = self.blocks(stage, True), self.blocks(stage, False)
        where = self.positions(stage)
        for i, block in enumerate(sending):
            self.add(unit, block, came(where[1][i], block))
            self.exchange(unit, stage, i, block).start()
        for i, block in enumerate(staying):
            self.add(unit, block, came(where[0][i], block))

    def positions(self, stage):
        place, n = self.place, self.n_bits
        if stage == 0:
            return [[None] * (1 << (n - 1))] * 2
        out = [[], []]
        for flip in range(2):
            for i in range(1 << (n - 1 - stage)):
                both = []
                for core in range(2):
                    done = [self.order(core, s) for s in range(stage)]
                    now = self.order(core, stage)
                    rest_before = [bit for bit in range(n) if bit not in done]
                    rest = [bit for bit in rest_before if bit != now]
                    own = place.bits[now + 1]
                    at = 0
                    for index, bit in enumerate(rest_before):
                        if bit == now:
                            at = at + ((1 - own) if flip else own) * (1 << index)
                        else:
                            at = at + ((i >> rest.index(bit)) & 1) * (1 << index)
                    both.append(at)
                out[flip].append((1 - place.core) * both[0] + place.core * both[1])
        return out

    def own_block(self):
        return lax.div(self.place.f, 2)

    def parts(self, kind, x, w):
        V = self.place.V
        if kind == 0:
            size, width = FF // UNITS // V, FF // UNITS
            return jnp.concatenate([x[:, q * width + w * size : q * width + w * size + size] for q in range(UNITS)], axis=1)
        if kind == 1:
            size = D // V
            return jnp.concatenate([x[:, q * D + w * size : q * D + w * size + size] for q in range(4)], axis=1)
        size, last = 3 * D // V, D // V
        return jnp.concatenate(
            [x[:, w * size : w * size + size], x[:, 3 * D + w * last : 3 * D + w * last + last]], axis=1
        )

    def across(self, unit, hop):
        place, sems = self.place, self.sems
        to = lax.rem(place.v + hop, place.V)
        return remote(
            self.send3.at[unit, to], self.recv3.at[unit, hop],
            sems["send3"].at[unit, hop], sems["recv3"].at[unit, hop], place.video_peer(hop),
        )

    def middle(self, unit):
        for stage in range(1, self.n_bits):
            self.stage(unit, stage)

    def land(self, unit):
        self.stage(unit, self.n_bits)
        return self.acc(unit, self.own_block())

    def send_video(self, unit, kind, value):
        value = value.astype(F32)
        for w in range(self.place.V):
            self.send3[unit, w] = self.parts(kind, value, w).astype(BF)
        pl.loop(1, self.place.V)(lambda hop: self.across(unit, hop).start())

    def finish(self, unit):
        self.result[unit] = self.send3[unit, self.place.v].astype(F32)

        @pl.loop(1, self.place.V)
        def _(hop):
            self.across(unit, hop).wait_recv()
            self.result[unit] += self.recv3[unit, hop].astype(F32)

    def drain(self, unit, source):
        self.exchange0(unit, source).wait_send()
        for stage in range(self.n_bits):
            for i in range(1 << (self.n_bits - 1 - stage)):
                self.exchange(unit, stage, i, 0).wait_send()

    def drain_video(self, unit):
        pl.loop(1, self.place.V)(lambda hop: self.across(unit, hop).wait_send())


class Totals:
    def __init__(self, place, which, own, near, middle, far, result, sems):
        self.place, self.which, self.own, self.near_buf, self.middle = place, which, own, near, middle
        self.far_buf, self.result, self.sems = far, result, sems

    def near(self, step):
        sems = self.sems
        return remote(
            self.own, self.near_buf.at[self.which, step], sems["vec_send"].at[self.which, 0, step],
            sems["vec_recv"].at[self.which, 0, step], self.place.frame_peer(step),
        )

    def far(self, hop):
        sems = self.sems
        return remote(
            self.middle.at[self.which], self.far_buf.at[self.which, hop], sems["vec_send"].at[self.which, 1, hop],
            sems["vec_recv"].at[self.which, 1, hop], self.place.video_peer(hop),
        )

    def start(self):
        pl.loop(1, self.place.F)(lambda step: self.near(step).start())

    def forward(self):
        self.middle[self.which] = self.own[...]

        @pl.loop(1, self.place.F)
        def _(step):
            self.near(step).wait_recv()
            self.middle[self.which] += self.near_buf[self.which, step]

        pl.loop(1, self.place.V)(lambda hop: self.far(hop).start())

    def finish(self):
        self.result[self.which] = self.middle[self.which]

        @pl.loop(1, self.place.V)
        def _(hop):
            self.far(hop).wait_recv()
            self.result[self.which] += self.far_buf[self.which, hop]
            self.far(hop).wait_send()

        pl.loop(1, self.place.F)(lambda step: self.near(step).wait_send())


def mlp_kernel(
    frame_size, video_size, videos_here, frames_here,
    kept_ref, cot_ref, gain, shift, fc_bias, proj_bias, fc_hbm, proj_hbm,
    out_ref, grad_ref, done_ref, mid_ref, raw_hbm, sums,
    wide, normed2, cot2, act, grad_h, out_acc, grad_acc, bias_rows, bias_sums, fc_buf, proj_buf, fc_all,
    grads, recv0, recv_a, recv_b, recv_c, send3, recv3,
    s_load, s_raw, s_send0, s_recv0, s_sendb, s_recvb, s_send3, s_recv3,
):
    chunk = pl.program_id(0)
    frames = videos_here * frames_here
    place = Place(frame_size, video_size)
    step = D // frame_size // UNITS
    wide_step = 4 * step
    width = FF // UNITS
    sems = dict(send0=s_send0, recv0=s_recv0, send_bits=s_sendb, recv_bits=s_recvb, send3=s_send3, recv3=s_recv3)
    scatter = Scatter(
        place, step, lambda unit, block: grads.at[unit, 0, block], recv0, [recv_a, recv_b, recv_c], send3, recv3, done_ref, sems
    )
    sliced = wide_step % 128 == 0

    def rows_of(b, count=1):
        return pl.ds(pl.multiple_of(b * count * ROWS, ROWS), count * ROWS)

    def loads(c):
        slot = lax.rem(c, 2)
        out = []
        for f in range(frame_size):
            at = pl.multiple_of((f * UNITS + c) * wide_step, wide_step)
            to = slice(f * wide_step, f * wide_step + wide_step)
            out.append(pltpu.make_async_copy(proj_hbm.at[pl.ds(at, wide_step)], proj_buf.at[slot, to], s_load.at[slot, 0, f]))
            if sliced:
                out.append(pltpu.make_async_copy(fc_hbm.at[:, pl.ds(at, wide_step)], fc_buf.at[slot, :, to], s_load.at[slot, 1, f]))
        return out

    def load_all():
        return pltpu.make_async_copy(fc_hbm, fc_all, s_load.at[0, 1, 0])

    @pl.when(chunk == 0)
    def _():
        place.announce()
        for load in loads(chunk):
            load.start()
        if not sliced:
            load_all().start()
        sums[...] = jnp.zeros_like(sums)
        bias_sums[...] = jnp.zeros_like(bias_sums)
        wide[:, PATCHES:ROWS, :] = jnp.zeros((frames_here, ROWS - PATCHES, D), F32)
        bias = fc_bias[...].astype(F32).reshape(1, FF)
        for c in range(UNITS):
            for f in range(frame_size):
                at = (f * UNITS + c) * wide_step
                bias_rows[c : c + 1, f * wide_step : f * wide_step + wide_step] = bias[:, at : at + wide_step]

        @pl.loop(0, videos_here)
        def _(i):
            cot = cot_ref[i].astype(F32)
            for j in range(frames_here):
                wide[j, 0:PATCHES, :] = cot[:, j, :]
            for j in range(frames_here):
                b = i * frames_here + j
                cot_j = wide[j]
                cot2[rows_of(b), :] = cot_j.astype(BF)
                sums[6:7, :] += column_sum(cot_j)
                normed, _, _ = norm_fwd(kept_ref[b], vec(gain), vec(shift))
                normed2[rows_of(b), :] = normed.astype(BF)
                out_acc[rows_of(b), :] = kept_ref[b] + vec(proj_bias)
                grad_acc[rows_of(b), :] = jnp.zeros((ROWS, D), F32)

        if not sliced:
            load_all().wait()
        place.meet()

    for load in loads(chunk):
        load.wait()

    @pl.when(chunk < UNITS - 1)
    def _():
        for load in loads(chunk + 1):
            load.start()

    slot = lax.rem(chunk, 2)
    if not sliced:
        for c in range(UNITS):

            @pl.when(chunk == c)
            def _(c=c):
                for f in range(frame_size):
                    at = (f * UNITS + c) * wide_step
                    fc_buf[slot, :, f * wide_step : f * wide_step + wide_step] = fc_all[:, at : at + wide_step]

    fc, proj = fc_buf.at[slot], proj_buf.at[slot]
    bias = bias_rows[pl.ds(chunk, 1), :]
    per_tile = 2 if frames % 2 == 0 else 1
    tiles = frames // per_tile

    def due(c, t, now, call):
        pl.when(jnp.logical_and(chunk == c, now == min(t, tiles - 1)))(call)

    def both(call, first):
        return lambda: pl.loop(first, first + 2)(call)

    def video():
        for unit in range(2):
            scatter.send_video(unit, unit % 2, scatter.land(unit)[...])

    @pl.loop(0, tiles)
    def _(t):
        due(1, 1, t, both(lambda unit: scatter.stage(unit, 0), 0))
        due(2, 0, t, both(scatter.middle, 0))
        due(2, 1, t, both(lambda unit: scatter.stage(unit, 0), 2))
        due(2, 2, t, video)
        rows = rows_of(t, per_tile)
        hidden = dims(normed2[rows, :], fc[...], 1, 0) + bias
        grad_a = dims(cot2[rows, :], proj[...], 1, 1)
        gate = 0.5 * jnp.tanh(0.851 * hidden) + 0.5
        active = hidden * gate
        grad = (grad_a * (gate + 1.702 * active * (1.0 - gate))).astype(BF)
        active = active.astype(BF)
        act[rows, :] = active
        grad_h[rows, :] = grad
        bias_sums[pl.ds(chunk, 1), :] += column_sum(grad.astype(F32))
        out_acc[rows, :] += dims(active, proj[...], 1, 0)
        grad_acc[rows, :] += dims(grad, fc[...], 1, 1)

    unit = 2 * chunk

    @pl.loop(0, 2)
    def _(m):
        size = width // 2
        count = frame_size // 4
        value = dims(act[:, pl.ds(pl.multiple_of(m * size, size), size)], cot2[...], 0, 0).astype(BF)
        value = value.reshape(count, 2, 4, step, D)
        for core in range(2):
            for q in range(4):
                grads[
                    unit + 1, lax.rem(core + place.core, 2), pl.ds(m * count, count), :, q * D : q * D + D
                ] = value[:, core, q]

    @pl.loop(0, 2)
    def _(m):
        size = D // 2
        value = dims(normed2[:, pl.ds(pl.multiple_of(m * size, size), size)], grad_h[...], 0, 0).astype(BF)
        count = frame_size // 4
        value = value.reshape(count, 2, UNITS, step, width)
        for core in range(2):
            for q in range(UNITS):
                grads[
                    unit, lax.rem(core + place.core, 2), pl.ds(m * count, count), :, q * width : q * width + width
                ] = value[:, core, q]

    def raw():
        return pltpu.make_async_copy(grads.at[pl.ds(4, 2)], raw_hbm, s_raw.at[0])

    def source(unit):
        return grads.at[unit, 1]

    @pl.when(chunk == 0)
    def _():
        pl.loop(0, 2)(lambda unit: scatter.exchange0(unit, source(unit)).start())

    @pl.when(chunk == 1)
    def _():
        pl.loop(2, 4)(lambda unit: scatter.exchange0(unit, source(unit)).start())

    @pl.when(chunk == 2)
    def _():
        raw().start()
        both(scatter.middle, 2)()
        both(scatter.finish, 0)()
        for c in range(UNITS):
            for f in range(frame_size):
                at = (f * UNITS + c) * wide_step
                row, column = 2 + at // D, at % D
                sums[row : row + 1, column : column + wide_step] = bias_sums[
                    c : c + 1, f * wide_step : f * wide_step + wide_step
                ]

        @pl.loop(0, videos_here)
        def _(i):
            outs = [out_acc[rows_of(i * frames_here + j), :][:PATCHES] for j in range(frames_here)]
            out_ref[i] = jnp.stack(outs, axis=1).astype(BF)

        @pl.loop(0, frames)
        def _(b):
            rows = rows_of(b)
            _, unit, inv = norm_fwd(kept_ref[b], vec(gain), vec(shift))
            grad = grad_acc[rows, :]
            sums[0:1, :] += column_sum(grad * unit)
            sums[1:2, :] += column_sum(grad)
            grad_ref[b] = norm_back(grad, unit, inv, vec(gain)) + cot2[rows, :].astype(F32)

        @pl.loop(0, 2)
        def _(unit):
            mid_ref[unit] = scatter.land(2 + unit)[...]
            scatter.drain_video(unit)

        pl.loop(0, 4)(lambda unit: scatter.drain(unit, source(unit)))
        raw().wait()


def attn_back_kernel(
    frame_size, video_size, videos_here, frames_here,
    x_hbm, normed_hbm, msg_ref, gk_ref, gain, shift, w_in, w_out, mlp_sums, mid_ref, raw_hbm, cls_ref, *rest,
):
    msg_operands, rest = rest[:8], rest[8:]
    (
        mixed_ref, q_ref, k_ref, v_ref, p_ref, inv_ref,
        tg_ref, reduced_ref, totals_ref, msg_ref_out, in_ref_out, out_ref_out, msg_sums, grad_cls,
        x_ref, normed_ref, joined, staged, gqkv_all, gk_all, sums, gm_wide, gm_own, gm_rows, gm_all, wide, cls_grads,
        acc_mlp, acc_attn, recv0, recv_a, recv_b, recv_c, send3, recv3,
        vec_near, vec_mid, vec_far, *rest,
    ) = rest
    msg_kept, (msg_gqkv, msg_mixed), msg_state, rest = list(rest[:7]), rest[7:9], rest[9:15], rest[15:]
    msg_kept.insert(6, gqkv_all.at[0:D])
    (
        s_late, s_msg, s_local, s_staged, s_send0, s_recv0, s_sendb, s_recvb, s_send3, s_recv3, s_vsend, s_vrecv, s_gsend, s_grecv,
    ) = rest
    frames = videos_here * frames_here
    b = pl.program_id(0)
    place = Place(frame_size, video_size)
    step = D // frame_size // UNITS
    sems = dict(
        send0=s_send0, recv0=s_recv0, send_bits=s_sendb, recv_bits=s_recvb, send3=s_send3, recv3=s_recv3,
        vec_send=s_vsend, vec_recv=s_vrecv,
    )
    each_mid, each_last, each_attn = pl.loop(0, 2), pl.loop(2, 4), pl.loop(4, 4 + UNITS)
    buffers = (recv0, [recv_a, recv_b, recv_c], send3, recv3, reduced_ref, sems)
    lasts = Scatter(place, step, lambda unit, block: acc_mlp.at[unit - 2, block], *buffers, first=2)
    attns = Scatter(place, step, lambda unit, block: acc_attn.at[0, unit - 4, block], *buffers, first=2)

    def last_source(unit):
        return raw_hbm.at[unit - 2, 1]

    def attn_source(unit):
        return acc_attn.at[1, unit - 4]

    early = Totals(place, 0, mlp_sums, vec_near, vec_mid, vec_far, totals_ref, sems)
    late = Totals(place, 1, sums, vec_near, vec_mid, vec_far, totals_ref, sems)
    gather = Gather(place, gm_own, gm_rows, s_gsend, s_grecv)

    def local(unit):
        return pltpu.make_async_copy(raw_hbm.at[unit - 2, 0], acc_mlp.at[unit - 2], s_local.at[unit - 2])

    def msg_loads():
        return [pltpu.make_async_copy(a, b, s_msg.at[i]) for i, (a, b) in enumerate(zip(msg_operands, msg_kept))]

    def due(at, call):
        pl.when(b == min(at, frames - 1))(call)

    def late_loads():
        return [
            pltpu.make_async_copy(x_hbm, x_ref, s_late.at[0]), pltpu.make_async_copy(normed_hbm, normed_ref, s_late.at[1]),
        ]

    def begin():
        place.greet()
        sums[...] = jnp.zeros_like(sums)

        @each_last
        def _(unit):
            lasts.exchange0(unit, last_source(unit)).start()
            local(unit).start()

        early.start()
        for at, load in enumerate(msg_loads()):
            if at != 6:
                load.start()
        for load in late_loads():
            load.start()
        for unit in range(2):
            lasts.send_video(unit, unit, mid_ref[unit])

    def open_lasts():
        @each_last
        def _(unit):
            local(unit).wait()
            lasts.stage(unit, 0)

    def land_lasts():
        for unit in (2, 3):
            lasts.send_video(unit, unit % 2, lasts.land(unit)[...])

    due(0, begin)
    rows = pl.ds(pl.multiple_of(b * ROWS, ROWS), ROWS)
    gk_low = gk_ref[b].astype(BF)
    gk_all[b] = gk_low
    sums[0:1, :] += column_sum(gk_low.astype(F32))
    grad_mixed = dims(gk_low, w_out[...], 1, 1)

    def run_pairs(pairs):
        for pair in pairs:
            grads = pair_back(
                q_ref[0, pair], k_ref[0, pair], v_ref[0, pair], grad_mixed[:, lanes(pair)],
                mixed_ref[b, :, lanes(pair)], inv_ref[0, pair],
                lambda head, pair=pair: p_ref[0, pair, :, head * KEYS : head * KEYS + KEYS],
            )
            for kind in range(3):
                gqkv_all[rows, kind * D + pair * 128 : kind * D + pair * 128 + 128] = grads[kind][:ROWS].astype(BF)

    due(1, open_lasts)
    due(3, lambda: each_last(lasts.middle))
    due(2, early.forward)
    run_pairs(range(PAIRS // 2))
    due(1, lambda: each_mid(lasts.finish))
    due(4, land_lasts)
    due(5, lambda: each_last(lasts.finish))
    run_pairs(range(PAIRS // 2, PAIRS))
    gqkv = gqkv_all[rows, :]
    sums[1:2, :] += column_sum(gqkv[:, :D].astype(F32))
    sums[2:3, :] += column_sum(gqkv[:, 2 * D :].astype(F32))

    @pl.when(b == frames - 1)
    def _():
        at = JOINED - 1 - (JOINED - 1) % 16
        for c in range(frames):
            piece = dims(gqkv_all[c * ROWS + at : c * ROWS + at + 16, :], w_in[...], 1, 1)
            gm_wide[c : c + 1, :] = piece[PATCHES - at : PATCHES - at + 1]
            joined[c : c + 1, :] = msg_ref[c]
        _, unit, inv = norm_fwd(joined[0:frames, :], vec(gain), vec(shift))
        gm_wide[0:frames, :] = norm_back(gm_wide[0:frames, :], unit, inv, vec(gain))
        for i in range(videos_here):
            gm_own[i] = gm_wide[i * frames_here : i * frames_here + frames_here, :].astype(BF)
            gm_rows[place.v, i, place.f] = gm_own[i]
        gather.start()
        early.finish()

        total = frames * ROWS
        for load in late_loads():
            load.wait()

        def attn_unit(m, left, right, lo):
            size = D // 2
            value = dims(left[:, :, pl.ds(pl.multiple_of(m * size, size), size)].reshape(total, size), right, 0, 0).astype(BF)
            count = frame_size // 4
            value = value.reshape(count, 2, UNITS, step, D)
            for u in range(UNITS):
                for core in range(2):
                    acc_attn[lax.rem(core + place.core, 2), u, pl.ds(m * count, count), :, lo : lo + D] = value[:, core, u]

        @pl.loop(0, 2)
        def _(m):
            for kind in range(3):
                attn_unit(m, normed_ref, gqkv_all[0:total, kind * D : kind * D + D], kind * D)
            attn_unit(m, mixed_ref, gk_all[...].reshape(total, D), 3 * D)

        each_attn(lambda unit: attns.exchange0(unit, attn_source(unit)).start())
        gather.near()
        gather.forward()

        def put(i, j):
            return pltpu.make_async_copy(staged.at[j], tg_ref.at[i, :, j], s_staged.at[j])

        def norm_frames(lo, hi):
            @pl.loop(lo, hi)
            def _(i):
                x = x_ref[i].astype(F32)
                for j in range(frames_here):
                    c = i * frames_here + j
                    joined[0:PATCHES, :] = x[:, j, :]
                    joined[PATCHES:ROWS, :] = jnp.zeros((ROWS - PATCHES, D), F32)
                    joined[PATCHES : PATCHES + 1, :] = msg_ref[c]
                    _, unit, inv = norm_fwd(joined[...], vec(gain), vec(shift))
                    rows = pl.ds(pl.multiple_of(c * ROWS, ROWS), ROWS)
                    grad = dims(gqkv_all[rows, :], w_in[...], 1, 1)
                    sums[3:4, :] += column_sum(grad * unit)
                    sums[4:5, :] += column_sum(grad)
                    pl.when(i > 0)(lambda j=j: put(i - 1, j).wait())
                    staged[j] = (gk_ref[c] + norm_back(grad, unit, inv, vec(gain)))[:PATCHES]
                    put(i, j).start()

        norm_frames(0, 1)
        each_attn(lambda unit: attns.stage(unit, 0))
        norm_frames(1, videos_here)
        msg_loads()[6].start()
        late.start()
        attns.middle(4)
        for load in msg_loads():
            load.wait()
        for ref in (msg_sums, msg_ref_out, in_ref_out, out_ref_out):
            ref[...] = jnp.zeros_like(ref)
        count = videos_here * FRAMES

        def between():
            pl.loop(5, 4 + UNITS)(attns.middle)
            late.forward()
            gather.finish()
            for video in range(video_size):
                for i in range(videos_here):
                    for f in range(frame_size):
                        at_row = (i * frame_size + f) * frames_here
                        wide[at_row : at_row + frames_here, :] = gm_rows[video, i, f].astype(F32)
                gm_all[video * count : video * count + count, :] = wide[...].astype(BF)

        blocks = video_size * count // BLOCK
        if blocks > 1:
            between()

        @pl.loop(0, blocks)
        def _(block):
            at = pl.ds(pl.multiple_of(block * BLOCK, BLOCK), BLOCK)
            msg_back_block(
                place, cls_ref[at, :], gm_all.at[at], msg_kept, msg_ref_out, in_ref_out, out_ref_out, msg_sums, cls_grads.at[at],
                msg_state, msg_gqkv, msg_mixed, between if blocks == 1 else lambda: None,
            )

        for i in range(videos_here):
            for j in range(frames_here):
                row = (place.v * videos_here + i) * FRAMES + place.f * frames_here + j
                grad_cls[i * frames_here + j] = cls_grads[pl.ds(row, 1), :]
        for j in range(frames_here):
            put(videos_here - 1, j).wait()

        @each_attn
        def _(unit):
            attns.send_video(unit, 2, attns.land(unit)[...])

        late.finish()
        each_attn(attns.finish)
        each_last(lambda unit: lasts.drain(unit, last_source(unit)))
        each_attn(lambda unit: attns.drain(unit, attn_source(unit)))
        pl.loop(0, 4 + UNITS)(attns.drain_video)


def msg_back_block(place, cls, gm_ref, kept, acc_msg, acc_in, acc_out, sums, cls_grad, scratch, gqkv, grad_mixed, between):
    bias, gain, shift, in_bias, out_bias, w_msg, w_in, w_out = kept
    qkv, probs, invs, mixed, normed, _ = scratch
    own_rows = D // place.F
    padded = acc_msg.shape[0]

    def own_columns(x):
        return pltpu.roll(x.astype(F32), lax.rem(D - place.f * own_rows, D), 1)[:, :padded].astype(BF)

    unit, inv_std = msg_forward(cls, (bias, gain, shift, in_bias, out_bias), w_msg, w_in, w_out, scratch, PAIRS // 2)
    between()
    gm = gm_ref[...]
    acc_out[...] += dims(own_columns(mixed[...]), gm, 0, 0)
    sums[5:6, :] += column_sum(gm.astype(F32))
    grad_mixed[...] = dims(gm, w_out[...], 1, 1)

    @pl.loop(0, PAIRS, unroll=PAIRS // 2)
    def _(pair):
        at = pair_lanes(pair)
        grads = pair_back(
            qkv[:, at], qkv[:, pair_lanes(pair, 1)], qkv[:, pair_lanes(pair, 2)], grad_mixed[:, at],
            mixed[:, at], invs[:, at], lambda head: probs[2 * pair + head],
        )
        for kind in range(3):
            gqkv[:, pair_lanes(pair, kind)] = grads[kind].astype(BF)

    own_normed = own_columns(normed[...])
    grad = None
    for kind in range(3):
        columns = slice(kind * D, kind * D + D)
        part = gqkv[:, columns]
        acc_in[:, columns] += dims(own_normed, part, 0, 0)
        if kind != 1:
            row = 3 + kind // 2
            sums[row : row + 1, :] += column_sum(part.astype(F32))
        term = dims(part, w_in[:, columns], 1, 1)
        grad = term if grad is None else grad + term
    sums[1:2, :] += column_sum(grad * unit)
    sums[2:3, :] += column_sum(grad)
    grad_message = norm_back(grad, unit, inv_std, vec(gain)) + gm.astype(F32)
    grad_message = grad_message.astype(BF)
    acc_msg[...] += dims(own_columns(cls), grad_message, 0, 0)
    sums[0:1, :] += column_sum(grad_message.astype(F32))
    cls_grad[...] = dims(grad_message, w_msg[...], 1, 1)


def collect_kernel(
    frame_size, video_size, videos_here, frames_here,
    done, reduced, totals, acc_msg, acc_in, acc_out, sums, grad_cls, tg_hbm, output_hbm,
    output, tokens_grad, msg_grad, in_grad, out_grad, *rest,
):
    (
        msg_bias_g, msg_gain_g, msg_shift_g, msg_in_bias_g, msg_out_bias_g, gain1_g, shift1_g,
        attn_in_g, attn_in_bias_g, attn_out_g, attn_out_bias_g, gain2_g, shift2_g, fc_g, fc_bias_g, proj_g, proj_bias_g,
        tg, out, sem,
    ) = rest
    f, v = lax.axis_index("frame"), lax.axis_index("video")
    own_rows = D // frame_size

    def load(i):
        return pltpu.make_async_copy(tg_hbm.at[i], tg.at[i], sem.at[0, i])

    def store(i):
        return pltpu.make_async_copy(tg.at[i], tokens_grad.at[i], sem.at[0, i])

    def load_out(i):
        return pltpu.make_async_copy(output_hbm.at[i], out.at[i], sem.at[1, i])

    def store_out(i):
        return pltpu.make_async_copy(out.at[i], output.at[i], sem.at[1, i])

    for i in range(videos_here):
        load(i).start()
        load_out(i).start()
    for i in range(videos_here):
        load(i).wait()
        added = [grad_cls[i * frames_here + j] for j in range(frames_here)]
        tg[i, 0] = tg[i, 0] + jnp.concatenate(added, axis=0)
        store(i).start()
        load_out(i).wait()
        store_out(i).start()

    def own_matrix(target, x):
        size = x.shape[1] // video_size
        target[...] = pltpu.roll(x[:own_rows], lax.rem(x.shape[1] - v * size, x.shape[1]), 1)[:, :size]

    own_matrix(msg_grad, acc_msg[...])
    own_matrix(in_grad, acc_in[...])
    own_matrix(out_grad, acc_out[...])

    def own_vector(target, ref, first, count):
        size = count * D // frame_size
        per_row = frame_size // count
        row = first + lax.div(f, per_row)
        x = ref[pl.ds(row, 1), :]
        x = pltpu.roll(jnp.broadcast_to(x, (8, D)), lax.rem(D - lax.rem(f, per_row) * size, D), 1)
        target[...] = x[0:1, :size].reshape(size)

    mlp_sums, attn_sums = totals.at[0], totals.at[1]
    for target, ref, first, count in (
        (msg_bias_g, sums, 0, 1), (msg_gain_g, sums, 1, 1), (msg_shift_g, sums, 2, 1), (msg_in_bias_g, sums, 3, 2),
        (msg_out_bias_g, sums, 5, 1), (gain1_g, attn_sums, 3, 1), (shift1_g, attn_sums, 4, 1),
        (attn_in_bias_g, attn_sums, 1, 2), (attn_out_bias_g, attn_sums, 0, 1), (gain2_g, mlp_sums, 0, 1),
        (shift2_g, mlp_sums, 1, 1), (fc_bias_g, mlp_sums, 2, 4), (proj_bias_g, mlp_sums, 6, 1),
    ):
        own_vector(target, ref, first, count)
    step = own_rows // UNITS
    columns = D // video_size
    wide_step = 4 * step
    part = FF // UNITS // video_size
    fc = [done[0], reduced[0], reduced[2]]
    for c in range(UNITS):
        for q in range(UNITS):
            for g in range(frame_size // video_size):
                from_at = q * part + g * wide_step
                to = (g * UNITS + c) * wide_step
                fc_g[q * step : q * step + step, to : to + wide_step] = fc[c][:, from_at : from_at + wide_step]
    for u in range(UNITS):
        rows = slice(u * step, u * step + step)
        attn_in_g[rows, :] = reduced[4 + u][:, : 3 * columns]
        attn_out_g[rows, :] = reduced[4 + u][:, 3 * columns :]
    proj = [done[1], reduced[1], reduced[3]]
    proj = [x[:, q * columns : q * columns + columns] for x in proj for q in range(4)]
    proj_g[...] = jnp.concatenate(proj, axis=0).T
    for i in range(videos_here):
        store(i).wait()
        store_out(i).wait()


def shaped(shape, dtype):
    return jax.ShapeDtypeStruct(shape, dtype)


def whole(array):
    shape = array.shape
    return pl.BlockSpec(shape, lambda *_: (0,) * len(shape), pipeline_mode=pl.Buffered(1))


def wholes(*arrays):
    return [whole(array) for array in arrays]


def in_hbm():
    return pl.BlockSpec(memory_space=pl.ANY)


def in_vmem():
    return pl.BlockSpec(memory_space=pltpu.VMEM)


def per_step(count, shape):
    return pl.BlockSpec((count,) + shape, lambda b: (b,) + (0,) * len(shape))


def params(mib, **more):
    return pltpu.CompilerParams(vmem_limit_bytes=mib * MIB, **more)


def on_device(frame_size, video_size, *args):
    (
        tokens, cotangent, msg_weight, msg_bias, msg_norm_gain, msg_norm_shift, msg_in_weight,
        msg_in_bias, msg_out_weight, msg_out_bias, norm1_gain, norm1_shift, attn_in_weight,
        attn_in_bias, attn_out_weight, attn_out_bias, norm2_gain, norm2_shift, fc_weight, fc_bias,
        proj_weight, proj_bias,
    ) = args
    videos_here, frames_here = tokens.shape[:2]
    frames = videos_here * frames_here
    msgs = videos_here * video_size * FRAMES
    group = videos_here * FRAMES
    total = frames * ROWS
    F, V = frame_size, video_size
    step = D // F // UNITS
    n_bits = int(math.log2(F)) - 1
    x = tokens.transpose(0, 2, 1, 3)
    cot = cotangent.transpose(0, 2, 1, 3)
    msg_vectors = (msg_bias, msg_norm_gain, msg_norm_shift, msg_in_bias, msg_out_bias)
    DMA = pltpu.SemaphoreType.DMA

    msg_out, cls = pl.pallas_call(
        functools.partial(msg_fwd_kernel, F, V, frames_here, videos_here),
        in_specs=[in_hbm()] * 9,
        out_specs=[in_vmem()] * 2,
        out_shape=[shaped((frames, 1, D), F32), shaped((msgs, D), BF)],
        scratch_shapes=[
            pltpu.VMEM((videos_here, frames_here, D), BF),
            pltpu.VMEM((V, videos_here, F, frames_here, D), BF),
            pltpu.VMEM((group, D), F32), pltpu.VMEM((group, D), F32),
        ]
        + [pltpu.VMEM(a.shape, BF) for a in (*msg_vectors, msg_weight, msg_in_weight, msg_out_weight)]
        + msg_scratch(group) + [DMA((V, F + V)), DMA((V, F + V)), DMA((10,))],
        compiler_params=params(63, collective_id=1, has_side_effects=True),
        name="msg_fwd",
    )(x, *msg_vectors, msg_weight, msg_in_weight, msg_out_weight)

    q, k, v, p, inv, mixed, kept, normed = pl.pallas_call(
        functools.partial(attn_fwd_kernel, frames_here),
        grid=(videos_here,),
        in_specs=[per_step(1, (PATCHES, frames_here, D)), per_step(frames_here, (1, D))]
        + wholes(norm1_gain, norm1_shift, attn_in_bias, attn_out_bias, attn_in_weight, attn_out_weight),
        out_specs=[
            per_step(frames_here, shape) for shape in (
                (PAIRS, ROWS, 128), (PAIRS, KEYS, 128), (PAIRS, KEYS, 128), (PAIRS, ROWS, 2 * KEYS),
                (PAIRS, ROWS, 128), (ROWS, D), (ROWS, D), (ROWS, D),
            )
        ],
        out_shape=[
            shaped((frames, PAIRS, ROWS, 128), BF), shaped((frames, PAIRS, KEYS, 128), BF),
            shaped((frames, PAIRS, KEYS, 128), BF), shaped((frames, PAIRS, ROWS, 2 * KEYS), BF),
            shaped((frames, PAIRS, ROWS, 128), F32), shaped((frames, ROWS, D), BF),
            shaped((frames, ROWS, D), F32), shaped((frames, ROWS, D), BF),
        ],
        scratch_shapes=[pltpu.VMEM((frames_here, ROWS, D), F32)],
        compiler_params=params(56),
        name="attn_fwd",
    )(x, msg_out, norm1_gain, norm1_shift, attn_in_bias, attn_out_bias, attn_in_weight, attn_out_weight)

    def bit_buffers(units):
        return [
            pltpu.VMEM((units, max(1, F >> (2 + i)), step, FF), BF) if i < n_bits else pltpu.VMEM((1, 1, 16, 128), BF)
            for i in range(3)
        ]

    def exchange_sems(units):
        return [DMA((units,)), DMA((units,)), DMA((units, n_bits, F // 4)), DMA((units, n_bits, F // 4)), DMA((units, V)), DMA((units, V))]

    def unit_buffers(count, units):
        return [pltpu.VMEM((count,) + shape, BF) for shape in units]

    block_shape = (F // 2, step, FF)
    part_shape = (V, step, FF // V)
    width = FF // UNITS
    mlp_outs = [
        shaped(x.shape, BF), shaped(kept.shape, F32), shaped((2, step, FF // V), F32), shaped((2, step, FF), BF),
        shaped((2, 2) + block_shape, BF), shaped((8, D), F32),
    ]
    output, grad_kept, done, mid, raw, mlp_sums = pl.pallas_call(
        functools.partial(mlp_kernel, F, V, videos_here, frames_here),
        grid=(UNITS,),
        in_specs=wholes(kept, cot, norm2_gain, norm2_shift, fc_bias, proj_bias) + [in_hbm(), in_hbm()],
        out_specs=wholes(*mlp_outs[:4]) + [in_hbm()] + wholes(mlp_outs[5]),
        out_shape=mlp_outs,
        scratch_shapes=[
            pltpu.VMEM((frames_here, ROWS, D), F32),
            pltpu.VMEM((total, D), BF), pltpu.VMEM((total, D), BF), pltpu.VMEM((total, width), BF), pltpu.VMEM((total, width), BF),
            pltpu.VMEM((total, D), F32), pltpu.VMEM((total, D), F32),
            pltpu.VMEM((UNITS, width), F32), pltpu.VMEM((UNITS, width), F32),
            pltpu.VMEM((2, D, width), BF), pltpu.VMEM((2, width, D), BF),
            pltpu.VMEM((D, FF) if 4 * step % 128 else (16, 128), BF),
            pltpu.VMEM((2 * UNITS, 2) + block_shape, BF), pltpu.VMEM((4,) + block_shape, BF),
        ]
        + bit_buffers(4) + unit_buffers(2, [part_shape] * 2)
        + [DMA((2, 2, F)), DMA((1,))] + exchange_sems(4),
        compiler_params=params(63, collective_id=2, has_side_effects=True),
        name="mlp",
    )(kept, cot, norm2_gain, norm2_shift, fc_bias, proj_bias, fc_weight, proj_weight)

    own_units = 4 + UNITS
    rows_own, columns = D // F, D // V
    padded = -(-rows_own // 128) * 128
    back_outs = [
        shaped(x.shape, F32), shaped((own_units, step, FF // V), F32), shaped((2, 8, D), F32),
        shaped((padded, D), F32), shaped((padded, 3 * D), F32), shaped((padded, D), F32), shaped((8, D), F32),
        shaped((frames, 1, D), F32),
    ]
    msg_arrays = (*msg_vectors, msg_weight, msg_in_weight, msg_out_weight)
    tg, reduced, totals, acc_msg, acc_in, acc_out, msg_sums, grad_cls = pl.pallas_call(
        functools.partial(attn_back_kernel, F, V, videos_here, frames_here),
        grid=(frames,),
        in_specs=[in_hbm()] * 2
        + wholes(msg_out, grad_kept, norm1_gain, norm1_shift, attn_in_weight, attn_out_weight, mlp_sums, mid)
        + [in_hbm()] + wholes(cls) + [in_hbm()] * 8 + wholes(mixed)
        + [
            per_step(1, shape) for shape in (
                (PAIRS, ROWS, 128), (PAIRS, KEYS, 128), (PAIRS, KEYS, 128), (PAIRS, ROWS, 2 * KEYS), (PAIRS, ROWS, 128),
            )
        ],
        out_specs=[in_hbm()] + wholes(*back_outs[1:]),
        out_shape=back_outs,
        scratch_shapes=[
            pltpu.VMEM(x.shape, BF), pltpu.VMEM(normed.shape, BF),
            pltpu.VMEM((ROWS, D), F32), pltpu.VMEM((frames_here, PATCHES, D), F32),
            pltpu.VMEM((max(total, D), 3 * D), BF), pltpu.VMEM((frames, ROWS, D), BF), pltpu.VMEM((8, D), F32), pltpu.VMEM((8, D), F32),
            pltpu.VMEM((videos_here, frames_here, D), BF), pltpu.VMEM((V, videos_here, F, frames_here, D), BF),
            pltpu.VMEM((msgs, D), BF), pltpu.VMEM((group, D), F32), pltpu.VMEM((msgs, D), F32),
        ]
        + unit_buffers(2, [block_shape, (UNITS,) + block_shape]) + unit_buffers(own_units - 2, [block_shape])
        + bit_buffers(own_units - 2) + unit_buffers(own_units, [part_shape] * 2)
        + [pltpu.VMEM((2, F, 8, D), F32), pltpu.VMEM((2, 8, D), F32), pltpu.VMEM((2, V, 8, D), F32)]
        + [pltpu.VMEM(a.shape, BF) for a in msg_arrays if a is not msg_in_weight]
        + [pltpu.VMEM((BLOCK, 3 * D), BF), pltpu.VMEM((BLOCK, D), F32)] + msg_scratch(BLOCK)
        + [DMA((2,)), DMA((8,)), DMA((2,)), DMA((frames_here,))] + exchange_sems(own_units)
        + [DMA((2, 2, max(F, V))), DMA((2, 2, max(F, V))), DMA((V, F + V)), DMA((V, F + V))],
        compiler_params=params(63, collective_id=3, has_side_effects=True),
        name="attn_back",
    )(
        x, normed, msg_out, grad_kept, norm1_gain, norm1_shift, attn_in_weight, attn_out_weight, mlp_sums, mid, raw, cls,
        *msg_arrays, mixed, q, k, v, p, inv,
    )

    out_shapes = [
        (rows_own, columns), (rows_own, 3 * columns), (rows_own, columns),
        (rows_own,), (rows_own,), (rows_own,), (2 * rows_own,), (rows_own,), (rows_own,), (rows_own,),
        (rows_own, 3 * columns), (2 * rows_own,), (rows_own, columns), (rows_own,), (rows_own,), (rows_own,),
        (rows_own, 4 * columns), (4 * rows_own,), (columns, 4 * rows_own), (rows_own,),
    ]
    out_shapes = [shaped(shape, F32) for shape in out_shapes]
    (
        output, tokens_grad, msg_grad, msg_in_grad, msg_out_grad,
        msg_bias_g, msg_gain_g, msg_shift_g, msg_in_bias_g, msg_out_bias_g, gain1_g, shift1_g,
        attn_in_g, attn_in_bias_g, attn_out_g, attn_out_bias_g, gain2_g, shift2_g, fc_g, fc_bias_g, proj_g, proj_bias_g,
    ) = pl.pallas_call(
        functools.partial(collect_kernel, F, V, videos_here, frames_here),
        grid=(1,),
        in_specs=wholes(done, reduced, totals, acc_msg, acc_in, acc_out, msg_sums, grad_cls) + [in_hbm()] * 2,
        out_specs=[in_hbm()] * 2 + wholes(*out_shapes),
        out_shape=[shaped(x.shape, BF), shaped(x.shape, F32)] + out_shapes,
        scratch_shapes=[pltpu.VMEM(x.shape, F32), pltpu.VMEM(x.shape, BF), DMA((2, videos_here))],
        compiler_params=params(63),
        name="collect",
    )(done, reduced, totals, acc_msg, acc_in, acc_out, msg_sums, grad_cls, tg, output)

    return (
        output.transpose(0, 2, 1, 3), tokens_grad.transpose(0, 2, 1, 3),
        msg_grad, msg_bias_g, msg_gain_g, msg_shift_g, msg_in_grad, msg_in_bias_g, msg_out_grad, msg_out_bias_g,
        gain1_g, shift1_g, attn_in_g, attn_in_bias_g, attn_out_g, attn_out_bias_g,
        gain2_g, shift2_g, fc_g, fc_bias_g, proj_g.T, proj_bias_g,
    )


def solution(mesh):
    rows = P("video", "frame", None, None)
    matrix, vector = P("frame", "video"), P("frame")
    out_specs = (
        rows, rows,
        matrix, vector, vector, vector, matrix, vector, matrix, vector,
        vector, vector, matrix, vector, matrix, vector,
        vector, vector, matrix, vector, matrix, vector,
    )
    return jax.shard_map(
        functools.partial(on_device, mesh.shape["frame"], mesh.shape["video"]),
        mesh=mesh, in_specs=(rows, rows) + (P(),) * 20, out_specs=out_specs, check_vma=False,
    )
```

```python
import functools
import math

import jax
import jax.numpy as jnp
from jax import lax
from jax.experimental import pallas as pl
from jax.experimental.pallas import tpu as pltpu
from jax.sharding import PartitionSpec as P

D = 768
HEADS = 12
PAIRS = 6
FF = 3072
PATCHES = 197
JOINED = 198
ROWS = 208
KEYS = 256
HALF = D // 2
FRAMES = 16
BLOCK = 192
UNITS = 3
BF = jnp.bfloat16
F32 = jnp.float32
MIB = 1 << 20
MESH = pl.DeviceIdType.MESH


def vec(ref, at=0):
    return ref[...].astype(F32).reshape(1, ref.shape[0])[:, at * D : at * D + D]


def dims(a, b, ca, cb):
    return lax.dot_general(a, b, (((ca,), (cb,)), ((), ())), preferred_element_type=F32)


def column_sum(x):
    return jnp.sum(x, axis=0, keepdims=True)


def norm_fwd(x, gain, shift):
    centre = x - jnp.mean(x, axis=-1, keepdims=True)
    inv = lax.rsqrt(jnp.mean(centre * centre, axis=-1, keepdims=True) + 1e-05)
    unit = centre * inv
    return unit * gain + shift, unit, inv


def norm_back(grad, unit, inv, gain):
    scaled = grad * gain
    return inv * (
        scaled
        - jnp.mean(scaled, axis=-1, keepdims=True)
        - unit * jnp.mean(scaled * unit, axis=-1, keepdims=True)
    )


def low_half():
    return lax.broadcasted_iota(jnp.int32, (1, 128), 1) < 64


def half(low, head, value, other):
    return jnp.where(low, value, other) if head == 0 else jnp.where(low, other, value)


def pair_fwd(q, k, v, mask_scores, keep):
    low = low_half()
    sums = []
    for head in range(2):
        scores = mask_scores(dims(q, half(low, head, k, jnp.zeros_like(k)), 1, 1))
        top = jnp.max(scores, axis=1, keepdims=True)
        probs = jnp.exp(scores - top).astype(BF)
        keep(head, probs)
        sums.append(dims(probs, half(low, head, v, jnp.ones_like(v)), 1, 0))
    inv = 1.0 / pltpu.roll(jnp.where(low, sums[1], sums[0]), 64, 1)
    return jnp.where(low, sums[0], sums[1]) * inv, inv


def pair_back(q, k, v, grad, mixed, inv, probs):
    low = low_half()
    scaled = grad * inv
    scaled_low = scaled.astype(BF)
    both = mixed.astype(F32) * scaled
    zero = jnp.zeros_like(both)
    totals = None
    for head in range(2):
        p = probs(head)
        grad_p = dims(scaled_low, half(low, head, v, jnp.zeros_like(v)), 1, 1)
        delta = jnp.sum(half(low, head, both, zero), axis=1, keepdims=True)
        grad_s = (p.astype(F32) * (grad_p - delta)).astype(BF)
        terms = (
            dims(grad_s, half(low, head, k, jnp.zeros_like(k)), 1, 0),
            dims(grad_s, half(low, head, q, jnp.zeros_like(q)), 0, 0),
            dims(p, half(low, head, scaled_low, jnp.zeros_like(scaled_low)), 0, 0),
        )
        totals = terms if totals is None else tuple(a + b for a, b in zip(totals, terms))
    return totals[0] * 0.125, totals[1], totals[2]


def lanes(pair):
    return slice(pair * 128, pair * 128 + 128)


def msg_mask(rows):
    row = lax.broadcasted_iota(jnp.int32, (rows, rows), 0) // FRAMES
    col = lax.broadcasted_iota(jnp.int32, (rows, rows), 1) // FRAMES
    same = row == col
    return lambda scores: jnp.where(same, scores, -1e30)


def msg_scratch(rows):
    return [
        pltpu.VMEM((rows, 3 * D), BF), pltpu.VMEM((HEADS, rows, rows), BF), pltpu.VMEM((rows, D), F32), pltpu.VMEM((rows, D), BF),
        pltpu.VMEM((rows, D), BF), pltpu.VMEM((rows, D), F32),
    ]


def pair_lanes(pair, kind=0):
    return pl.ds(pl.multiple_of(kind * D + pair * 128, 128), 128)


def msg_forward(cls, biases, w_msg, w_in, w_out, scratch, unroll):
    bias, gain, shift, in_bias, _ = biases
    qkv, probs, invs, mixed, normed_low, message = scratch
    message[...] = dims(cls, w_msg[...], 1, 0) + vec(bias)
    normed, unit, inv_std = norm_fwd(message[...], vec(gain), vec(shift))
    normed_low[...] = normed.astype(BF)

    def project(kind, bias, scale):
        columns = slice(kind * D, kind * D + D)
        qkv[:, columns] = ((dims(normed_low[...], w_in[:, columns], 1, 0) + bias) * scale).astype(BF)

    project(0, vec(in_bias), 0.125)
    project(1, 0.0, 1.0)
    project(2, vec(in_bias, 1), 1.0)
    mask = msg_mask(cls.shape[0])

    @pl.loop(0, PAIRS, unroll=unroll)
    def _(pair):
        def keep(head, p):
            probs[2 * pair + head] = p

        out, inv = pair_fwd(qkv[:, pair_lanes(pair)], qkv[:, pair_lanes(pair, 1)], qkv[:, pair_lanes(pair, 2)], mask, keep)
        mixed[:, pair_lanes(pair)] = out.astype(BF)
        invs[:, pair_lanes(pair)] = inv

    return unit, inv_std


class Place:
    def __init__(self, frame_size, video_size):
        self.F, self.V = frame_size, video_size
        self.f, self.v = lax.axis_index("frame"), lax.axis_index("video")
        self.core = lax.rem(self.f, 2)
        self.bits = [lax.rem(lax.div(self.f, 1 << i), 2) for i in range(int(math.log2(frame_size)))]

    def frame_peer(self, step):
        return {"frame": lax.rem(self.f + step, self.F)}

    def video_peer(self, step):
        return {"video": lax.rem(self.v + step, self.V)}

    def greet(self):
        self.announce()
        self.meet()

    def announce(self):
        barrier = pltpu.get_barrier_semaphore()

        @pl.loop(1, self.F)
        def _(step):
            pl.semaphore_signal(barrier, inc=1, device_id=self.frame_peer(step), device_id_type=MESH)

        @pl.loop(1, self.V)
        def _(step):
            pl.semaphore_signal(barrier, inc=1, device_id=self.video_peer(step), device_id_type=MESH)

    def meet(self):
        pl.semaphore_wait(pltpu.get_barrier_semaphore(), self.F + self.V - 2)


def remote(src, dst, send, recv, peer):
    return pltpu.make_async_remote_copy(
        src_ref=src, dst_ref=dst, send_sem=send, recv_sem=recv, device_id=peer, device_id_type=MESH
    )


class Gather:
    def __init__(self, place, own, rows, send, recv):
        self.place, self.own, self.rows, self.send, self.recv = place, own, rows, send, recv

    def near_copy(self, step, arriving):
        place = self.place
        frame = lax.rem(place.f + place.F - step, place.F) if arriving else place.f
        return remote(
            self.own, self.rows.at[place.v, :, frame], self.send.at[0, step], self.recv.at[0, step], place.frame_peer(step)
        )

    def far_copy(self, hop, arriving):
        place = self.place
        video = lax.rem(place.v + place.V - hop, place.V) if arriving else place.v
        slot = place.F - 1 + hop
        return remote(
            self.own, self.rows.at[video, :, place.f], self.send.at[0, slot], self.recv.at[0, slot], place.video_peer(hop)
        )

    def passed_copy(self, hop, step, arriving):
        place = self.place
        video = lax.rem(place.v + place.V - hop, place.V)
        frame = lax.rem(place.f + place.F - step, place.F) if arriving else place.f
        part = self.rows.at[video, :, frame]
        return remote(part, part, self.send.at[hop, step], self.recv.at[hop, step], place.frame_peer(step))

    def each_frame(self, call):
        pl.loop(1, self.place.F)(call)

    def each_video(self, call):
        pl.loop(1, self.place.V)(call)

    def start(self, far=True):
        self.each_frame(lambda step: self.near_copy(step, False).start())
        self.each_video(lambda hop: self.far_copy(hop, False).start())

    def near(self):
        self.each_frame(lambda step: self.near_copy(step, True).wait_recv())

    def forward(self):
        @pl.loop(1, self.place.V)
        def _(hop):
            self.far_copy(hop, True).wait_recv()
            self.each_frame(lambda step: self.passed_copy(hop, step, False).start())

    def finish(self):
        @pl.loop(1, self.place.V)
        def _(hop):
            def passed(step):
                self.passed_copy(hop, step, True).wait_recv()
                self.passed_copy(hop, step, False).wait_send()

            self.each_frame(passed)
            self.far_copy(hop, False).wait_send()

        self.each_frame(lambda step: self.near_copy(step, False).wait_send())


def attn_fwd_kernel(
    frame_size, video_size, frames_here, videos_here,
    x_ref, x_hbm, gain1, shift1, in_bias1, out_bias1, w_in1, w_out_hbm, *rest,
):
    operands, rest = rest[:8], rest[8:]
    (
        q_hbm, k_hbm, v_hbm, normed_hbm, p_ref, inv_ref, mixed_ref, kept_ref, out_ref, cls_ref,
        q_ref, k_ref, v_ref, normed_ref, joined, w_out1, msg_rows, msg_wide, own, rows, wide, mixed_out, *rest,
    ) = rest
    kept, scratch, (send, recv, local, s_out) = rest[:8], rest[8:14], rest[14:]
    bias, gain, shift, in_bias, out_bias, w_msg, w_in, w_out = kept
    place = Place(frame_size, video_size)
    t = pl.program_id(0)
    i = lax.rem(t, videos_here)
    frames = videos_here * frames_here
    every = frames_here * ROWS
    gather = Gather(place, own, rows, send, recv)

    def loads():
        pairs = [(x_hbm.at[:, 0], own), (x_hbm.at[:, 0], rows.at[place.v, :, place.f]), (w_out_hbm, w_out1)]
        pairs += list(zip(operands, kept))
        return [pltpu.make_async_copy(source, target, local.at[at]) for at, (source, target) in enumerate(pairs)]

    def stores():
        pairs = ((q_ref, q_hbm), (k_ref, k_hbm), (v_ref, v_hbm), (normed_ref, normed_hbm))
        return [pltpu.make_async_copy(source, target, s_out.at[at]) for at, (source, target) in enumerate(pairs)]

    @pl.when(t == 0)
    def _():
        place.announce()
        for load in loads():
            load.start()

    @pl.when(t == min(1, videos_here - 1))
    def _():
        for load in loads()[:2]:
            load.wait()
        place.meet()
        gather.start()

    @pl.when(t < videos_here)
    def _():
        x = x_ref[0].astype(F32)
        first = i * frames_here
        for j in range(frames_here):
            joined[first + j, 0:PATCHES, :] = x[:, j, :]
            joined[first + j, PATCHES:ROWS, :] = jnp.zeros((ROWS - PATCHES, D), F32)
        here = pl.ds(first, frames_here)
        normed, _, _ = norm_fwd(joined[here].reshape(every, D), vec(gain1), vec(shift1))
        normed_ref[here] = normed.astype(BF).reshape(frames_here, ROWS, D)
        normed = normed_ref[here].reshape(every, D)
        pad = jnp.zeros((KEYS - ROWS, 128), BF)
        q = ((dims(normed, w_in1[:, :D], 1, 0) + vec(in_bias1)) * 0.125).astype(BF)
        k = dims(normed, w_in1[:, D : 2 * D], 1, 0).astype(BF)
        v = (dims(normed, w_in1[:, 2 * D :], 1, 0) + vec(in_bias1, 1)).astype(BF)
        for j in range(frames_here):
            part = slice(j * ROWS, j * ROWS + ROWS)
            for pair in range(PAIRS):
                sl = lanes(pair)
                q_ref[first + j, pair] = q[part, sl]
                k_ref[first + j, pair, 0:ROWS] = k[part, sl]
                k_ref[first + j, pair, ROWS:KEYS] = pad
                v_ref[first + j, pair, 0:ROWS] = v[part, sl]
                v_ref[first + j, pair, ROWS:KEYS] = pad

    def unpack(video):
        for n in range(videos_here):
            for f in range(frame_size):
                at = (n * frame_size + f) * frames_here
                wide[at : at + frames_here, :] = rows[video, n, f].astype(F32)

    @pl.when(t == videos_here)
    def _():
        gather.near()
        gather.forward()
        unpack(place.v)
        for load in loads()[2:]:
            load.wait()
        biases = (bias, gain, shift, in_bias, out_bias)
        msg_forward(wide[...].astype(BF), biases, w_msg, w_in, w_out, scratch, PAIRS)
        mixed_out[...] = scratch[5][...] + dims(scratch[3][...], w_out[...], 1, 0) + vec(out_bias)
        msg_rows[...] = jnp.zeros_like(msg_rows)
        for n in range(videos_here):
            for j in range(frames_here):
                c = n * frames_here + j
                row = mixed_out[pl.ds(n * FRAMES + place.f * frames_here + j, 1), :]
                out_ref[c] = row
                msg_rows[c : c + 1, :] = row
                joined[c, PATCHES : PATCHES + 1, :] = row
        normed, _, _ = norm_fwd(msg_rows[...], vec(gain1), vec(shift1))
        low = normed.astype(BF)
        msg_wide[:, :D] = low.astype(F32)
        msg_wide[:, D : 2 * D] = dims(low, w_in1[:, D : 2 * D], 1, 0)
        msg_wide[:, 2 * D :] = dims(low, w_in1[:, 2 * D :], 1, 0) + vec(in_bias1, 1)
        at = PATCHES - PATCHES % 16
        mine = lax.broadcasted_iota(jnp.int32, (16, 1), 0) == PATCHES % 16
        block = slice(at, at + 16)

        @pl.loop(0, frames)
        def _(c):
            row = msg_wide[pl.ds(c, 1), :]
            normed_ref[c, block, :] = jnp.where(mine, row[:, :D], normed_ref[c, block, :].astype(F32)).astype(BF)
            for pair in range(PAIRS):
                for target, lo in ((k_ref, D), (v_ref, 2 * D)):
                    part = row[:, lo + pair * 128 : lo + pair * 128 + 128]
                    target[c, pair, block, :] = jnp.where(mine, part, target[c, pair, block, :].astype(F32)).astype(BF)

        for store in stores():
            store.start()

    valid = lax.broadcasted_iota(jnp.int32, (1, KEYS - 128), 1) < JOINED - 128

    def mask(scores):
        return jnp.concatenate([scores[:, :128], jnp.where(valid, scores[:, 128:], -1e30)], axis=1)

    @pl.when(t >= videos_here)
    def _():
        first = i * frames_here

        @pl.loop(0, frames_here)
        def _(j):
            c = first + j
            for pair in range(PAIRS):

                def keep(head, p, pair=pair):
                    p_ref[j, pair, :, head * KEYS : head * KEYS + KEYS] = p

                out, inv = pair_fwd(q_ref[c, pair], k_ref[c, pair], v_ref[c, pair], mask, keep)
                inv_ref[j, pair] = inv
                mixed_ref[j, :, lanes(pair)] = out.astype(BF)

        attended = dims(mixed_ref[...].reshape(every, D), w_out1[...], 1, 0) + vec(out_bias1)
        kept_ref[...] = joined[pl.ds(first, frames_here)] + attended.reshape(frames_here, ROWS, D)

    @pl.when(t == 2 * videos_here - 1)
    def _():
        gather.finish()
        count = videos_here * FRAMES
        for video in range(video_size):
            unpack(video)
            cls_ref[video * count : video * count + count, :] = wide[...].astype(BF)
        for store in stores():
            store.wait()


def fc_parts(x, w, V):
    size, width = FF // UNITS // V, FF // UNITS
    return jnp.concatenate([x[:, q * width + w * size : q * width + w * size + size] for q in range(UNITS)], axis=1)


def proj_parts(x, w, V):
    size = D // V
    return jnp.concatenate([x[:, q * D + w * size : q * D + w * size + size] for q in range(4)], axis=1)


MLP_PARTS = (fc_parts, proj_parts)


def in_pieces(group, w, V):
    size, out = 3 * D // V, []
    for kind in range(3):
        first = kind * D + group * HALF
        lo, hi = max(first, w * size), min(first + HALF, w * size + size)
        if hi > lo:
            out.append((kind * HALF + lo - first, hi - lo, lo - w * size))
    return out


def in_width(V):
    return max(sum(piece[1] for piece in in_pieces(g, w, V)) for g in range(2) for w in range(V))


def attn_parts(group):
    def parts(x, w, V):
        pieces = [x[:, at : at + count] for at, count, _ in in_pieces(group, w, V)]
        short = in_width(V) - sum(piece.shape[1] for piece in pieces)
        if short:
            pieces.append(jnp.zeros((x.shape[0], short), F32))
        if group == 0:
            size = D // V
            pieces.append(x[:, 3 * HALF + w * size : 3 * HALF + w * size + size])
        return jnp.concatenate(pieces, axis=1) if len(pieces) > 1 else pieces[0]

    return parts


class Scatter:
    def __init__(self, place, step, acc, recv0, recv_bits, send3, recv3, result, sems, first=0):
        self.place, self.step, self.acc, self.first = place, step, acc, first
        self.recv0, self.recv_bits, self.send3, self.recv3, self.result = recv0, recv_bits, send3, recv3, result
        self.sems = sems
        self.n_bits = len(place.bits) - 1

    def other_core(self):
        return {"frame": self.place.f + 1 - 2 * self.place.core}

    def exchange0(self, unit, source):
        return remote(source, self.recv0.at[unit - self.first], self.sems["send0"].at[unit], self.sems["recv0"].at[unit], self.other_core())

    def order(self, core, stage):
        return stage if core == 0 else self.n_bits - 1 - stage

    def blocks(self, stage, flip):
        place, n = self.place, self.n_bits
        free = n - 1 - stage
        out = []
        for i in range(1 << free):
            both = []
            for core in range(2):
                done = [self.order(core, s) for s in range(stage)]
                now = self.order(core, stage)
                rest = [bit for bit in range(n) if bit not in done and bit != now]
                at = 0
                for bit in done:
                    at = at + place.bits[bit + 1] * (1 << bit)
                own = place.bits[now + 1]
                at = at + ((1 - own) if flip else own) * (1 << now)
                for index, bit in enumerate(rest):
                    at = at + ((i >> index) & 1) * (1 << bit)
                both.append(at)
            out.append((1 - place.core) * both[0] + place.core * both[1])
        return out

    def partner(self, stage):
        place = self.place
        moves = []
        for core in range(2):
            bit = self.order(core, stage) + 1
            moves.append((1 - 2 * place.bits[bit]) * (1 << bit))
        return {"frame": place.f + (1 - place.core) * moves[0] + place.core * moves[1]}

    def exchange(self, unit, stage, i, block):
        sems = self.sems
        return remote(
            self.acc(unit, block), self.recv_bits[stage].at[unit - self.first, i],
            sems["send_bits"].at[unit, stage, i], sems["recv_bits"].at[unit, stage, i], self.partner(stage),
        )

    def add(self, unit, block, came):
        target = self.acc(unit, block)
        target[...] = (target[...].astype(F32) + came.astype(F32)).astype(BF)

    def stage(self, unit, stage):
        if stage == 0:
            self.exchange0(unit, self.recv0.at[unit - self.first]).wait_recv()
            came = lambda position, block: self.recv0[unit - self.first, block]
        else:
            for i in range(1 << (self.n_bits - stage)):
                self.exchange(unit, stage - 1, i, 0).wait_recv()
            came = lambda position, block: self.recv_bits[stage - 1][unit - self.first, position]
        if stage == self.n_bits:
            block = self.own_block()
            self.add(unit, block, came(0, block))
            return
        sending, staying = self.blocks(stage, True), self.blocks(stage, False)
        where = self.positions(stage)
        for i, block in enumerate(sending):
            self.add(unit, block, came(where[1][i], block))
            self.exchange(unit, stage, i, block).start()
        for i, block in enumerate(staying):
            self.add(unit, block, came(where[0][i], block))

    def positions(self, stage):
        place, n = self.place, self.n_bits
        if stage == 0:
            return [[None] * (1 << (n - 1))] * 2
        out = [[], []]
        for flip in range(2):
            for i in range(1 << (n - 1 - stage)):
                both = []
                for core in range(2):
                    done = [self.order(core, s) for s in range(stage)]
                    now = self.order(core, stage)
                    rest_before = [bit for bit in range(n) if bit not in done]
                    rest = [bit for bit in rest_before if bit != now]
                    own = place.bits[now + 1]
                    at = 0
                    for index, bit in enumerate(rest_before):
                        if bit == now:
                            at = at + ((1 - own) if flip else own) * (1 << index)
                        else:
                            at = at + ((i >> rest.index(bit)) & 1) * (1 << index)
                    both.append(at)
                out[flip].append((1 - place.core) * both[0] + place.core * both[1])
        return out

    def own_block(self):
        return lax.div(self.place.f, 2)

    def across(self, unit, hop):
        place, sems = self.place, self.sems
        to = lax.rem(place.v + hop, place.V)
        return remote(
            self.send3.at[unit, to], self.recv3.at[unit, hop],
            sems["send3"].at[unit, hop], sems["recv3"].at[unit, hop], place.video_peer(hop),
        )

    def middle(self, unit):
        for stage in range(1, self.n_bits):
            self.stage(unit, stage)

    def land(self, unit):
        self.stage(unit, self.n_bits)
        return self.acc(unit, self.own_block())

    def send_video(self, unit, parts, value):
        value = value.astype(F32)
        for w in range(self.place.V):
            self.send3[unit, w] = parts(value, w, self.place.V).astype(BF)
        pl.loop(1, self.place.V)(lambda hop: self.across(unit, hop).start())

    def finish(self, unit):
        self.result[unit] = self.send3[unit, self.place.v].astype(F32)

        @pl.loop(1, self.place.V)
        def _(hop):
            self.across(unit, hop).wait_recv()
            self.result[unit] += self.recv3[unit, hop].astype(F32)

    def drain(self, unit, source):
        self.exchange0(unit, source).wait_send()
        for stage in range(self.n_bits):
            for i in range(1 << (self.n_bits - 1 - stage)):
                self.exchange(unit, stage, i, 0).wait_send()

    def drain_video(self, unit):
        pl.loop(1, self.place.V)(lambda hop: self.across(unit, hop).wait_send())


class Totals:
    def __init__(self, place, which, own, near, middle, far, result, sems):
        self.place, self.which, self.own, self.near_buf, self.middle = place, which, own, near, middle
        self.far_buf, self.result, self.sems = far, result, sems

    def near(self, step):
        sems = self.sems
        return remote(
            self.own, self.near_buf.at[self.which, step], sems["vec_send"].at[self.which, 0, step],
            sems["vec_recv"].at[self.which, 0, step], self.place.frame_peer(step),
        )

    def far(self, hop):
        sems = self.sems
        return remote(
            self.middle.at[self.which], self.far_buf.at[self.which, hop], sems["vec_send"].at[self.which, 1, hop],
            sems["vec_recv"].at[self.which, 1, hop], self.place.video_peer(hop),
        )

    def start(self):
        pl.loop(1, self.place.F)(lambda step: self.near(step).start())

    def forward(self):
        self.middle[self.which] = self.own[...]

        @pl.loop(1, self.place.F)
        def _(step):
            self.near(step).wait_recv()
            self.middle[self.which] += self.near_buf[self.which, step]

        pl.loop(1, self.place.V)(lambda hop: self.far(hop).start())

    def finish(self):
        self.result[self.which] = self.middle[self.which]

        @pl.loop(1, self.place.V)
        def _(hop):
            self.far(hop).wait_recv()
            self.result[self.which] += self.far_buf[self.which, hop]
            self.far(hop).wait_send()

        pl.loop(1, self.place.F)(lambda step: self.near(step).wait_send())


def mlp_kernel(
    frame_size, video_size, videos_here, frames_here,
    kept_ref, cot_ref, gain, shift, fc_bias, proj_bias, fc_hbm, proj_hbm,
    out_ref, grad_ref, done_ref, mid_ref, raw_hbm, sums,
    wide, normed2, cot2, act, grad_h, out_acc, grad_acc, bias_rows, bias_sums, fc_buf, proj_buf, fc_all,
    grads, recv0, recv_a, recv_b, recv_c, send3, recv3,
    s_load, s_raw, s_send0, s_recv0, s_sendb, s_recvb, s_send3, s_recv3,
):
    chunk = pl.program_id(0)
    frames = videos_here * frames_here
    place = Place(frame_size, video_size)
    step = D // frame_size // UNITS
    wide_step = 4 * step
    width = FF // UNITS
    sems = dict(send0=s_send0, recv0=s_recv0, send_bits=s_sendb, recv_bits=s_recvb, send3=s_send3, recv3=s_recv3)
    scatter = Scatter(
        place, step, lambda unit, block: grads.at[unit, 0, block], recv0, [recv_a, recv_b, recv_c], send3, recv3, done_ref, sems
    )
    sliced = wide_step % 128 == 0

    def rows_of(b, count=1):
        return pl.ds(pl.multiple_of(b * count * ROWS, ROWS), count * ROWS)

    def loads(c):
        slot = lax.rem(c, 2)
        out = []
        for f in range(frame_size):
            at = pl.multiple_of((f * UNITS + c) * wide_step, wide_step)
            to = slice(f * wide_step, f * wide_step + wide_step)
            out.append(pltpu.make_async_copy(proj_hbm.at[pl.ds(at, wide_step)], proj_buf.at[slot, to], s_load.at[slot, 0, f]))
            if sliced:
                out.append(pltpu.make_async_copy(fc_hbm.at[:, pl.ds(at, wide_step)], fc_buf.at[slot, :, to], s_load.at[slot, 1, f]))
        return out

    def load_all():
        return pltpu.make_async_copy(fc_hbm, fc_all, s_load.at[0, 1, 0])

    @pl.when(chunk == 0)
    def _():
        place.announce()
        for load in loads(chunk):
            load.start()
        if not sliced:
            load_all().start()
        sums[...] = jnp.zeros_like(sums)
        bias_sums[...] = jnp.zeros_like(bias_sums)
        wide[:, PATCHES:ROWS, :] = jnp.zeros((frames_here, ROWS - PATCHES, D), F32)
        bias = fc_bias[...].astype(F32).reshape(1, FF)
        for c in range(UNITS):
            for f in range(frame_size):
                at = (f * UNITS + c) * wide_step
                bias_rows[c : c + 1, f * wide_step : f * wide_step + wide_step] = bias[:, at : at + wide_step]

        @pl.loop(0, videos_here)
        def _(i):
            cot = cot_ref[i].astype(F32)
            for j in range(frames_here):
                wide[j, 0:PATCHES, :] = cot[:, j, :]
            for j in range(frames_here):
                b = i * frames_here + j
                cot_j = wide[j]
                cot2[rows_of(b), :] = cot_j.astype(BF)
                sums[6:7, :] += column_sum(cot_j)
                normed, _, _ = norm_fwd(kept_ref[b], vec(gain), vec(shift))
                normed2[rows_of(b), :] = normed.astype(BF)
                out_acc[rows_of(b), :] = kept_ref[b] + vec(proj_bias)
                grad_acc[rows_of(b), :] = jnp.zeros((ROWS, D), F32)

        if not sliced:
            load_all().wait()
        place.meet()

    for load in loads(chunk):
        load.wait()

    @pl.when(chunk < UNITS - 1)
    def _():
        for load in loads(chunk + 1):
            load.start()

    slot = lax.rem(chunk, 2)
    if not sliced:
        for c in range(UNITS):

            @pl.when(chunk == c)
            def _(c=c):
                for f in range(frame_size):
                    at = (f * UNITS + c) * wide_step
                    fc_buf[slot, :, f * wide_step : f * wide_step + wide_step] = fc_all[:, at : at + wide_step]

    fc, proj = fc_buf.at[slot], proj_buf.at[slot]
    bias = bias_rows[pl.ds(chunk, 1), :]
    per_tile = 2 if frames % 2 == 0 else 1
    tiles = frames // per_tile

    def due(c, t, now, call):
        pl.when(jnp.logical_and(chunk == c, now == min(t, tiles - 1)))(call)

    def both(call, first):
        return lambda: pl.loop(first, first + 2)(call)

    def video():
        for unit in range(2):
            scatter.send_video(unit, MLP_PARTS[unit % 2], scatter.land(unit)[...])

    @pl.loop(0, tiles)
    def _(t):
        due(1, 1, t, both(lambda unit: scatter.stage(unit, 0), 0))
        due(2, 0, t, both(scatter.middle, 0))
        due(2, 1, t, both(lambda unit: scatter.stage(unit, 0), 2))
        due(2, 2, t, video)
        rows = rows_of(t, per_tile)
        hidden = dims(normed2[rows, :], fc[...], 1, 0) + bias
        grad_a = dims(cot2[rows, :], proj[...], 1, 1)
        gate = 0.5 * jnp.tanh(0.851 * hidden) + 0.5
        active = hidden * gate
        grad = (grad_a * (gate + 1.702 * active * (1.0 - gate))).astype(BF)
        active = active.astype(BF)
        act[rows, :] = active
        grad_h[rows, :] = grad
        bias_sums[pl.ds(chunk, 1), :] += column_sum(grad.astype(F32))
        out_acc[rows, :] += dims(active, proj[...], 1, 0)
        grad_acc[rows, :] += dims(grad, fc[...], 1, 1)

    unit = 2 * chunk

    @pl.loop(0, 2)
    def _(m):
        size = width // 2
        count = frame_size // 4
        value = dims(act[:, pl.ds(pl.multiple_of(m * size, size), size)], cot2[...], 0, 0).astype(BF)
        value = value.reshape(count, 2, 4, step, D)
        for core in range(2):
            for q in range(4):
                grads[
                    unit + 1, lax.rem(core + place.core, 2), pl.ds(m * count, count), :, q * D : q * D + D
                ] = value[:, core, q]

    @pl.loop(0, 2)
    def _(m):
        size = D // 2
        value = dims(normed2[:, pl.ds(pl.multiple_of(m * size, size), size)], grad_h[...], 0, 0).astype(BF)
        count = frame_size // 4
        value = value.reshape(count, 2, UNITS, step, width)
        for core in range(2):
            for q in range(UNITS):
                grads[
                    unit, lax.rem(core + place.core, 2), pl.ds(m * count, count), :, q * width : q * width + width
                ] = value[:, core, q]

    def raw():
        return pltpu.make_async_copy(grads.at[pl.ds(4, 2)], raw_hbm, s_raw.at[0])

    def source(unit):
        return grads.at[unit, 1]

    @pl.when(chunk == 0)
    def _():
        pl.loop(0, 2)(lambda unit: scatter.exchange0(unit, source(unit)).start())

    @pl.when(chunk == 1)
    def _():
        pl.loop(2, 4)(lambda unit: scatter.exchange0(unit, source(unit)).start())

    @pl.when(chunk == 2)
    def _():
        raw().start()
        both(scatter.middle, 2)()
        both(scatter.finish, 0)()
        for c in range(UNITS):
            for f in range(frame_size):
                at = (f * UNITS + c) * wide_step
                row, column = 2 + at // D, at % D
                sums[row : row + 1, column : column + wide_step] = bias_sums[
                    c : c + 1, f * wide_step : f * wide_step + wide_step
                ]

        @pl.loop(0, videos_here)
        def _(i):
            outs = [out_acc[rows_of(i * frames_here + j), :][:PATCHES] for j in range(frames_here)]
            out_ref[i] = jnp.stack(outs, axis=1).astype(BF)

        @pl.loop(0, frames)
        def _(b):
            rows = rows_of(b)
            _, unit, inv = norm_fwd(kept_ref[b], vec(gain), vec(shift))
            grad = grad_acc[rows, :]
            sums[0:1, :] += column_sum(grad * unit)
            sums[1:2, :] += column_sum(grad)
            grad_ref[b] = norm_back(grad, unit, inv, vec(gain)) + cot2[rows, :].astype(F32)

        @pl.loop(0, 2)
        def _(unit):
            mid_ref[unit] = scatter.land(2 + unit)[...]
            scatter.drain_video(unit)

        pl.loop(0, 4)(lambda unit: scatter.drain(unit, source(unit)))
        raw().wait()


def attn_back_kernel(
    frame_size, video_size, videos_here, frames_here,
    x_hbm, normed_hbm, w_in_hbm, msg_ref, gk_ref, gain, shift, w_out, mlp_sums, mid_ref, raw_hbm, cls_ref, *rest,
):
    msg_operands, rest = rest[:8], rest[8:]
    (
        mixed_ref, q_ref, k_ref, v_ref, p_ref, inv_ref,
        tg_ref, reduced_ref, near_ref, far_ref, totals_ref, msg_ref_out, in_ref_out, out_ref_out, msg_sums, grad_cls,
        x_ref, normed_ref, w_in, joined, staged, gqkv_all, gk_all, sums, gm_grads, gm_wide, gm_own, gm_rows, gm_all, wide, cls_grads,
        acc_mlp, *rest,
    ) = rest
    last_buffers, rest = rest[:6], rest[6:]
    (acc_near, *near_buffers), rest = rest[:7], rest[7:]
    (acc_far, *far_buffers), rest = rest[:7], rest[7:]
    (vec_near, vec_mid, vec_far), rest = rest[:3], rest[3:]
    msg_kept, (msg_gqkv, msg_mixed), msg_state, rest = list(rest[:7]), rest[7:9], rest[9:15], rest[15:]
    msg_kept.insert(6, gqkv_all.at[0:D])
    (s_late, s_msg, s_local, s_staged, s_vsend, s_vrecv, s_gsend, s_grecv), rest = rest[:8], rest[8:]
    names = ("send0", "recv0", "send_bits", "recv_bits", "send3", "recv3")
    last_sems, near_sems, far_sems = (dict(zip(names, rest[6 * i : 6 * i + 6])) for i in range(3))
    frames = videos_here * frames_here
    steps = 2 * frames
    t = pl.program_id(0)
    side, b = lax.div(t, frames), lax.rem(t, frames)
    place = Place(frame_size, video_size)
    step = D // frame_size // UNITS
    total = frames * ROWS
    each_mid, each_last, each_attn = pl.loop(0, 2), pl.loop(2, 4), pl.loop(0, UNITS)

    def scatter(acc, buffers, result, sems, first=0):
        recv0, recv_a, recv_b, recv_c, send3, recv3 = buffers
        return Scatter(place, step, acc, recv0, [recv_a, recv_b, recv_c], send3, recv3, result, sems, first)

    lasts = scatter(lambda unit, block: acc_mlp.at[unit - 2, block], last_buffers, reduced_ref, last_sems, first=2)
    near = scatter(lambda unit, block: acc_near.at[0, unit, block], near_buffers, near_ref, near_sems)
    far = scatter(lambda unit, block: acc_far.at[0, unit, block], far_buffers, far_ref, far_sems)
    vec_sems = dict(vec_send=s_vsend, vec_recv=s_vrecv)
    early = Totals(place, 0, mlp_sums, vec_near, vec_mid, vec_far, totals_ref, vec_sems)
    late = Totals(place, 1, sums, vec_near, vec_mid, vec_far, totals_ref, vec_sems)
    gather = Gather(place, gm_own, gm_rows, s_gsend, s_grecv)

    def last_source(unit):
        return raw_hbm.at[unit - 2, 1]

    def local(unit):
        return pltpu.make_async_copy(raw_hbm.at[unit - 2, 0], acc_mlp.at[unit - 2], s_local.at[unit - 2])

    def msg_loads():
        return [pltpu.make_async_copy(a, b, s_msg.at[i]) for i, (a, b) in enumerate(zip(msg_operands, msg_kept))]

    def late_loads():
        out = [
            pltpu.make_async_copy(x_hbm, x_ref, s_late.at[0]), pltpu.make_async_copy(normed_hbm, normed_ref, s_late.at[1]),
        ]
        for half_at in range(2):
            for kind in range(3):
                source = w_in_hbm.at[:, kind * D + half_at * HALF : kind * D + half_at * HALF + HALF]
                at = (half_at * 3 + kind) * HALF
                out.append(pltpu.make_async_copy(source, w_in.at[:, at : at + HALF], s_late.at[2 + half_at * 3 + kind]))
        return out

    def due(at, call):
        pl.when(t == min(at, steps - 1))(call)

    def begin():
        place.greet()
        sums[...] = jnp.zeros_like(sums)

        @each_last
        def _(unit):
            lasts.exchange0(unit, last_source(unit)).start()
            local(unit).start()

        early.start()
        for load in late_loads():
            load.start()
        for at, load in enumerate(msg_loads()):
            if at != 6:
                load.start()
        for unit in range(2):
            lasts.send_video(unit, MLP_PARTS[unit], mid_ref[unit])

    def open_lasts():
        @each_last
        def _(unit):
            local(unit).wait()
            lasts.stage(unit, 0)

    def land_lasts():
        for unit in (2, 3):
            lasts.send_video(unit, MLP_PARTS[unit % 2], lasts.land(unit)[...])

    def land(scatter, group):
        @each_attn
        def _(unit):
            scatter.send_video(unit, attn_parts(group), scatter.land(unit)[...])

    due(0, begin)
    due(2, open_lasts)
    due(4, lambda: each_mid(lasts.finish))
    due(5, early.forward)
    due(6, lambda: each_last(lasts.middle))
    due(8, land_lasts)
    due(frames + 2, lambda: each_attn(lambda unit: near.stage(unit, 0)))
    due(steps - 1, lambda: each_last(lasts.finish))
    rows = pl.ds(pl.multiple_of(b * ROWS, ROWS), ROWS)
    side_lanes = pl.ds(pl.multiple_of(side * HALF, HALF), HALF)

    @pl.when(side == 0)
    def _():
        gk_low = gk_ref[b].astype(BF)
        gk_all[b] = gk_low
        sums[0:1, :] += column_sum(gk_low.astype(F32))

    grad_mixed = dims(gk_all[b], w_out[side_lanes, :], 1, 1)
    for pair in range(PAIRS // 2):
        grads = pair_back(
            q_ref[0, pair], k_ref[0, pair], v_ref[0, pair], grad_mixed[:, lanes(pair)],
            mixed_ref[b, :, pl.ds(pl.multiple_of(side * HALF + pair * 128, 128), 128)], inv_ref[0, pair],
            lambda head, pair=pair: p_ref[0, pair, :, head * KEYS : head * KEYS + KEYS],
        )
        for kind in range(3):
            at = pl.ds(pl.multiple_of((side * 3 + kind) * HALF + pair * 128, 128), 128)
            gqkv_all[rows, at] = grads[kind][:ROWS].astype(BF)
    for row, kind in ((1, 0), (2, 2)):
        part = gqkv_all[rows, pl.ds(pl.multiple_of((side * 3 + kind) * HALF, HALF), HALF)]
        sums[row : row + 1, side_lanes] += column_sum(part.astype(F32))

    def attn_unit(m, target, left, right, lo):
        size, width = D // 2, right.shape[1]
        value = dims(left[:, :, pl.ds(pl.multiple_of(m * size, size), size)].reshape(total, size), right, 0, 0).astype(BF)
        count = frame_size // 4
        value = value.reshape(count, 2, UNITS, step, width)
        for u in range(UNITS):
            for core in range(2):
                target[lax.rem(core + place.core, 2), u, pl.ds(m * count, count), :, lo : lo + width] = value[:, core, u]

    def attn_units(group, target, scatter):
        @pl.loop(0, 2)
        def _(m):
            attn_unit(m, target, normed_ref, gqkv_all[0:total, group * 3 * HALF : (group + 1) * 3 * HALF], 0)
            if group == 0:
                attn_unit(m, target, mixed_ref, gk_all[...].reshape(total, D), 3 * HALF)

        each_attn(lambda unit: scatter.exchange0(unit, target.at[1, unit]).start())

    @pl.when(t == frames - 1)
    def _():
        for load in late_loads():
            load.wait()
        attn_units(0, acc_near, near)

    @pl.when(t == steps - 1)
    def _():
        at = JOINED - 1 - (JOINED - 1) % 16
        gm_grads[...] = jnp.zeros_like(gm_grads)
        for c in range(frames):
            piece = gqkv_all[c * ROWS + at : c * ROWS + at + 16, :].astype(F32)
            gm_grads[c : c + 1, :] = piece[PATCHES - at : PATCHES - at + 1]
            joined[c : c + 1, :] = msg_ref[c]
        _, unit, inv = norm_fwd(joined[0:frames, :], vec(gain), vec(shift))
        grad = dims(gm_grads[...].astype(BF), w_in[...], 1, 1)[0:frames]
        gm_wide[0:frames, :] = norm_back(grad, unit, inv, vec(gain))
        for i in range(videos_here):
            gm_own[i] = gm_wide[i * frames_here : i * frames_here + frames_here, :].astype(BF)
            gm_rows[place.v, i, place.f] = gm_own[i]
        gather.start()
        each_attn(near.middle)
        attn_units(1, acc_far, far)
        early.finish()
        gather.near()
        gather.forward()

        def put(i, j):
            return pltpu.make_async_copy(staged.at[j], tg_ref.at[i, :, j], s_staged.at[j])

        def norm_frames(lo, hi):
            @pl.loop(lo, hi)
            def _(i):
                x = x_ref[i].astype(F32)
                for j in range(frames_here):
                    c = i * frames_here + j
                    joined[0:PATCHES, :] = x[:, j, :]
                    joined[PATCHES:ROWS, :] = jnp.zeros((ROWS - PATCHES, D), F32)
                    joined[PATCHES : PATCHES + 1, :] = msg_ref[c]
                    _, unit, inv = norm_fwd(joined[...], vec(gain), vec(shift))
                    rows = pl.ds(pl.multiple_of(c * ROWS, ROWS), ROWS)
                    grad = dims(gqkv_all[rows, :], w_in[...], 1, 1)
                    sums[3:4, :] += column_sum(grad * unit)
                    sums[4:5, :] += column_sum(grad)
                    pl.when(i > 0)(lambda j=j: put(i - 1, j).wait())
                    staged[j] = (gk_ref[c] + norm_back(grad, unit, inv, vec(gain)))[:PATCHES]
                    put(i, j).start()

        norm_frames(0, 1)
        each_attn(lambda unit: far.stage(unit, 0))
        land(near, 0)
        norm_frames(1, videos_here)
        msg_loads()[6].start()
        late.start()
        each_attn(far.middle)
        each_attn(near.finish)
        for load in msg_loads():
            load.wait()
        for ref in (msg_sums, msg_ref_out, in_ref_out, out_ref_out):
            ref[...] = jnp.zeros_like(ref)
        count = videos_here * FRAMES

        def between():
            land(far, 1)
            late.forward()
            gather.finish()
            for video in range(video_size):
                for i in range(videos_here):
                    for f in range(frame_size):
                        at_row = (i * frame_size + f) * frames_here
                        wide[at_row : at_row + frames_here, :] = gm_rows[video, i, f].astype(F32)
                gm_all[video * count : video * count + count, :] = wide[...].astype(BF)

        blocks = video_size * count // BLOCK
        if blocks > 1:
            between()

        @pl.loop(0, blocks)
        def _(block):
            at = pl.ds(pl.multiple_of(block * BLOCK, BLOCK), BLOCK)
            msg_back_block(
                place, cls_ref[at, :], gm_all.at[at], msg_kept, msg_ref_out, in_ref_out, out_ref_out, msg_sums, cls_grads.at[at],
                msg_state, msg_gqkv, msg_mixed, between if blocks == 1 else lambda: None,
            )

        for i in range(videos_here):
            for j in range(frames_here):
                row = (place.v * videos_here + i) * FRAMES + place.f * frames_here + j
                grad_cls[i * frames_here + j] = cls_grads[pl.ds(row, 1), :]
        for j in range(frames_here):
            put(videos_here - 1, j).wait()
        late.finish()
        each_attn(far.finish)
        each_last(lambda unit: lasts.drain(unit, last_source(unit)))
        pl.loop(0, 4)(lasts.drain_video)

        @each_attn
        def _(unit):
            for scatter, target in ((near, acc_near), (far, acc_far)):
                scatter.drain(unit, target.at[1, unit])
                scatter.drain_video(unit)


def msg_back_block(place, cls, gm_ref, kept, acc_msg, acc_in, acc_out, sums, cls_grad, scratch, gqkv, grad_mixed, between):
    bias, gain, shift, in_bias, out_bias, w_msg, w_in, w_out = kept
    qkv, probs, invs, mixed, normed, _ = scratch
    own_rows = D // place.F
    padded = acc_msg.shape[0]

    def own_columns(x):
        return pltpu.roll(x.astype(F32), lax.rem(D - place.f * own_rows, D), 1)[:, :padded].astype(BF)

    unit, inv_std = msg_forward(cls, (bias, gain, shift, in_bias, out_bias), w_msg, w_in, w_out, scratch, PAIRS // 2)
    between()
    gm = gm_ref[...]
    acc_out[...] += dims(own_columns(mixed[...]), gm, 0, 0)
    sums[5:6, :] += column_sum(gm.astype(F32))
    grad_mixed[...] = dims(gm, w_out[...], 1, 1)

    @pl.loop(0, PAIRS, unroll=PAIRS // 2)
    def _(pair):
        at = pair_lanes(pair)
        grads = pair_back(
            qkv[:, at], qkv[:, pair_lanes(pair, 1)], qkv[:, pair_lanes(pair, 2)], grad_mixed[:, at],
            mixed[:, at], invs[:, at], lambda head: probs[2 * pair + head],
        )
        for kind in range(3):
            gqkv[:, pair_lanes(pair, kind)] = grads[kind].astype(BF)

    own_normed = own_columns(normed[...])
    grad = None
    for kind in range(3):
        columns = slice(kind * D, kind * D + D)
        part = gqkv[:, columns]
        acc_in[:, columns] += dims(own_normed, part, 0, 0)
        if kind != 1:
            row = 3 + kind // 2
            sums[row : row + 1, :] += column_sum(part.astype(F32))
        term = dims(part, w_in[:, columns], 1, 1)
        grad = term if grad is None else grad + term
    sums[1:2, :] += column_sum(grad * unit)
    sums[2:3, :] += column_sum(grad)
    grad_message = norm_back(grad, unit, inv_std, vec(gain)) + gm.astype(F32)
    grad_message = grad_message.astype(BF)
    acc_msg[...] += dims(own_columns(cls), grad_message, 0, 0)
    sums[0:1, :] += column_sum(grad_message.astype(F32))
    cls_grad[...] = dims(grad_message, w_msg[...], 1, 1)


def collect_kernel(
    frame_size, video_size, videos_here, frames_here,
    done, reduced, near, far, totals, acc_msg, acc_in, acc_out, sums, grad_cls, tg_hbm, output_hbm,
    output, tokens_grad, msg_grad, in_grad, out_grad, *rest,
):
    (
        msg_bias_g, msg_gain_g, msg_shift_g, msg_in_bias_g, msg_out_bias_g, gain1_g, shift1_g,
        attn_in_g, attn_in_bias_g, attn_out_g, attn_out_bias_g, gain2_g, shift2_g, fc_g, fc_bias_g, proj_g, proj_bias_g,
        tg, out, sem,
    ) = rest
    f, v = lax.axis_index("frame"), lax.axis_index("video")
    own_rows = D // frame_size

    def load(i):
        return pltpu.make_async_copy(tg_hbm.at[i], tg.at[i], sem.at[0, i])

    def store(i):
        return pltpu.make_async_copy(tg.at[i], tokens_grad.at[i], sem.at[0, i])

    def load_out(i):
        return pltpu.make_async_copy(output_hbm.at[i], out.at[i], sem.at[1, i])

    def store_out(i):
        return pltpu.make_async_copy(out.at[i], output.at[i], sem.at[1, i])

    for i in range(videos_here):
        load(i).start()
        load_out(i).start()
    for i in range(videos_here):
        load(i).wait()
        added = [grad_cls[i * frames_here + j] for j in range(frames_here)]
        tg[i, 0] = tg[i, 0] + jnp.concatenate(added, axis=0)
        store(i).start()
        load_out(i).wait()
        store_out(i).start()

    def own_matrix(target, x):
        size = x.shape[1] // video_size
        target[...] = pltpu.roll(x[:own_rows], lax.rem(x.shape[1] - v * size, x.shape[1]), 1)[:, :size]

    own_matrix(msg_grad, acc_msg[...])
    own_matrix(in_grad, acc_in[...])
    own_matrix(out_grad, acc_out[...])

    def own_vector(target, ref, first, count):
        size = count * D // frame_size
        per_row = frame_size // count
        row = first + lax.div(f, per_row)
        x = ref[pl.ds(row, 1), :]
        x = pltpu.roll(jnp.broadcast_to(x, (8, D)), lax.rem(D - lax.rem(f, per_row) * size, D), 1)
        target[...] = x[0:1, :size].reshape(size)

    mlp_sums, attn_sums = totals.at[0], totals.at[1]
    for target, ref, first, count in (
        (msg_bias_g, sums, 0, 1), (msg_gain_g, sums, 1, 1), (msg_shift_g, sums, 2, 1), (msg_in_bias_g, sums, 3, 2),
        (msg_out_bias_g, sums, 5, 1), (gain1_g, attn_sums, 3, 1), (shift1_g, attn_sums, 4, 1),
        (attn_in_bias_g, attn_sums, 1, 2), (attn_out_bias_g, attn_sums, 0, 1), (gain2_g, mlp_sums, 0, 1),
        (shift2_g, mlp_sums, 1, 1), (fc_bias_g, mlp_sums, 2, 4), (proj_bias_g, mlp_sums, 6, 1),
    ):
        own_vector(target, ref, first, count)
    step = own_rows // UNITS
    columns = D // video_size
    wide_step = 4 * step
    part = FF // UNITS // video_size
    fc = [done[0], reduced[0], reduced[2]]
    for c in range(UNITS):
        for q in range(UNITS):
            for g in range(frame_size // video_size):
                from_at = q * part + g * wide_step
                to = (g * UNITS + c) * wide_step
                fc_g[q * step : q * step + step, to : to + wide_step] = fc[c][:, from_at : from_at + wide_step]
    for u in range(UNITS):
        rows = slice(u * step, u * step + step)
        attn_out_g[rows, :] = near[u][:, in_width(video_size) :]
        for w in range(video_size):

            @pl.when(v == w)
            def _(rows=rows, u=u, w=w):
                for group, parts in enumerate((near, far)):
                    at = 0
                    for _, count, to in in_pieces(group, w, video_size):
                        attn_in_g[rows, to : to + count] = parts[u][:, at : at + count]
                        at += count

    proj = [done[1], reduced[1], reduced[3]]
    proj = [x[:, q * columns : q * columns + columns] for x in proj for q in range(4)]
    proj_g[...] = jnp.concatenate(proj, axis=0).T
    for i in range(videos_here):
        store(i).wait()
        store_out(i).wait()


def shaped(shape, dtype):
    return jax.ShapeDtypeStruct(shape, dtype)


def whole(array):
    shape = array.shape
    return pl.BlockSpec(shape, lambda *_: (0,) * len(shape), pipeline_mode=pl.Buffered(1))


def wholes(*arrays):
    return [whole(array) for array in arrays]


def in_hbm():
    return pl.BlockSpec(memory_space=pl.ANY)


def in_vmem():
    return pl.BlockSpec(memory_space=pltpu.VMEM)


def per_step(count, shape):
    return pl.BlockSpec((count,) + shape, lambda b: (b,) + (0,) * len(shape))


def params(mib, **more):
    return pltpu.CompilerParams(vmem_limit_bytes=mib * MIB, **more)


def on_device(frame_size, video_size, *args):
    (
        tokens, cotangent, msg_weight, msg_bias, msg_norm_gain, msg_norm_shift, msg_in_weight,
        msg_in_bias, msg_out_weight, msg_out_bias, norm1_gain, norm1_shift, attn_in_weight,
        attn_in_bias, attn_out_weight, attn_out_bias, norm2_gain, norm2_shift, fc_weight, fc_bias,
        proj_weight, proj_bias,
    ) = args
    videos_here, frames_here = tokens.shape[:2]
    frames = videos_here * frames_here
    msgs = videos_here * video_size * FRAMES
    group = videos_here * FRAMES
    total = frames * ROWS
    F, V = frame_size, video_size
    step = D // F // UNITS
    n_bits = int(math.log2(F)) - 1
    x = tokens.transpose(0, 2, 1, 3)
    cot = cotangent.transpose(0, 2, 1, 3)
    msg_vectors = (msg_bias, msg_norm_gain, msg_norm_shift, msg_in_bias, msg_out_bias)
    DMA = pltpu.SemaphoreType.DMA

    msg_arrays = (*msg_vectors, msg_weight, msg_in_weight, msg_out_weight)
    kv_shape = (frames, PAIRS, KEYS, 128)

    def second(shape):
        zeros = (0,) * len(shape)
        return pl.BlockSpec((frames_here,) + shape, lambda t: (jnp.maximum(t - videos_here, 0),) + zeros)

    block_shapes = [(PAIRS, ROWS, 2 * KEYS), (PAIRS, ROWS, 128), (ROWS, D), (ROWS, D)]
    fwd_outs = [
        shaped((frames, PAIRS, ROWS, 128), BF), shaped(kv_shape, BF), shaped(kv_shape, BF), shaped((frames, ROWS, D), BF),
        shaped((frames,) + block_shapes[0], BF), shaped((frames,) + block_shapes[1], F32),
        shaped((frames,) + block_shapes[2], BF), shaped((frames,) + block_shapes[3], F32),
        shaped((frames, 1, D), F32), shaped((msgs, D), BF),
    ]
    q, k, v, normed, p, inv, mixed, kept, msg_out, cls = pl.pallas_call(
        functools.partial(attn_fwd_kernel, F, V, frames_here, videos_here),
        grid=(2 * videos_here,),
        in_specs=[
            pl.BlockSpec((1, PATCHES, frames_here, D), lambda t: (jnp.minimum(t, videos_here - 1), 0, 0, 0)), in_hbm(),
        ]
        + wholes(norm1_gain, norm1_shift, attn_in_bias, attn_out_bias, attn_in_weight) + [in_hbm()] * 9,
        out_specs=[in_hbm()] * 4 + [second(shape) for shape in block_shapes] + wholes(*fwd_outs[8:]),
        out_shape=fwd_outs,
        scratch_shapes=[pltpu.VMEM(out.shape, BF) for out in fwd_outs[:4]]
        + [
            pltpu.VMEM((frames, ROWS, D), F32), pltpu.VMEM((D, D), BF),
            pltpu.VMEM((16, D), F32), pltpu.VMEM((16, 3 * D), F32),
            pltpu.VMEM((videos_here, frames_here, D), BF),
            pltpu.VMEM((V, videos_here, F, frames_here, D), BF),
            pltpu.VMEM((group, D), F32), pltpu.VMEM((group, D), F32),
        ]
        + [pltpu.VMEM(a.shape, BF) for a in msg_arrays]
        + msg_scratch(group) + [DMA((V, F + V)), DMA((V, F + V)), DMA((11,)), DMA((4,))],
        compiler_params=params(63, collective_id=1, has_side_effects=True),
        name="attn_fwd",
    )(x, x, norm1_gain, norm1_shift, attn_in_bias, attn_out_bias, attn_in_weight, attn_out_weight, *msg_arrays)

    def bit_buffers(units, width=FF):
        return [
            pltpu.VMEM((units, max(1, F >> (2 + i)), step, width), BF) if i < n_bits else pltpu.VMEM((1, 1, 16, 128), BF)
            for i in range(3)
        ]

    def exchange_sems(units):
        return [DMA((units,)), DMA((units,)), DMA((units, n_bits, F // 4)), DMA((units, n_bits, F // 4)), DMA((units, V)), DMA((units, V))]

    def unit_buffers(count, units):
        return [pltpu.VMEM((count,) + shape, BF) for shape in units]

    block_shape = (F // 2, step, FF)
    part_shape = (V, step, FF // V)
    width = FF // UNITS
    mlp_outs = [
        shaped(x.shape, BF), shaped(kept.shape, F32), shaped((2, step, FF // V), F32), shaped((2, step, FF), BF),
        shaped((2, 2) + block_shape, BF), shaped((8, D), F32),
    ]
    output, grad_kept, done, mid, raw, mlp_sums = pl.pallas_call(
        functools.partial(mlp_kernel, F, V, videos_here, frames_here),
        grid=(UNITS,),
        in_specs=wholes(kept, cot, norm2_gain, norm2_shift, fc_bias, proj_bias) + [in_hbm(), in_hbm()],
        out_specs=wholes(*mlp_outs[:4]) + [in_hbm()] + wholes(mlp_outs[5]),
        out_shape=mlp_outs,
        scratch_shapes=[
            pltpu.VMEM((frames_here, ROWS, D), F32),
            pltpu.VMEM((total, D), BF), pltpu.VMEM((total, D), BF), pltpu.VMEM((total, width), BF), pltpu.VMEM((total, width), BF),
            pltpu.VMEM((total, D), F32), pltpu.VMEM((total, D), F32),
            pltpu.VMEM((UNITS, width), F32), pltpu.VMEM((UNITS, width), F32),
            pltpu.VMEM((2, D, width), BF), pltpu.VMEM((2, width, D), BF),
            pltpu.VMEM((D, FF) if 4 * step % 128 else (16, 128), BF),
            pltpu.VMEM((2 * UNITS, 2) + block_shape, BF), pltpu.VMEM((4,) + block_shape, BF),
        ]
        + bit_buffers(4) + unit_buffers(2, [part_shape] * 2)
        + [DMA((2, 2, F)), DMA((1,))] + exchange_sems(4),
        compiler_params=params(63, collective_id=2, has_side_effects=True),
        name="mlp",
    )(kept, cot, norm2_gain, norm2_shift, fc_bias, proj_bias, fc_weight, proj_weight)

    rows_own, columns = D // F, D // V
    padded = -(-rows_own // 128) * 128
    widths = (3 * HALF + D, 3 * HALF)
    part_widths = (in_width(V) + columns, in_width(V))
    back_outs = [
        shaped(x.shape, F32), shaped((4, step, FF // V), F32), shaped((UNITS, step, part_widths[0]), F32),
        shaped((UNITS, step, part_widths[1]), F32), shaped((2, 8, D), F32),
        shaped((padded, D), F32), shaped((padded, 3 * D), F32), shaped((padded, D), F32), shaped((8, D), F32),
        shaped((frames, 1, D), F32),
    ]
    def group_buffers(width, part_width):
        block = (F // 2, step, width)
        return [pltpu.VMEM((2, UNITS) + block, BF), pltpu.VMEM((UNITS,) + block, BF)] + bit_buffers(UNITS, width) + [
            pltpu.VMEM((UNITS, V, step, part_width), BF)
        ] * 2

    def by_pairs(shape):
        return pl.BlockSpec((1, PAIRS // 2) + shape, lambda t: (lax.rem(t, frames), lax.div(t, frames), 0, 0))

    tg, reduced, near, far, totals, acc_msg, acc_in, acc_out, msg_sums, grad_cls = pl.pallas_call(
        functools.partial(attn_back_kernel, F, V, videos_here, frames_here),
        grid=(2 * frames,),
        in_specs=[in_hbm()] * 3
        + wholes(msg_out, grad_kept, norm1_gain, norm1_shift, attn_out_weight, mlp_sums, mid)
        + [in_hbm()] + wholes(cls) + [in_hbm()] * 8 + wholes(mixed)
        + [by_pairs(shape) for shape in ((ROWS, 128), (KEYS, 128), (KEYS, 128), (ROWS, 2 * KEYS), (ROWS, 128))],
        out_specs=[in_hbm()] + wholes(*back_outs[1:]),
        out_shape=back_outs,
        scratch_shapes=[
            pltpu.VMEM(x.shape, BF), pltpu.VMEM(normed.shape, BF), pltpu.VMEM((D, 3 * D), BF),
            pltpu.VMEM((ROWS, D), F32), pltpu.VMEM((frames_here, PATCHES, D), F32),
            pltpu.VMEM((max(total, D), 3 * D), BF), pltpu.VMEM((frames, ROWS, D), BF), pltpu.VMEM((8, D), F32), pltpu.VMEM((16, 3 * D), F32), pltpu.VMEM((8, D), F32),
            pltpu.VMEM((videos_here, frames_here, D), BF), pltpu.VMEM((V, videos_here, F, frames_here, D), BF),
            pltpu.VMEM((msgs, D), BF), pltpu.VMEM((group, D), F32), pltpu.VMEM((msgs, D), F32),
            pltpu.VMEM((2,) + block_shape, BF), pltpu.VMEM((2,) + block_shape, BF),
        ]
        + bit_buffers(2) + unit_buffers(4, [part_shape] * 2)
        + group_buffers(widths[0], part_widths[0]) + group_buffers(widths[1], part_widths[1])
        + [pltpu.VMEM((2, F, 8, D), F32), pltpu.VMEM((2, 8, D), F32), pltpu.VMEM((2, V, 8, D), F32)]
        + [pltpu.VMEM(a.shape, BF) for a in msg_arrays if a is not msg_in_weight]
        + [pltpu.VMEM((BLOCK, 3 * D), BF), pltpu.VMEM((BLOCK, D), F32)] + msg_scratch(BLOCK)
        + [DMA((8,)), DMA((8,)), DMA((2,)), DMA((frames_here,))]
        + [DMA((2, 2, max(F, V))), DMA((2, 2, max(F, V))), DMA((V, F + V)), DMA((V, F + V))]
        + exchange_sems(4) + exchange_sems(UNITS) + exchange_sems(UNITS),
        compiler_params=params(63, collective_id=3, has_side_effects=True),
        name="attn_back",
    )(
        x, normed, attn_in_weight, msg_out, grad_kept, norm1_gain, norm1_shift, attn_out_weight, mlp_sums, mid, raw, cls,
        *msg_arrays, mixed, q, k, v, p, inv,
    )

    out_shapes = [
        (rows_own, columns), (rows_own, 3 * columns), (rows_own, columns),
        (rows_own,), (rows_own,), (rows_own,), (2 * rows_own,), (rows_own,), (rows_own,), (rows_own,),
        (rows_own, 3 * columns), (2 * rows_own,), (rows_own, columns), (rows_own,), (rows_own,), (rows_own,),
        (rows_own, 4 * columns), (4 * rows_own,), (columns, 4 * rows_own), (rows_own,),
    ]
    out_shapes = [shaped(shape, F32) for shape in out_shapes]
    (
        output, tokens_grad, msg_grad, msg_in_grad, msg_out_grad,
        msg_bias_g, msg_gain_g, msg_shift_g, msg_in_bias_g, msg_out_bias_g, gain1_g, shift1_g,
        attn_in_g, attn_in_bias_g, attn_out_g, attn_out_bias_g, gain2_g, shift2_g, fc_g, fc_bias_g, proj_g, proj_bias_g,
    ) = pl.pallas_call(
        functools.partial(collect_kernel, F, V, videos_here, frames_here),
        grid=(1,),
        in_specs=wholes(done, reduced, near, far, totals, acc_msg, acc_in, acc_out, msg_sums, grad_cls) + [in_hbm()] * 2,
        out_specs=[in_hbm()] * 2 + wholes(*out_shapes),
        out_shape=[shaped(x.shape, BF), shaped(x.shape, F32)] + out_shapes,
        scratch_shapes=[pltpu.VMEM(x.shape, F32), pltpu.VMEM(x.shape, BF), DMA((2, videos_here))],
        compiler_params=params(63),
        name="collect",
    )(done, reduced, near, far, totals, acc_msg, acc_in, acc_out, msg_sums, grad_cls, tg, output)

    return (
        output.transpose(0, 2, 1, 3), tokens_grad.transpose(0, 2, 1, 3),
        msg_grad, msg_bias_g, msg_gain_g, msg_shift_g, msg_in_grad, msg_in_bias_g, msg_out_grad, msg_out_bias_g,
        gain1_g, shift1_g, attn_in_g, attn_in_bias_g, attn_out_g, attn_out_bias_g,
        gain2_g, shift2_g, fc_g, fc_bias_g, proj_g.T, proj_bias_g,
    )


def solution(mesh):
    rows = P("video", "frame", None, None)
    matrix, vector = P("frame", "video"), P("frame")
    out_specs = (
        rows, rows,
        matrix, vector, vector, vector, matrix, vector, matrix, vector,
        vector, vector, matrix, vector, matrix, vector,
        vector, vector, matrix, vector, matrix, vector,
    )
    return jax.shard_map(
        functools.partial(on_device, mesh.shape["frame"], mesh.shape["video"]),
        mesh=mesh, in_specs=(rows, rows) + (P(),) * 20, out_specs=out_specs, check_vma=False,
    )
```

```python
import functools
import math

import jax
import jax.numpy as jnp
from jax import lax
from jax.experimental import pallas as pl
from jax.experimental.pallas import tpu as pltpu
from jax.sharding import PartitionSpec as P

D = 768
HEADS = 12
PAIRS = 6
FF = 3072
PATCHES = 197
JOINED = 198
ROWS = 208
KEYS = 256
HALF = D // 2
FRAMES = 16
BLOCK = 192
UNITS = 3
BF = jnp.bfloat16
F32 = jnp.float32
MIB = 1 << 20
MESH = pl.DeviceIdType.MESH


def vec(ref, at=0):
    return ref[...].astype(F32).reshape(1, ref.shape[0])[:, at * D : at * D + D]


def dims(a, b, ca, cb):
    return lax.dot_general(a, b, (((ca,), (cb,)), ((), ())), preferred_element_type=F32)


def column_sum(x):
    return jnp.sum(x, axis=0, keepdims=True)


def norm_fwd(x, gain, shift):
    centre = x - jnp.mean(x, axis=-1, keepdims=True)
    inv = lax.rsqrt(jnp.mean(centre * centre, axis=-1, keepdims=True) + 1e-05)
    unit = centre * inv
    return unit * gain + shift, unit, inv


def norm_back(grad, unit, inv, gain):
    scaled = grad * gain
    return inv * (
        scaled
        - jnp.mean(scaled, axis=-1, keepdims=True)
        - unit * jnp.mean(scaled * unit, axis=-1, keepdims=True)
    )


def low_half():
    return lax.broadcasted_iota(jnp.int32, (1, 128), 1) < 64


def half(low, head, value, other):
    return jnp.where(low, value, other) if head == 0 else jnp.where(low, other, value)


def pair_fwd(q, k, v, mask_scores, keep):
    low = low_half()
    sums = []
    for head in range(2):
        scores = mask_scores(dims(q, half(low, head, k, jnp.zeros_like(k)), 1, 1))
        top = jnp.max(scores, axis=1, keepdims=True)
        probs = jnp.exp(scores - top).astype(BF)
        keep(head, probs)
        sums.append(dims(probs, half(low, head, v, jnp.ones_like(v)), 1, 0))
    inv = 1.0 / pltpu.roll(jnp.where(low, sums[1], sums[0]), 64, 1)
    return jnp.where(low, sums[0], sums[1]) * inv, inv


def pair_back(q, k, v, grad, mixed, inv, probs):
    low = low_half()
    scaled = grad * inv
    scaled_low = scaled.astype(BF)
    minus = -pltpu.roll(mixed.astype(F32) * scaled, 64, 1)
    totals = None
    for head in range(2):
        p = probs(head)
        centred = dims(half(low, head, scaled, minus).astype(BF), half(low, head, v, jnp.ones_like(v)), 1, 1)
        grad_s = (p.astype(F32) * centred).astype(BF)
        terms = (
            dims(grad_s, half(low, head, k, jnp.zeros_like(k)), 1, 0),
            dims(grad_s, half(low, head, q, jnp.zeros_like(q)), 0, 0),
            dims(p, half(low, head, scaled_low, jnp.zeros_like(scaled_low)), 0, 0),
        )
        totals = terms if totals is None else tuple(a + b for a, b in zip(totals, terms))
    return totals[0] * 0.125, totals[1], totals[2]


def lanes(pair):
    return slice(pair * 128, pair * 128 + 128)


def msg_mask(rows):
    row = lax.broadcasted_iota(jnp.int32, (rows, rows), 0) // FRAMES
    col = lax.broadcasted_iota(jnp.int32, (rows, rows), 1) // FRAMES
    same = row == col
    return lambda scores: jnp.where(same, scores, -1e30)


def msg_scratch(rows):
    return [
        pltpu.VMEM((rows, 3 * D), BF), pltpu.VMEM((HEADS, rows, rows), BF), pltpu.VMEM((rows, D), F32), pltpu.VMEM((rows, D), BF),
        pltpu.VMEM((rows, D), BF), pltpu.VMEM((rows, D), F32),
    ]


def pair_lanes(pair, kind=0):
    return pl.ds(pl.multiple_of(kind * D + pair * 128, 128), 128)


def msg_forward(cls, biases, w_msg, w_in, w_out, scratch, unroll):
    bias, gain, shift, in_bias, _ = biases
    qkv, probs, invs, mixed, normed_low, message = scratch
    message[...] = dims(cls, w_msg[...], 1, 0) + vec(bias)
    normed, unit, inv_std = norm_fwd(message[...], vec(gain), vec(shift))
    normed_low[...] = normed.astype(BF)

    def project(kind, bias, scale):
        columns = slice(kind * D, kind * D + D)
        qkv[:, columns] = ((dims(normed_low[...], w_in[:, columns], 1, 0) + bias) * scale).astype(BF)

    project(0, vec(in_bias), 0.125)
    project(1, 0.0, 1.0)
    project(2, vec(in_bias, 1), 1.0)
    mask = msg_mask(cls.shape[0])

    @pl.loop(0, PAIRS, unroll=unroll)
    def _(pair):
        def keep(head, p):
            probs[2 * pair + head] = p

        out, inv = pair_fwd(qkv[:, pair_lanes(pair)], qkv[:, pair_lanes(pair, 1)], qkv[:, pair_lanes(pair, 2)], mask, keep)
        mixed[:, pair_lanes(pair)] = out.astype(BF)
        invs[:, pair_lanes(pair)] = inv

    return unit, inv_std


class Place:
    def __init__(self, frame_size, video_size):
        self.F, self.V = frame_size, video_size
        self.f, self.v = lax.axis_index("frame"), lax.axis_index("video")
        self.core = lax.rem(self.f, 2)
        self.bits = [lax.rem(lax.div(self.f, 1 << i), 2) for i in range(int(math.log2(frame_size)))]

    def frame_peer(self, step):
        return {"frame": lax.rem(self.f + step, self.F)}

    def video_peer(self, step):
        return {"video": lax.rem(self.v + step, self.V)}

    def greet(self):
        self.announce()
        self.meet()

    def announce(self):
        barrier = pltpu.get_barrier_semaphore()

        @pl.loop(1, self.F)
        def _(step):
            pl.semaphore_signal(barrier, inc=1, device_id=self.frame_peer(step), device_id_type=MESH)

        @pl.loop(1, self.V)
        def _(step):
            pl.semaphore_signal(barrier, inc=1, device_id=self.video_peer(step), device_id_type=MESH)

    def meet(self):
        pl.semaphore_wait(pltpu.get_barrier_semaphore(), self.F + self.V - 2)


def remote(src, dst, send, recv, peer):
    return pltpu.make_async_remote_copy(
        src_ref=src, dst_ref=dst, send_sem=send, recv_sem=recv, device_id=peer, device_id_type=MESH
    )


class Gather:
    def __init__(self, place, own, rows, send, recv):
        self.place, self.own, self.rows, self.send, self.recv = place, own, rows, send, recv

    def near_copy(self, step, arriving):
        place = self.place
        frame = lax.rem(place.f + place.F - step, place.F) if arriving else place.f
        return remote(
            self.own, self.rows.at[place.v, :, frame], self.send.at[0, step], self.recv.at[0, step], place.frame_peer(step)
        )

    def far_copy(self, hop, arriving):
        place = self.place
        video = lax.rem(place.v + place.V - hop, place.V) if arriving else place.v
        slot = place.F - 1 + hop
        return remote(
            self.own, self.rows.at[video, :, place.f], self.send.at[0, slot], self.recv.at[0, slot], place.video_peer(hop)
        )

    def passed_copy(self, hop, step, arriving):
        place = self.place
        video = lax.rem(place.v + place.V - hop, place.V)
        frame = lax.rem(place.f + place.F - step, place.F) if arriving else place.f
        part = self.rows.at[video, :, frame]
        return remote(part, part, self.send.at[hop, step], self.recv.at[hop, step], place.frame_peer(step))

    def each_frame(self, call):
        pl.loop(1, self.place.F)(call)

    def each_video(self, call):
        pl.loop(1, self.place.V)(call)

    def start(self, far=True):
        self.each_frame(lambda step: self.near_copy(step, False).start())
        self.each_video(lambda hop: self.far_copy(hop, False).start())

    def near(self):
        self.each_frame(lambda step: self.near_copy(step, True).wait_recv())

    def forward(self):
        @pl.loop(1, self.place.V)
        def _(hop):
            self.far_copy(hop, True).wait_recv()
            self.each_frame(lambda step: self.passed_copy(hop, step, False).start())

    def finish(self):
        @pl.loop(1, self.place.V)
        def _(hop):
            def passed(step):
                self.passed_copy(hop, step, True).wait_recv()
                self.passed_copy(hop, step, False).wait_send()

            self.each_frame(passed)
            self.far_copy(hop, False).wait_send()

        self.each_frame(lambda step: self.near_copy(step, False).wait_send())


def attn_fwd_kernel(
    frame_size, video_size, frames_here, videos_here,
    x_ref, x_hbm, gain1, shift1, in_bias1, out_bias1, w_in1, w_out_hbm, *rest,
):
    operands, rest = rest[:8], rest[8:]
    (
        q_hbm, k_hbm, v_hbm, normed_hbm, p_ref, inv_ref, mixed_ref, kept_ref, out_ref, cls_ref,
        q_ref, k_ref, v_ref, normed_ref, joined, w_out1, msg_rows, msg_wide, own, rows, wide, mixed_out, *rest,
    ) = rest
    kept, scratch, (send, recv, local, s_out) = rest[:8], rest[8:14], rest[14:]
    bias, gain, shift, in_bias, out_bias, w_msg, w_in, w_out = kept
    place = Place(frame_size, video_size)
    t = pl.program_id(0)
    i = lax.rem(t, videos_here)
    frames = videos_here * frames_here
    every = frames_here * ROWS
    gather = Gather(place, own, rows, send, recv)

    def loads():
        pairs = [(x_hbm.at[:, 0], own), (x_hbm.at[:, 0], rows.at[place.v, :, place.f]), (w_out_hbm, w_out1)]
        pairs += list(zip(operands, kept))
        return [pltpu.make_async_copy(source, target, local.at[at]) for at, (source, target) in enumerate(pairs)]

    def stores():
        pairs = ((q_ref, q_hbm), (k_ref, k_hbm), (v_ref, v_hbm), (normed_ref, normed_hbm))
        return [pltpu.make_async_copy(source, target, s_out.at[at]) for at, (source, target) in enumerate(pairs)]

    @pl.when(t == 0)
    def _():
        place.announce()
        for load in loads():
            load.start()

    @pl.when(t == min(1, videos_here - 1))
    def _():
        for load in loads()[:2]:
            load.wait()
        place.meet()
        gather.start()

    @pl.when(t < videos_here)
    def _():
        x = x_ref[0].astype(F32)
        first = i * frames_here
        for j in range(frames_here):
            joined[first + j, 0:PATCHES, :] = x[:, j, :]
            joined[first + j, PATCHES:ROWS, :] = jnp.zeros((ROWS - PATCHES, D), F32)
        here = pl.ds(first, frames_here)
        normed, _, _ = norm_fwd(joined[here].reshape(every, D), vec(gain1), vec(shift1))
        normed_ref[here] = normed.astype(BF).reshape(frames_here, ROWS, D)
        normed = normed_ref[here].reshape(every, D)
        pad = jnp.zeros((KEYS - ROWS, 128), BF)
        q = ((dims(normed, w_in1[:, :D], 1, 0) + vec(in_bias1)) * 0.125).astype(BF)
        k = dims(normed, w_in1[:, D : 2 * D], 1, 0).astype(BF)
        v = (dims(normed, w_in1[:, 2 * D :], 1, 0) + vec(in_bias1, 1)).astype(BF)
        for j in range(frames_here):
            part = slice(j * ROWS, j * ROWS + ROWS)
            for pair in range(PAIRS):
                sl = lanes(pair)
                q_ref[first + j, pair] = q[part, sl]
                k_ref[first + j, pair, 0:ROWS] = k[part, sl]
                k_ref[first + j, pair, ROWS:KEYS] = pad
                v_ref[first + j, pair, 0:ROWS] = v[part, sl]
                v_ref[first + j, pair, ROWS:KEYS] = pad

    def unpack(video):
        for n in range(videos_here):
            for f in range(frame_size):
                at = (n * frame_size + f) * frames_here
                wide[at : at + frames_here, :] = rows[video, n, f].astype(F32)

    @pl.when(t == videos_here)
    def _():
        gather.near()
        gather.forward()
        unpack(place.v)
        for load in loads()[2:]:
            load.wait()
        biases = (bias, gain, shift, in_bias, out_bias)
        msg_forward(wide[...].astype(BF), biases, w_msg, w_in, w_out, scratch, PAIRS)
        mixed_out[...] = scratch[5][...] + dims(scratch[3][...], w_out[...], 1, 0) + vec(out_bias)
        msg_rows[...] = jnp.zeros_like(msg_rows)
        for n in range(videos_here):
            for j in range(frames_here):
                c = n * frames_here + j
                row = mixed_out[pl.ds(n * FRAMES + place.f * frames_here + j, 1), :]
                out_ref[c] = row
                msg_rows[c : c + 1, :] = row
                joined[c, PATCHES : PATCHES + 1, :] = row
        normed, _, _ = norm_fwd(msg_rows[...], vec(gain1), vec(shift1))
        low = normed.astype(BF)
        msg_wide[:, :D] = low.astype(F32)
        msg_wide[:, D : 2 * D] = dims(low, w_in1[:, D : 2 * D], 1, 0)
        msg_wide[:, 2 * D :] = dims(low, w_in1[:, 2 * D :], 1, 0) + vec(in_bias1, 1)
        at = PATCHES - PATCHES % 16
        mine = lax.broadcasted_iota(jnp.int32, (16, 1), 0) == PATCHES % 16
        block = slice(at, at + 16)

        @pl.loop(0, frames)
        def _(c):
            row = msg_wide[pl.ds(c, 1), :]
            normed_ref[c, block, :] = jnp.where(mine, row[:, :D], normed_ref[c, block, :].astype(F32)).astype(BF)
            for pair in range(PAIRS):
                for target, lo in ((k_ref, D), (v_ref, 2 * D)):
                    part = row[:, lo + pair * 128 : lo + pair * 128 + 128]
                    target[c, pair, block, :] = jnp.where(mine, part, target[c, pair, block, :].astype(F32)).astype(BF)

        for store in stores():
            store.start()

    valid = lax.broadcasted_iota(jnp.int32, (1, KEYS - 128), 1) < JOINED - 128

    def mask(scores):
        return jnp.concatenate([scores[:, :128], jnp.where(valid, scores[:, 128:], -1e30)], axis=1)

    @pl.when(t >= videos_here)
    def _():
        first = i * frames_here

        @pl.loop(0, frames_here)
        def _(j):
            c = first + j
            for pair in range(PAIRS):

                def keep(head, p, pair=pair):
                    p_ref[j, pair, :, head * KEYS : head * KEYS + KEYS] = p

                out, inv = pair_fwd(q_ref[c, pair], k_ref[c, pair], v_ref[c, pair], mask, keep)
                inv_ref[j, pair] = inv
                mixed_ref[j, :, lanes(pair)] = out.astype(BF)

        attended = dims(mixed_ref[...].reshape(every, D), w_out1[...], 1, 0) + vec(out_bias1)
        kept_ref[...] = joined[pl.ds(first, frames_here)] + attended.reshape(frames_here, ROWS, D)

    @pl.when(t == 2 * videos_here - 1)
    def _():
        gather.finish()
        count = videos_here * FRAMES
        for video in range(video_size):
            unpack(video)
            cls_ref[video * count : video * count + count, :] = wide[...].astype(BF)
        for store in stores():
            store.wait()


def fc_parts(x, w, V):
    size, width = FF // UNITS // V, FF // UNITS
    return jnp.concatenate([x[:, q * width + w * size : q * width + w * size + size] for q in range(UNITS)], axis=1)


def proj_parts(x, w, V):
    size = D // V
    return jnp.concatenate([x[:, q * D + w * size : q * D + w * size + size] for q in range(4)], axis=1)


MLP_PARTS = (fc_parts, proj_parts)


def in_pieces(group, w, V):
    size, out = 3 * D // V, []
    for kind in range(3):
        first = kind * D + group * HALF
        lo, hi = max(first, w * size), min(first + HALF, w * size + size)
        if hi > lo:
            out.append((kind * HALF + lo - first, hi - lo, lo - w * size))
    return out


def in_width(V):
    return max(sum(piece[1] for piece in in_pieces(g, w, V)) for g in range(2) for w in range(V))


def attn_parts(group):
    def parts(x, w, V):
        pieces = [x[:, at : at + count] for at, count, _ in in_pieces(group, w, V)]
        short = in_width(V) - sum(piece.shape[1] for piece in pieces)
        if short:
            pieces.append(jnp.zeros((x.shape[0], short), F32))
        if group == 0:
            size = D // V
            pieces.append(x[:, 3 * HALF + w * size : 3 * HALF + w * size + size])
        return jnp.concatenate(pieces, axis=1) if len(pieces) > 1 else pieces[0]

    return parts


class Scatter:
    def __init__(self, place, step, acc, recv0, recv_bits, send3, recv3, result, sems, first=0):
        self.place, self.step, self.acc, self.first = place, step, acc, first
        self.recv0, self.recv_bits, self.send3, self.recv3, self.result = recv0, recv_bits, send3, recv3, result
        self.sems = sems
        self.n_bits = len(place.bits) - 1

    def other_core(self):
        return {"frame": self.place.f + 1 - 2 * self.place.core}

    def exchange0(self, unit, source):
        return remote(source, self.recv0.at[unit - self.first], self.sems["send0"].at[unit], self.sems["recv0"].at[unit], self.other_core())

    def order(self, core, stage):
        return stage if core == 0 else self.n_bits - 1 - stage

    def blocks(self, stage, flip):
        place, n = self.place, self.n_bits
        free = n - 1 - stage
        out = []
        for i in range(1 << free):
            both = []
            for core in range(2):
                done = [self.order(core, s) for s in range(stage)]
                now = self.order(core, stage)
                rest = [bit for bit in range(n) if bit not in done and bit != now]
                at = 0
                for bit in done:
                    at = at + place.bits[bit + 1] * (1 << bit)
                own = place.bits[now + 1]
                at = at + ((1 - own) if flip else own) * (1 << now)
                for index, bit in enumerate(rest):
                    at = at + ((i >> index) & 1) * (1 << bit)
                both.append(at)
            out.append((1 - place.core) * both[0] + place.core * both[1])
        return out

    def partner(self, stage):
        place = self.place
        moves = []
        for core in range(2):
            bit = self.order(core, stage) + 1
            moves.append((1 - 2 * place.bits[bit]) * (1 << bit))
        return {"frame": place.f + (1 - place.core) * moves[0] + place.core * moves[1]}

    def exchange(self, unit, stage, i, block):
        sems = self.sems
        return remote(
            self.acc(unit, block), self.recv_bits[stage].at[unit - self.first, i],
            sems["send_bits"].at[unit, stage, i], sems["recv_bits"].at[unit, stage, i], self.partner(stage),
        )

    def add(self, unit, block, came):
        target = self.acc(unit, block)
        target[...] = (target[...].astype(F32) + came.astype(F32)).astype(BF)

    def stage(self, unit, stage):
        if stage == 0:
            self.exchange0(unit, self.recv0.at[unit - self.first]).wait_recv()
            came = lambda position, block: self.recv0[unit - self.first, block]
        else:
            for i in range(1 << (self.n_bits - stage)):
                self.exchange(unit, stage - 1, i, 0).wait_recv()
            came = lambda position, block: self.recv_bits[stage - 1][unit - self.first, position]
        if stage == self.n_bits:
            block = self.own_block()
            self.add(unit, block, came(0, block))
            return
        sending, staying = self.blocks(stage, True), self.blocks(stage, False)
        where = self.positions(stage)
        for i, block in enumerate(sending):
            self.add(unit, block, came(where[1][i], block))
            self.exchange(unit, stage, i, block).start()
        for i, block in enumerate(staying):
            self.add(unit, block, came(where[0][i], block))

    def positions(self, stage):
        place, n = self.place, self.n_bits
        if stage == 0:
            return [[None] * (1 << (n - 1))] * 2
        out = [[], []]
        for flip in range(2):
            for i in range(1 << (n - 1 - stage)):
                both = []
                for core in range(2):
                    done = [self.order(core, s) for s in range(stage)]
                    now = self.order(core, stage)
                    rest_before = [bit for bit in range(n) if bit not in done]
                    rest = [bit for bit in rest_before if bit != now]
                    own = place.bits[now + 1]
                    at = 0
                    for index, bit in enumerate(rest_before):
                        if bit == now:
                            at = at + ((1 - own) if flip else own) * (1 << index)
                        else:
                            at = at + ((i >> rest.index(bit)) & 1) * (1 << index)
                    both.append(at)
                out[flip].append((1 - place.core) * both[0] + place.core * both[1])
        return out

    def own_block(self):
        return lax.div(self.place.f, 2)

    def across(self, unit, hop):
        place, sems = self.place, self.sems
        to = lax.rem(place.v + hop, place.V)
        return remote(
            self.send3.at[unit, to], self.recv3.at[unit, hop],
            sems["send3"].at[unit, hop], sems["recv3"].at[unit, hop], place.video_peer(hop),
        )

    def middle(self, unit):
        for stage in range(1, self.n_bits):
            self.stage(unit, stage)

    def land(self, unit):
        self.stage(unit, self.n_bits)
        return self.acc(unit, self.own_block())

    def send_video(self, unit, parts, value):
        value = value.astype(F32)
        for w in range(self.place.V):
            self.send3[unit, w] = parts(value, w, self.place.V).astype(BF)
        pl.loop(1, self.place.V)(lambda hop: self.across(unit, hop).start())

    def finish(self, unit):
        self.result[unit] = self.send3[unit, self.place.v].astype(F32)

        @pl.loop(1, self.place.V)
        def _(hop):
            self.across(unit, hop).wait_recv()
            self.result[unit] += self.recv3[unit, hop].astype(F32)

    def drain(self, unit, source):
        self.exchange0(unit, source).wait_send()
        for stage in range(self.n_bits):
            for i in range(1 << (self.n_bits - 1 - stage)):
                self.exchange(unit, stage, i, 0).wait_send()

    def drain_video(self, unit):
        pl.loop(1, self.place.V)(lambda hop: self.across(unit, hop).wait_send())


class Totals:
    def __init__(self, place, which, own, near, middle, far, result, sems):
        self.place, self.which, self.own, self.near_buf, self.middle = place, which, own, near, middle
        self.far_buf, self.result, self.sems = far, result, sems

    def near(self, step):
        sems = self.sems
        return remote(
            self.own, self.near_buf.at[self.which, step], sems["vec_send"].at[self.which, 0, step],
            sems["vec_recv"].at[self.which, 0, step], self.place.frame_peer(step),
        )

    def far(self, hop):
        sems = self.sems
        return remote(
            self.middle.at[self.which], self.far_buf.at[self.which, hop], sems["vec_send"].at[self.which, 1, hop],
            sems["vec_recv"].at[self.which, 1, hop], self.place.video_peer(hop),
        )

    def start(self):
        pl.loop(1, self.place.F)(lambda step: self.near(step).start())

    def forward(self):
        self.middle[self.which] = self.own[...]

        @pl.loop(1, self.place.F)
        def _(step):
            self.near(step).wait_recv()
            self.middle[self.which] += self.near_buf[self.which, step]

        pl.loop(1, self.place.V)(lambda hop: self.far(hop).start())

    def finish(self):
        self.result[self.which] = self.middle[self.which]

        @pl.loop(1, self.place.V)
        def _(hop):
            self.far(hop).wait_recv()
            self.result[self.which] += self.far_buf[self.which, hop]
            self.far(hop).wait_send()

        pl.loop(1, self.place.F)(lambda step: self.near(step).wait_send())


def mlp_kernel(
    frame_size, video_size, videos_here, frames_here,
    kept_hbm, cot_hbm, gain, shift, fc_bias, proj_bias, fc_hbm, proj_hbm,
    out_hbm, grad_hbm, done_ref, mid_ref, raw_hbm, sums,
    kept_ref, cot_ref, grad_ref, wide, normed2, cot2, act, grad_h, out_acc, grad_acc, bias_rows, bias_sums, fc_buf, proj_buf, fc_all,
    grads, recv0, recv_a, recv_b, recv_c, send3, recv3,
    s_rows, s_load, s_raw, s_send0, s_recv0, s_sendb, s_recvb, s_send3, s_recv3,
):
    chunk = pl.program_id(0)
    frames = videos_here * frames_here
    place = Place(frame_size, video_size)
    step = D // frame_size // UNITS
    wide_step = 4 * step
    width = FF // UNITS
    sems = dict(send0=s_send0, recv0=s_recv0, send_bits=s_sendb, recv_bits=s_recvb, send3=s_send3, recv3=s_recv3)
    scatter = Scatter(
        place, step, lambda unit, block: grads.at[unit, 0, block], recv0, [recv_a, recv_b, recv_c], send3, recv3, done_ref, sems
    )
    sliced = wide_step % 128 == 0

    def rows_of(b, count=1):
        return pl.ds(pl.multiple_of(b * count * ROWS, ROWS), count * ROWS)

    def loads(c):
        slot = lax.rem(c, 2)
        out = []
        for f in range(frame_size):
            at = pl.multiple_of((f * UNITS + c) * wide_step, wide_step)
            to = slice(f * wide_step, f * wide_step + wide_step)
            out.append(pltpu.make_async_copy(proj_hbm.at[pl.ds(at, wide_step)], proj_buf.at[slot, to], s_load.at[slot, 0, f]))
            if sliced:
                out.append(pltpu.make_async_copy(fc_hbm.at[:, pl.ds(at, wide_step)], fc_buf.at[slot, :, to], s_load.at[slot, 1, f]))
        return out

    def row_loads(i):
        part = pl.ds(i * frames_here, frames_here)
        return [
            pltpu.make_async_copy(kept_hbm.at[part], kept_ref.at[part], s_rows.at[0, i]),
            pltpu.make_async_copy(cot_hbm.at[i], cot_ref.at[i], s_rows.at[1, i]),
        ]

    def row_stores(i):
        part = pl.ds(i * frames_here, frames_here)
        return [
            pltpu.make_async_copy(grad_ref.at[part], grad_hbm.at[part], s_rows.at[0, i]),
            pltpu.make_async_copy(cot_ref.at[i], out_hbm.at[i], s_rows.at[1, i]),
        ]

    def load_all():
        return pltpu.make_async_copy(fc_hbm, fc_all, s_load.at[0, 1, 0])

    @pl.when(chunk == 0)
    def _():
        place.announce()
        for n in range(videos_here):
            for load in row_loads(n):
                load.start()
        for load in loads(chunk):
            load.start()
        if not sliced:
            load_all().start()
        sums[...] = jnp.zeros_like(sums)
        bias_sums[...] = jnp.zeros_like(bias_sums)
        wide[:, PATCHES:ROWS, :] = jnp.zeros((frames_here, ROWS - PATCHES, D), F32)
        bias = fc_bias[...].astype(F32).reshape(1, FF)
        for c in range(UNITS):
            for f in range(frame_size):
                at = (f * UNITS + c) * wide_step
                bias_rows[c : c + 1, f * wide_step : f * wide_step + wide_step] = bias[:, at : at + wide_step]

        @pl.loop(0, videos_here)
        def _(i):
            for load in row_loads(i):
                load.wait()
            cot = cot_ref[i].astype(F32)
            for j in range(frames_here):
                wide[j, 0:PATCHES, :] = cot[:, j, :]
            for j in range(frames_here):
                b = i * frames_here + j
                cot_j = wide[j]
                cot2[rows_of(b), :] = cot_j.astype(BF)
                sums[6:7, :] += column_sum(cot_j)
                normed, _, _ = norm_fwd(kept_ref[b], vec(gain), vec(shift))
                normed2[rows_of(b), :] = normed.astype(BF)
                out_acc[rows_of(b), :] = kept_ref[b] + vec(proj_bias)
                grad_acc[rows_of(b), :] = jnp.zeros((ROWS, D), F32)

        if not sliced:
            load_all().wait()
        place.meet()

    for load in loads(chunk):
        load.wait()

    @pl.when(chunk < UNITS - 1)
    def _():
        for load in loads(chunk + 1):
            load.start()

    slot = lax.rem(chunk, 2)
    if not sliced:
        for c in range(UNITS):

            @pl.when(chunk == c)
            def _(c=c):
                for f in range(frame_size):
                    at = (f * UNITS + c) * wide_step
                    fc_buf[slot, :, f * wide_step : f * wide_step + wide_step] = fc_all[:, at : at + wide_step]

    fc, proj = fc_buf.at[slot], proj_buf.at[slot]
    bias = bias_rows[pl.ds(chunk, 1), :]
    per_tile = 2 if frames % 2 == 0 else 1
    tiles = frames // per_tile

    def due(c, t, now, call):
        pl.when(jnp.logical_and(chunk == c, now == min(t, tiles - 1)))(call)

    def both(call, first):
        return lambda: pl.loop(first, first + 2)(call)

    def video():
        for unit in range(2):
            scatter.send_video(unit, MLP_PARTS[unit % 2], scatter.land(unit)[...])

    @pl.loop(0, tiles)
    def _(t):
        due(1, 1, t, both(lambda unit: scatter.stage(unit, 0), 0))
        due(2, 0, t, both(scatter.middle, 0))
        due(2, 1, t, both(lambda unit: scatter.stage(unit, 0), 2))
        due(2, 2, t, video)
        rows = rows_of(t, per_tile)
        hidden = dims(normed2[rows, :], fc[...], 1, 0) + bias
        grad_a = dims(cot2[rows, :], proj[...], 1, 1)
        gate = 0.5 * jnp.tanh(0.851 * hidden) + 0.5
        active = hidden * gate
        grad = (grad_a * (gate + 1.702 * active * (1.0 - gate))).astype(BF)
        active = active.astype(BF)
        act[rows, :] = active
        grad_h[rows, :] = grad
        bias_sums[pl.ds(chunk, 1), :] += column_sum(grad.astype(F32))
        out_acc[rows, :] += dims(active, proj[...], 1, 0)
        grad_acc[rows, :] += dims(grad, fc[...], 1, 1)

    unit = 2 * chunk

    @pl.loop(0, 2)
    def _(m):
        size = width // 2
        count = frame_size // 4
        value = dims(act[:, pl.ds(pl.multiple_of(m * size, size), size)], cot2[...], 0, 0).astype(BF)
        value = value.reshape(count, 2, 4, step, D)
        for core in range(2):
            for q in range(4):
                grads[
                    unit + 1, lax.rem(core + place.core, 2), pl.ds(m * count, count), :, q * D : q * D + D
                ] = value[:, core, q]

    @pl.loop(0, 2)
    def _(m):
        size = D // 2
        value = dims(normed2[:, pl.ds(pl.multiple_of(m * size, size), size)], grad_h[...], 0, 0).astype(BF)
        count = frame_size // 4
        value = value.reshape(count, 2, UNITS, step, width)
        for core in range(2):
            for q in range(UNITS):
                grads[
                    unit, lax.rem(core + place.core, 2), pl.ds(m * count, count), :, q * width : q * width + width
                ] = value[:, core, q]

    def raw():
        return pltpu.make_async_copy(grads.at[pl.ds(4, 2)], raw_hbm, s_raw.at[0])

    def source(unit):
        return grads.at[unit, 1]

    @pl.when(chunk == 0)
    def _():
        pl.loop(0, 2)(lambda unit: scatter.exchange0(unit, source(unit)).start())

    @pl.when(chunk == 1)
    def _():
        pl.loop(2, 4)(lambda unit: scatter.exchange0(unit, source(unit)).start())

    @pl.when(chunk == 2)
    def _():
        raw().start()
        both(scatter.middle, 2)()
        both(scatter.finish, 0)()
        for c in range(UNITS):
            for f in range(frame_size):
                at = (f * UNITS + c) * wide_step
                row, column = 2 + at // D, at % D
                sums[row : row + 1, column : column + wide_step] = bias_sums[
                    c : c + 1, f * wide_step : f * wide_step + wide_step
                ]

        @pl.loop(0, videos_here)
        def _(i):
            outs = [out_acc[rows_of(i * frames_here + j), :][:PATCHES] for j in range(frames_here)]
            cot_ref[i] = jnp.stack(outs, axis=1).astype(BF)
            every = frames_here * ROWS
            here = pl.ds(i * frames_here, frames_here)
            rows = rows_of(i, frames_here)
            _, unit, inv = norm_fwd(kept_ref[here].reshape(every, D), vec(gain), vec(shift))
            grad = grad_acc[rows, :]
            sums[0:1, :] += column_sum(grad * unit)
            sums[1:2, :] += column_sum(grad)
            grad = norm_back(grad, unit, inv, vec(gain)) + cot2[rows, :].astype(F32)
            grad_ref[here] = grad.reshape(frames_here, ROWS, D)
            for store in row_stores(i):
                store.start()

        @pl.loop(0, 2)
        def _(unit):
            mid_ref[unit] = scatter.land(2 + unit)[...]
            scatter.drain_video(unit)

        pl.loop(0, 4)(lambda unit: scatter.drain(unit, source(unit)))
        raw().wait()
        for n in range(videos_here):
            for store in row_stores(n):
                store.wait()


def attn_back_kernel(
    frame_size, video_size, videos_here, frames_here,
    x_hbm, normed_hbm, w_in_hbm, gk_hbm, mixed_hbm, msg_ref, gain, shift, w_out, mlp_sums, mid_ref, raw_hbm, cls_ref, *rest,
):
    msg_operands, rest = rest[:8], rest[8:]
    (
        q_ref, k_ref, v_ref, p_ref, inv_ref,
        tg_ref, reduced_ref, near_ref, far_ref, totals_ref, msg_ref_out, in_ref_out, out_ref_out, msg_sums, grad_cls,
        x_ref, normed_ref, w_in, gk_ref, mixed_ref, joined, staged, gqkv_all, gk_all, sums, gm_grads, gm_wide, gm_own, gm_rows, gm_all, wide, cls_grads,
        acc_mlp, *rest,
    ) = rest
    last_buffers, rest = rest[:6], rest[6:]
    (acc_near, *near_buffers), rest = rest[:7], rest[7:]
    (acc_far, *far_buffers), rest = rest[:7], rest[7:]
    (vec_near, vec_mid, vec_far), rest = rest[:3], rest[3:]
    msg_kept, (msg_gqkv, msg_mixed), msg_state, rest = list(rest[:7]), rest[7:9], rest[9:15], rest[15:]
    msg_kept.insert(6, gqkv_all.at[0:D])
    (s_rows, s_late, s_msg, s_local, s_staged, s_vsend, s_vrecv, s_gsend, s_grecv), rest = rest[:9], rest[9:]
    names = ("send0", "recv0", "send_bits", "recv_bits", "send3", "recv3")
    last_sems, near_sems, far_sems = (dict(zip(names, rest[6 * i : 6 * i + 6])) for i in range(3))
    frames = videos_here * frames_here
    steps = 2 * frames
    t = pl.program_id(0)
    side, b = lax.div(t, frames), lax.rem(t, frames)
    place = Place(frame_size, video_size)
    step = D // frame_size // UNITS
    total = frames * ROWS
    each_mid, each_last, each_attn = pl.loop(0, 2), pl.loop(2, 4), pl.loop(0, UNITS)

    def scatter(acc, buffers, result, sems, first=0):
        recv0, recv_a, recv_b, recv_c, send3, recv3 = buffers
        return Scatter(place, step, acc, recv0, [recv_a, recv_b, recv_c], send3, recv3, result, sems, first)

    lasts = scatter(lambda unit, block: acc_mlp.at[unit - 2, block], last_buffers, reduced_ref, last_sems, first=2)
    near = scatter(lambda unit, block: acc_near.at[0, unit, block], near_buffers, near_ref, near_sems)
    far = scatter(lambda unit, block: acc_far.at[0, unit, block], far_buffers, far_ref, far_sems)
    vec_sems = dict(vec_send=s_vsend, vec_recv=s_vrecv)
    early = Totals(place, 0, mlp_sums, vec_near, vec_mid, vec_far, totals_ref, vec_sems)
    late = Totals(place, 1, sums, vec_near, vec_mid, vec_far, totals_ref, vec_sems)
    gather = Gather(place, gm_own, gm_rows, s_gsend, s_grecv)

    def last_source(unit):
        return raw_hbm.at[unit - 2, 1]

    def local(unit):
        return pltpu.make_async_copy(raw_hbm.at[unit - 2, 0], acc_mlp.at[unit - 2], s_local.at[unit - 2])

    def msg_loads():
        return [pltpu.make_async_copy(a, b, s_msg.at[i]) for i, (a, b) in enumerate(zip(msg_operands, msg_kept))]

    def row_loads(c):
        return [
            pltpu.make_async_copy(gk_hbm.at[c], gk_ref.at[c], s_rows.at[0, c]),
            pltpu.make_async_copy(mixed_hbm.at[c], mixed_ref.at[c], s_rows.at[1, c]),
        ]

    def late_loads():
        out = [
            pltpu.make_async_copy(x_hbm, x_ref, s_late.at[0]), pltpu.make_async_copy(normed_hbm, normed_ref, s_late.at[1]),
        ]
        for half_at in range(2):
            for kind in range(3):
                source = w_in_hbm.at[:, kind * D + half_at * HALF : kind * D + half_at * HALF + HALF]
                at = (half_at * 3 + kind) * HALF
                out.append(pltpu.make_async_copy(source, w_in.at[:, at : at + HALF], s_late.at[2 + half_at * 3 + kind]))
        return out

    def due(at, call):
        pl.when(t == min(at, steps - 1))(call)

    def begin():
        place.announce()

        @pl.loop(0, frames)
        def _(c):
            for load in row_loads(c):
                load.start()

        place.meet()
        sums[...] = jnp.zeros_like(sums)

        @each_last
        def _(unit):
            lasts.exchange0(unit, last_source(unit)).start()
            local(unit).start()

        early.start()
        for load in late_loads():
            load.start()
        for at, load in enumerate(msg_loads()):
            if at != 6:
                load.start()
        for unit in range(2):
            lasts.send_video(unit, MLP_PARTS[unit], mid_ref[unit])

    def open_lasts():
        @each_last
        def _(unit):
            local(unit).wait()
            lasts.stage(unit, 0)

    def land_lasts():
        for unit in (2, 3):
            lasts.send_video(unit, MLP_PARTS[unit % 2], lasts.land(unit)[...])

    def land(scatter, group):
        @each_attn
        def _(unit):
            scatter.send_video(unit, attn_parts(group), scatter.land(unit)[...])

    due(0, begin)
    due(2, open_lasts)
    due(4, lambda: each_mid(lasts.finish))
    due(5, early.forward)
    due(6, lambda: each_last(lasts.middle))
    due(8, land_lasts)
    due(frames + 2, lambda: each_attn(lambda unit: near.stage(unit, 0)))
    rows = pl.ds(pl.multiple_of(b * ROWS, ROWS), ROWS)
    side_lanes = pl.ds(pl.multiple_of(side * HALF, HALF), HALF)

    @pl.when(side == 0)
    def _():
        for load in row_loads(b):
            load.wait()
        gk_low = gk_ref[b].astype(BF)
        gk_all[b] = gk_low
        sums[0:1, :] += column_sum(gk_low.astype(F32))

    grad_mixed = dims(gk_all[b], w_out[side_lanes, :], 1, 1)
    for pair in range(PAIRS // 2):
        grads = pair_back(
            q_ref[0, pair], k_ref[0, pair], v_ref[0, pair], grad_mixed[:, lanes(pair)],
            mixed_ref[b, :, pl.ds(pl.multiple_of(side * HALF + pair * 128, 128), 128)], inv_ref[0, pair],
            lambda head, pair=pair: p_ref[0, pair, :, head * KEYS : head * KEYS + KEYS],
        )
        for kind in range(3):
            at = pl.ds(pl.multiple_of((side * 3 + kind) * HALF + pair * 128, 128), 128)
            gqkv_all[rows, at] = grads[kind][:ROWS].astype(BF)
    for row, kind in ((1, 0), (2, 2)):
        part = gqkv_all[rows, pl.ds(pl.multiple_of((side * 3 + kind) * HALF, HALF), HALF)]
        sums[row : row + 1, side_lanes] += column_sum(part.astype(F32))

    def attn_unit(m, target, left, right, lo):
        size, width = D // 2, right.shape[1]
        value = dims(left[:, :, pl.ds(pl.multiple_of(m * size, size), size)].reshape(total, size), right, 0, 0).astype(BF)
        count = frame_size // 4
        value = value.reshape(count, 2, UNITS, step, width)
        for u in range(UNITS):
            for core in range(2):
                target[lax.rem(core + place.core, 2), u, pl.ds(m * count, count), :, lo : lo + width] = value[:, core, u]

    def attn_units(group, target, scatter):
        @pl.loop(0, 2)
        def _(m):
            attn_unit(m, target, normed_ref, gqkv_all[0:total, group * 3 * HALF : (group + 1) * 3 * HALF], 0)
            if group == 0:
                attn_unit(m, target, mixed_ref, gk_all[...].reshape(total, D), 3 * HALF)

        each_attn(lambda unit: scatter.exchange0(unit, target.at[1, unit]).start())

    @pl.when(t == frames - 1)
    def _():
        for load in late_loads():
            load.wait()
        attn_units(0, acc_near, near)

    @pl.when(t == steps - 1)
    def _():
        at = JOINED - 1 - (JOINED - 1) % 16
        gm_grads[...] = jnp.zeros_like(gm_grads)
        for c in range(frames):
            piece = gqkv_all[c * ROWS + at : c * ROWS + at + 16, :].astype(F32)
            gm_grads[c : c + 1, :] = piece[PATCHES - at : PATCHES - at + 1]
            joined[0, c : c + 1, :] = msg_ref[c]
        _, unit, inv = norm_fwd(joined[0, 0:frames, :], vec(gain), vec(shift))
        grad = dims(gm_grads[...].astype(BF), w_in[...], 1, 1)[0:frames]
        gm_wide[0:frames, :] = norm_back(grad, unit, inv, vec(gain))
        for i in range(videos_here):
            gm_own[i] = gm_wide[i * frames_here : i * frames_here + frames_here, :].astype(BF)
            gm_rows[place.v, i, place.f] = gm_own[i]
        gather.start()
        each_attn(near.middle)
        attn_units(1, acc_far, far)
        each_last(lasts.finish)
        early.finish()
        gather.near()
        gather.forward()

        def put(i, j):
            return pltpu.make_async_copy(staged.at[j], tg_ref.at[i, :, j], s_staged.at[j])

        def norm_frames(lo, hi):
            @pl.loop(lo, hi)
            def _(i):
                @pl.when(i > 0)
                def _():
                    for j in range(frames_here):
                        put(i - 1, j).wait()

                x = x_ref[i].astype(F32)
                first = i * frames_here
                for j in range(frames_here):
                    joined[j, 0:PATCHES, :] = x[:, j, :]
                    joined[j, PATCHES:ROWS, :] = jnp.zeros((ROWS - PATCHES, D), F32)
                    joined[j, PATCHES : PATCHES + 1, :] = msg_ref[first + j]
                every = frames_here * ROWS
                rows = pl.ds(pl.multiple_of(first * ROWS, ROWS), every)
                grad = dims(gqkv_all[rows, :], w_in[...], 1, 1)
                _, unit, inv = norm_fwd(joined[...].reshape(every, D), vec(gain), vec(shift))
                sums[3:4, :] += column_sum(grad * unit)
                sums[4:5, :] += column_sum(grad)
                back = gk_ref[pl.ds(first, frames_here)].reshape(every, D) + norm_back(grad, unit, inv, vec(gain))
                for j in range(frames_here):
                    staged[j] = back[j * ROWS : j * ROWS + PATCHES]
                    put(i, j).start()

        norm_frames(0, 1)
        each_attn(lambda unit: far.stage(unit, 0))
        land(near, 0)
        norm_frames(1, videos_here)
        msg_loads()[6].start()
        late.start()
        each_attn(far.middle)
        each_attn(near.finish)
        for load in msg_loads():
            load.wait()
        for ref in (msg_sums, msg_ref_out, in_ref_out, out_ref_out):
            ref[...] = jnp.zeros_like(ref)
        count = videos_here * FRAMES

        def between():
            land(far, 1)
            late.forward()
            gather.finish()
            for video in range(video_size):
                for i in range(videos_here):
                    for f in range(frame_size):
                        at_row = (i * frame_size + f) * frames_here
                        wide[at_row : at_row + frames_here, :] = gm_rows[video, i, f].astype(F32)
                gm_all[video * count : video * count + count, :] = wide[...].astype(BF)

        def after():
            pass

        blocks = video_size * count // BLOCK
        if blocks > 1:
            between()
            after()

        @pl.loop(0, blocks)
        def _(block):
            at = pl.ds(pl.multiple_of(block * BLOCK, BLOCK), BLOCK)
            msg_back_block(
                place, cls_ref[at, :], gm_all.at[at], msg_kept, msg_ref_out, in_ref_out, out_ref_out, msg_sums, cls_grads.at[at],
                msg_state, msg_gqkv, msg_mixed, *((between, after) if blocks == 1 else (lambda: None,) * 2),
            )

        for i in range(videos_here):
            for j in range(frames_here):
                row = (place.v * videos_here + i) * FRAMES + place.f * frames_here + j
                grad_cls[i * frames_here + j] = cls_grads[pl.ds(row, 1), :]
        for j in range(frames_here):
            put(videos_here - 1, j).wait()
        late.finish()
        each_attn(far.finish)
        each_last(lambda unit: lasts.drain(unit, last_source(unit)))
        pl.loop(0, 4)(lasts.drain_video)

        @each_attn
        def _(unit):
            for scatter, target in ((near, acc_near), (far, acc_far)):
                scatter.drain(unit, target.at[1, unit])
                scatter.drain_video(unit)


def msg_back_block(place, cls, gm_ref, kept, acc_msg, acc_in, acc_out, sums, cls_grad, scratch, gqkv, grad_mixed, between, after):
    bias, gain, shift, in_bias, out_bias, w_msg, w_in, w_out = kept
    qkv, probs, invs, mixed, normed, _ = scratch
    own_rows = D // place.F
    padded = acc_msg.shape[0]

    def own_columns(x):
        return pltpu.roll(x.astype(F32), lax.rem(D - place.f * own_rows, D), 1)[:, :padded].astype(BF)

    unit, inv_std = msg_forward(cls, (bias, gain, shift, in_bias, out_bias), w_msg, w_in, w_out, scratch, PAIRS)
    between()
    gm = gm_ref[...]
    acc_out[...] += dims(own_columns(mixed[...]), gm, 0, 0)
    sums[5:6, :] += column_sum(gm.astype(F32))
    grad_mixed[...] = dims(gm, w_out[...], 1, 1)

    @pl.loop(0, PAIRS, unroll=PAIRS)
    def _(pair):
        at = pair_lanes(pair)
        grads = pair_back(
            qkv[:, at], qkv[:, pair_lanes(pair, 1)], qkv[:, pair_lanes(pair, 2)], grad_mixed[:, at],
            mixed[:, at], invs[:, at], lambda head: probs[2 * pair + head],
        )
        for kind in range(3):
            gqkv[:, pair_lanes(pair, kind)] = grads[kind].astype(BF)

    after()
    own_normed = own_columns(normed[...])
    grad = None
    for kind in range(3):
        columns = slice(kind * D, kind * D + D)
        part = gqkv[:, columns]
        acc_in[:, columns] += dims(own_normed, part, 0, 0)
        if kind != 1:
            row = 3 + kind // 2
            sums[row : row + 1, :] += column_sum(part.astype(F32))
        term = dims(part, w_in[:, columns], 1, 1)
        grad = term if grad is None else grad + term
    sums[1:2, :] += column_sum(grad * unit)
    sums[2:3, :] += column_sum(grad)
    grad_message = norm_back(grad, unit, inv_std, vec(gain)) + gm.astype(F32)
    grad_message = grad_message.astype(BF)
    acc_msg[...] += dims(own_columns(cls), grad_message, 0, 0)
    sums[0:1, :] += column_sum(grad_message.astype(F32))
    cls_grad[...] = dims(grad_message, w_msg[...], 1, 1)


def collect_kernel(
    frame_size, video_size, videos_here, frames_here,
    done, reduced, near, far, totals, acc_msg, acc_in, acc_out, sums, grad_cls, tg_hbm, output_hbm,
    output, tokens_grad, msg_grad, in_grad, out_grad, *rest,
):
    (
        msg_bias_g, msg_gain_g, msg_shift_g, msg_in_bias_g, msg_out_bias_g, gain1_g, shift1_g,
        attn_in_g, attn_in_bias_g, attn_out_g, attn_out_bias_g, gain2_g, shift2_g, fc_g, fc_bias_g, proj_g, proj_bias_g,
        tg, out, sem,
    ) = rest
    f, v = lax.axis_index("frame"), lax.axis_index("video")
    own_rows = D // frame_size

    def load(i):
        return pltpu.make_async_copy(tg_hbm.at[i], tg.at[i], sem.at[0, i])

    def store(i):
        return pltpu.make_async_copy(tg.at[i], tokens_grad.at[i], sem.at[0, i])

    def load_out(i):
        return pltpu.make_async_copy(output_hbm.at[i], out.at[i], sem.at[1, i])

    def store_out(i):
        return pltpu.make_async_copy(out.at[i], output.at[i], sem.at[1, i])

    for i in range(videos_here):
        load(i).start()
        load_out(i).start()
    for i in range(videos_here):
        load(i).wait()
        added = [grad_cls[i * frames_here + j] for j in range(frames_here)]
        tg[i, 0] = tg[i, 0] + jnp.concatenate(added, axis=0)
        store(i).start()
        load_out(i).wait()
        store_out(i).start()

    def own_matrix(target, x):
        size = x.shape[1] // video_size
        target[...] = pltpu.roll(x[:own_rows], lax.rem(x.shape[1] - v * size, x.shape[1]), 1)[:, :size]

    own_matrix(msg_grad, acc_msg[...])
    own_matrix(in_grad, acc_in[...])
    own_matrix(out_grad, acc_out[...])

    def own_vector(target, ref, first, count):
        size = count * D // frame_size
        per_row = frame_size // count
        row = first + lax.div(f, per_row)
        x = ref[pl.ds(row, 1), :]
        x = pltpu.roll(jnp.broadcast_to(x, (8, D)), lax.rem(D - lax.rem(f, per_row) * size, D), 1)
        target[...] = x[0:1, :size].reshape(size)

    mlp_sums, attn_sums = totals.at[0], totals.at[1]
    for target, ref, first, count in (
        (msg_bias_g, sums, 0, 1), (msg_gain_g, sums, 1, 1), (msg_shift_g, sums, 2, 1), (msg_in_bias_g, sums, 3, 2),
        (msg_out_bias_g, sums, 5, 1), (gain1_g, attn_sums, 3, 1), (shift1_g, attn_sums, 4, 1),
        (attn_in_bias_g, attn_sums, 1, 2), (attn_out_bias_g, attn_sums, 0, 1), (gain2_g, mlp_sums, 0, 1),
        (shift2_g, mlp_sums, 1, 1), (fc_bias_g, mlp_sums, 2, 4), (proj_bias_g, mlp_sums, 6, 1),
    ):
        own_vector(target, ref, first, count)
    step = own_rows // UNITS
    columns = D // video_size
    wide_step = 4 * step
    part = FF // UNITS // video_size
    fc = [done[0], reduced[0], reduced[2]]
    for c in range(UNITS):
        for q in range(UNITS):
            for g in range(frame_size // video_size):
                from_at = q * part + g * wide_step
                to = (g * UNITS + c) * wide_step
                fc_g[q * step : q * step + step, to : to + wide_step] = fc[c][:, from_at : from_at + wide_step]
    for u in range(UNITS):
        rows = slice(u * step, u * step + step)
        attn_out_g[rows, :] = near[u][:, in_width(video_size) :]
        for w in range(video_size):

            @pl.when(v == w)
            def _(rows=rows, u=u, w=w):
                for group, parts in enumerate((near, far)):
                    at = 0
                    for _, count, to in in_pieces(group, w, video_size):
                        attn_in_g[rows, to : to + count] = parts[u][:, at : at + count]
                        at += count

    proj = [done[1], reduced[1], reduced[3]]
    proj = [x[:, q * columns : q * columns + columns] for x in proj for q in range(4)]
    proj_g[...] = jnp.concatenate(proj, axis=0).T
    for i in range(videos_here):
        store(i).wait()
        store_out(i).wait()


def shaped(shape, dtype):
    return jax.ShapeDtypeStruct(shape, dtype)


def whole(array):
    shape = array.shape
    return pl.BlockSpec(shape, lambda *_: (0,) * len(shape), pipeline_mode=pl.Buffered(1))


def wholes(*arrays):
    return [whole(array) for array in arrays]


def in_hbm():
    return pl.BlockSpec(memory_space=pl.ANY)


def in_vmem():
    return pl.BlockSpec(memory_space=pltpu.VMEM)


def per_step(count, shape):
    return pl.BlockSpec((count,) + shape, lambda b: (b,) + (0,) * len(shape))


def params(mib, **more):
    return pltpu.CompilerParams(vmem_limit_bytes=mib * MIB, **more)


def on_device(frame_size, video_size, *args):
    (
        tokens, cotangent, msg_weight, msg_bias, msg_norm_gain, msg_norm_shift, msg_in_weight,
        msg_in_bias, msg_out_weight, msg_out_bias, norm1_gain, norm1_shift, attn_in_weight,
        attn_in_bias, attn_out_weight, attn_out_bias, norm2_gain, norm2_shift, fc_weight, fc_bias,
        proj_weight, proj_bias,
    ) = args
    videos_here, frames_here = tokens.shape[:2]
    frames = videos_here * frames_here
    msgs = videos_here * video_size * FRAMES
    group = videos_here * FRAMES
    total = frames * ROWS
    F, V = frame_size, video_size
    step = D // F // UNITS
    n_bits = int(math.log2(F)) - 1
    x = tokens.transpose(0, 2, 1, 3)
    cot = cotangent.transpose(0, 2, 1, 3)
    msg_vectors = (msg_bias, msg_norm_gain, msg_norm_shift, msg_in_bias, msg_out_bias)
    DMA = pltpu.SemaphoreType.DMA

    msg_arrays = (*msg_vectors, msg_weight, msg_in_weight, msg_out_weight)
    kv_shape = (frames, PAIRS, KEYS, 128)

    def second(shape):
        zeros = (0,) * len(shape)
        return pl.BlockSpec((frames_here,) + shape, lambda t: (jnp.maximum(t - videos_here, 0),) + zeros)

    block_shapes = [(PAIRS, ROWS, 2 * KEYS), (PAIRS, ROWS, 128), (ROWS, D), (ROWS, D)]
    fwd_outs = [
        shaped((frames, PAIRS, ROWS, 128), BF), shaped(kv_shape, BF), shaped(kv_shape, BF), shaped((frames, ROWS, D), BF),
        shaped((frames,) + block_shapes[0], BF), shaped((frames,) + block_shapes[1], F32),
        shaped((frames,) + block_shapes[2], BF), shaped((frames,) + block_shapes[3], F32),
        shaped((frames, 1, D), F32), shaped((msgs, D), BF),
    ]
    q, k, v, normed, p, inv, mixed, kept, msg_out, cls = pl.pallas_call(
        functools.partial(attn_fwd_kernel, F, V, frames_here, videos_here),
        grid=(2 * videos_here,),
        in_specs=[
            pl.BlockSpec((1, PATCHES, frames_here, D), lambda t: (jnp.minimum(t, videos_here - 1), 0, 0, 0)), in_hbm(),
        ]
        + wholes(norm1_gain, norm1_shift, attn_in_bias, attn_out_bias, attn_in_weight) + [in_hbm()] * 9,
        out_specs=[in_hbm()] * 4 + [second(shape) for shape in block_shapes] + wholes(*fwd_outs[8:]),
        out_shape=fwd_outs,
        scratch_shapes=[pltpu.VMEM(out.shape, BF) for out in fwd_outs[:4]]
        + [
            pltpu.VMEM((frames, ROWS, D), F32), pltpu.VMEM((D, D), BF),
            pltpu.VMEM((16, D), F32), pltpu.VMEM((16, 3 * D), F32),
            pltpu.VMEM((videos_here, frames_here, D), BF),
            pltpu.VMEM((V, videos_here, F, frames_here, D), BF),
            pltpu.VMEM((group, D), F32), pltpu.VMEM((group, D), F32),
        ]
        + [pltpu.VMEM(a.shape, BF) for a in msg_arrays]
        + msg_scratch(group) + [DMA((V, F + V)), DMA((V, F + V)), DMA((11,)), DMA((4,))],
        compiler_params=params(63, collective_id=1, has_side_effects=True),
        name="attn_fwd",
    )(x, x, norm1_gain, norm1_shift, attn_in_bias, attn_out_bias, attn_in_weight, attn_out_weight, *msg_arrays)

    def bit_buffers(units, width=FF):
        return [
            pltpu.VMEM((units, max(1, F >> (2 + i)), step, width), BF) if i < n_bits else pltpu.VMEM((1, 1, 16, 128), BF)
            for i in range(3)
        ]

    def exchange_sems(units):
        return [DMA((units,)), DMA((units,)), DMA((units, n_bits, F // 4)), DMA((units, n_bits, F // 4)), DMA((units, V)), DMA((units, V))]

    def unit_buffers(count, units):
        return [pltpu.VMEM((count,) + shape, BF) for shape in units]

    block_shape = (F // 2, step, FF)
    part_shape = (V, step, FF // V)
    width = FF // UNITS
    mlp_outs = [
        shaped(x.shape, BF), shaped(kept.shape, F32), shaped((2, step, FF // V), F32), shaped((2, step, FF), BF),
        shaped((2, 2) + block_shape, BF), shaped((8, D), F32),
    ]
    output, grad_kept, done, mid, raw, mlp_sums = pl.pallas_call(
        functools.partial(mlp_kernel, F, V, videos_here, frames_here),
        grid=(UNITS,),
        in_specs=[in_hbm()] * 2 + wholes(norm2_gain, norm2_shift, fc_bias, proj_bias) + [in_hbm()] * 2,
        out_specs=[in_hbm()] * 2 + wholes(*mlp_outs[2:4]) + [in_hbm()] + wholes(mlp_outs[5]),
        out_shape=mlp_outs,
        scratch_shapes=[
            pltpu.VMEM(kept.shape, F32), pltpu.VMEM(x.shape, BF), pltpu.VMEM(kept.shape, F32),
            pltpu.VMEM((frames_here, ROWS, D), F32),
            pltpu.VMEM((total, D), BF), pltpu.VMEM((total, D), BF), pltpu.VMEM((total, width), BF), pltpu.VMEM((total, width), BF),
            pltpu.VMEM((total, D), F32), pltpu.VMEM((total, D), F32),
            pltpu.VMEM((UNITS, width), F32), pltpu.VMEM((UNITS, width), F32),
            pltpu.VMEM((2, D, width), BF), pltpu.VMEM((2, width, D), BF),
            pltpu.VMEM((D, FF) if 4 * step % 128 else (16, 128), BF),
            pltpu.VMEM((2 * UNITS, 2) + block_shape, BF), pltpu.VMEM((4,) + block_shape, BF),
        ]
        + bit_buffers(4) + unit_buffers(2, [part_shape] * 2)
        + [DMA((2, videos_here)), DMA((2, 2, F)), DMA((1,))] + exchange_sems(4),
        compiler_params=params(63, collective_id=2, has_side_effects=True),
        name="mlp",
    )(kept, cot, norm2_gain, norm2_shift, fc_bias, proj_bias, fc_weight, proj_weight)

    rows_own, columns = D // F, D // V
    padded = -(-rows_own // 128) * 128
    widths = (3 * HALF + D, 3 * HALF)
    part_widths = (in_width(V) + columns, in_width(V))
    back_outs = [
        shaped(x.shape, F32), shaped((4, step, FF // V), F32), shaped((UNITS, step, part_widths[0]), F32),
        shaped((UNITS, step, part_widths[1]), F32), shaped((2, 8, D), F32),
        shaped((padded, D), F32), shaped((padded, 3 * D), F32), shaped((padded, D), F32), shaped((8, D), F32),
        shaped((frames, 1, D), F32),
    ]
    def group_buffers(width, part_width):
        block = (F // 2, step, width)
        return [pltpu.VMEM((2, UNITS) + block, BF), pltpu.VMEM((UNITS,) + block, BF)] + bit_buffers(UNITS, width) + [
            pltpu.VMEM((UNITS, V, step, part_width), BF)
        ] * 2

    def by_pairs(shape):
        return pl.BlockSpec((1, PAIRS // 2) + shape, lambda t: (lax.rem(t, frames), lax.div(t, frames), 0, 0))

    tg, reduced, near, far, totals, acc_msg, acc_in, acc_out, msg_sums, grad_cls = pl.pallas_call(
        functools.partial(attn_back_kernel, F, V, videos_here, frames_here),
        grid=(2 * frames,),
        in_specs=[in_hbm()] * 5
        + wholes(msg_out, norm1_gain, norm1_shift, attn_out_weight, mlp_sums, mid)
        + [in_hbm()] + wholes(cls) + [in_hbm()] * 8
        + [by_pairs(shape) for shape in ((ROWS, 128), (KEYS, 128), (KEYS, 128), (ROWS, 2 * KEYS), (ROWS, 128))],
        out_specs=[in_hbm()] + wholes(*back_outs[1:]),
        out_shape=back_outs,
        scratch_shapes=[
            pltpu.VMEM(x.shape, BF), pltpu.VMEM(normed.shape, BF), pltpu.VMEM((D, 3 * D), BF),
            pltpu.VMEM(grad_kept.shape, F32), pltpu.VMEM(mixed.shape, BF),
            pltpu.VMEM((frames_here, ROWS, D), F32), pltpu.VMEM((frames_here, PATCHES, D), F32),
            pltpu.VMEM((max(total, D), 3 * D), BF), pltpu.VMEM((frames, ROWS, D), BF), pltpu.VMEM((8, D), F32), pltpu.VMEM((16, 3 * D), F32), pltpu.VMEM((8, D), F32),
            pltpu.VMEM((videos_here, frames_here, D), BF), pltpu.VMEM((V, videos_here, F, frames_here, D), BF),
            pltpu.VMEM((msgs, D), BF), pltpu.VMEM((group, D), F32), pltpu.VMEM((msgs, D), F32),
            pltpu.VMEM((2,) + block_shape, BF), pltpu.VMEM((2,) + block_shape, BF),
        ]
        + bit_buffers(2) + unit_buffers(4, [part_shape] * 2)
        + group_buffers(widths[0], part_widths[0]) + group_buffers(widths[1], part_widths[1])
        + [pltpu.VMEM((2, F, 8, D), F32), pltpu.VMEM((2, 8, D), F32), pltpu.VMEM((2, V, 8, D), F32)]
        + [pltpu.VMEM(a.shape, BF) for a in msg_arrays if a is not msg_in_weight]
        + [pltpu.VMEM((BLOCK, 3 * D), BF), pltpu.VMEM((BLOCK, D), F32)] + msg_scratch(BLOCK)
        + [DMA((2, frames)), DMA((8,)), DMA((8,)), DMA((2,)), DMA((frames_here,))]
        + [DMA((2, 2, max(F, V))), DMA((2, 2, max(F, V))), DMA((V, F + V)), DMA((V, F + V))]
        + exchange_sems(4) + exchange_sems(UNITS) + exchange_sems(UNITS),
        compiler_params=params(63, collective_id=3, has_side_effects=True),
        name="attn_back",
    )(
        x, normed, attn_in_weight, grad_kept, mixed, msg_out, norm1_gain, norm1_shift, attn_out_weight, mlp_sums, mid, raw, cls,
        *msg_arrays, q, k, v, p, inv,
    )

    out_shapes = [
        (rows_own, columns), (rows_own, 3 * columns), (rows_own, columns),
        (rows_own,), (rows_own,), (rows_own,), (2 * rows_own,), (rows_own,), (rows_own,), (rows_own,),
        (rows_own, 3 * columns), (2 * rows_own,), (rows_own, columns), (rows_own,), (rows_own,), (rows_own,),
        (rows_own, 4 * columns), (4 * rows_own,), (columns, 4 * rows_own), (rows_own,),
    ]
    out_shapes = [shaped(shape, F32) for shape in out_shapes]
    (
        output, tokens_grad, msg_grad, msg_in_grad, msg_out_grad,
        msg_bias_g, msg_gain_g, msg_shift_g, msg_in_bias_g, msg_out_bias_g, gain1_g, shift1_g,
        attn_in_g, attn_in_bias_g, attn_out_g, attn_out_bias_g, gain2_g, shift2_g, fc_g, fc_bias_g, proj_g, proj_bias_g,
    ) = pl.pallas_call(
        functools.partial(collect_kernel, F, V, videos_here, frames_here),
        grid=(1,),
        in_specs=wholes(done, reduced, near, far, totals, acc_msg, acc_in, acc_out, msg_sums, grad_cls) + [in_hbm()] * 2,
        out_specs=[in_hbm()] * 2 + wholes(*out_shapes),
        out_shape=[shaped(x.shape, BF), shaped(x.shape, F32)] + out_shapes,
        scratch_shapes=[pltpu.VMEM(x.shape, F32), pltpu.VMEM(x.shape, BF), DMA((2, videos_here))],
        compiler_params=params(63),
        name="collect",
    )(done, reduced, near, far, totals, acc_msg, acc_in, acc_out, msg_sums, grad_cls, tg, output)

    return (
        output.transpose(0, 2, 1, 3), tokens_grad.transpose(0, 2, 1, 3),
        msg_grad, msg_bias_g, msg_gain_g, msg_shift_g, msg_in_grad, msg_in_bias_g, msg_out_grad, msg_out_bias_g,
        gain1_g, shift1_g, attn_in_g, attn_in_bias_g, attn_out_g, attn_out_bias_g,
        gain2_g, shift2_g, fc_g, fc_bias_g, proj_g.T, proj_bias_g,
    )


def solution(mesh):
    rows = P("video", "frame", None, None)
    matrix, vector = P("frame", "video"), P("frame")
    out_specs = (
        rows, rows,
        matrix, vector, vector, vector, matrix, vector, matrix, vector,
        vector, vector, matrix, vector, matrix, vector,
        vector, vector, matrix, vector, matrix, vector,
    )
    return jax.shard_map(
        functools.partial(on_device, mesh.shape["frame"], mesh.shape["video"]),
        mesh=mesh, in_specs=(rows, rows) + (P(),) * 20, out_specs=out_specs, check_vma=False,
    )
```

```python
import functools
import math

import jax
import jax.numpy as jnp
from jax import lax
from jax.experimental import pallas as pl
from jax.experimental.pallas import tpu as pltpu
from jax.sharding import PartitionSpec as P

D = 768
HEADS = 12
PAIRS = 6
FF = 3072
PATCHES = 197
JOINED = 198
ROWS = 208
KEYS = 256
HALF = D // 2
FRAMES = 16
BLOCK = 192
UNITS = 3
BF = jnp.bfloat16
F32 = jnp.float32
MIB = 1 << 20
MESH = pl.DeviceIdType.MESH


def vec(ref, at=0):
    return ref[...].astype(F32).reshape(1, ref.shape[0])[:, at * D : at * D + D]


def dims(a, b, ca, cb):
    return lax.dot_general(a, b, (((ca,), (cb,)), ((), ())), preferred_element_type=F32)


def column_sum(x):
    return jnp.sum(x, axis=0, keepdims=True)


def norm_fwd(x, gain, shift):
    centre = x - jnp.mean(x, axis=-1, keepdims=True)
    inv = lax.rsqrt(jnp.mean(centre * centre, axis=-1, keepdims=True) + 1e-05)
    unit = centre * inv
    return unit * gain + shift, unit, inv


def norm_back(grad, unit, inv, gain):
    scaled = grad * gain
    return inv * (
        scaled
        - jnp.mean(scaled, axis=-1, keepdims=True)
        - unit * jnp.mean(scaled * unit, axis=-1, keepdims=True)
    )


def low_half():
    return lax.broadcasted_iota(jnp.int32, (1, 128), 1) < 64


def half(low, head, value, other):
    return jnp.where(low, value, other) if head == 0 else jnp.where(low, other, value)


def pair_fwd(q, k, v, mask_scores, keep):
    low = low_half()
    sums = []
    for head in range(2):
        scores = mask_scores(dims(q, half(low, head, k, jnp.zeros_like(k)), 1, 1))
        top = jnp.max(scores, axis=1, keepdims=True)
        probs = jnp.exp(scores - top).astype(BF)
        keep(head, probs)
        sums.append(dims(probs, half(low, head, v, jnp.ones_like(v)), 1, 0))
    inv = 1.0 / pltpu.roll(jnp.where(low, sums[1], sums[0]), 64, 1)
    return jnp.where(low, sums[0], sums[1]) * inv, inv


def pair_back(q, k, v, grad, mixed, inv, probs):
    low = low_half()
    scaled = grad * inv
    scaled_low = scaled.astype(BF)
    minus = -pltpu.roll(mixed.astype(F32) * scaled, 64, 1)
    totals = None
    for head in range(2):
        p = probs(head)
        centred = dims(half(low, head, scaled, minus).astype(BF), half(low, head, v, jnp.ones_like(v)), 1, 1)
        grad_s = (p.astype(F32) * centred).astype(BF)
        terms = (
            dims(grad_s, half(low, head, k, jnp.zeros_like(k)), 1, 0),
            dims(grad_s, half(low, head, q, jnp.zeros_like(q)), 0, 0),
            dims(p, half(low, head, scaled_low, jnp.zeros_like(scaled_low)), 0, 0),
        )
        totals = terms if totals is None else tuple(a + b for a, b in zip(totals, terms))
    return totals[0] * 0.125, totals[1], totals[2]


def lanes(pair):
    return slice(pair * 128, pair * 128 + 128)


def msg_mask(rows):
    row = lax.broadcasted_iota(jnp.int32, (rows, rows), 0) // FRAMES
    col = lax.broadcasted_iota(jnp.int32, (rows, rows), 1) // FRAMES
    same = row == col
    return lambda scores: jnp.where(same, scores, -1e30)


def msg_scratch(rows):
    return [
        pltpu.VMEM((rows, 3 * D), BF), pltpu.VMEM((HEADS, rows, rows), BF), pltpu.VMEM((rows, D), F32), pltpu.VMEM((rows, D), BF),
        pltpu.VMEM((rows, D), BF), pltpu.VMEM((rows, D), F32),
    ]


def pair_lanes(pair, kind=0):
    return pl.ds(pl.multiple_of(kind * D + pair * 128, 128), 128)


def msg_forward(cls, biases, w_msg, w_in, w_out, scratch, unroll):
    bias, gain, shift, in_bias, _ = biases
    qkv, probs, invs, mixed, normed_low, message = scratch
    message[...] = dims(cls, w_msg[...], 1, 0) + vec(bias)
    normed, unit, inv_std = norm_fwd(message[...], vec(gain), vec(shift))
    normed_low[...] = normed.astype(BF)

    def project(kind, bias, scale):
        columns = slice(kind * D, kind * D + D)
        qkv[:, columns] = ((dims(normed_low[...], w_in[:, columns], 1, 0) + bias) * scale).astype(BF)

    project(0, vec(in_bias), 0.125)
    project(1, 0.0, 1.0)
    project(2, vec(in_bias, 1), 1.0)
    mask = msg_mask(cls.shape[0])

    @pl.loop(0, PAIRS, unroll=unroll)
    def _(pair):
        def keep(head, p):
            probs[2 * pair + head] = p

        out, inv = pair_fwd(qkv[:, pair_lanes(pair)], qkv[:, pair_lanes(pair, 1)], qkv[:, pair_lanes(pair, 2)], mask, keep)
        mixed[:, pair_lanes(pair)] = out.astype(BF)
        invs[:, pair_lanes(pair)] = inv

    return unit, inv_std


class Place:
    def __init__(self, frame_size, video_size):
        self.F, self.V = frame_size, video_size
        self.f, self.v = lax.axis_index("frame"), lax.axis_index("video")
        self.core = lax.rem(self.f, 2)
        self.bits = [lax.rem(lax.div(self.f, 1 << i), 2) for i in range(int(math.log2(frame_size)))]

    def frame_peer(self, step):
        return {"frame": lax.rem(self.f + step, self.F)}

    def video_peer(self, step):
        return {"video": lax.rem(self.v + step, self.V)}

    def greet(self):
        self.announce()
        self.meet()

    def announce(self):
        barrier = pltpu.get_barrier_semaphore()

        @pl.loop(1, self.F)
        def _(step):
            pl.semaphore_signal(barrier, inc=1, device_id=self.frame_peer(step), device_id_type=MESH)

        @pl.loop(1, self.V)
        def _(step):
            pl.semaphore_signal(barrier, inc=1, device_id=self.video_peer(step), device_id_type=MESH)

    def meet(self):
        pl.semaphore_wait(pltpu.get_barrier_semaphore(), self.F + self.V - 2)


def remote(src, dst, send, recv, peer):
    return pltpu.make_async_remote_copy(
        src_ref=src, dst_ref=dst, send_sem=send, recv_sem=recv, device_id=peer, device_id_type=MESH
    )


class Gather:
    def __init__(self, place, own, rows, send, recv):
        self.place, self.own, self.rows, self.send, self.recv = place, own, rows, send, recv

    def near_copy(self, step, arriving):
        place = self.place
        frame = lax.rem(place.f + place.F - step, place.F) if arriving else place.f
        return remote(
            self.own, self.rows.at[place.v, :, frame], self.send.at[0, step], self.recv.at[0, step], place.frame_peer(step)
        )

    def far_copy(self, hop, arriving):
        place = self.place
        video = lax.rem(place.v + place.V - hop, place.V) if arriving else place.v
        slot = place.F - 1 + hop
        return remote(
            self.own, self.rows.at[video, :, place.f], self.send.at[0, slot], self.recv.at[0, slot], place.video_peer(hop)
        )

    def passed_copy(self, hop, step, arriving):
        place = self.place
        video = lax.rem(place.v + place.V - hop, place.V)
        frame = lax.rem(place.f + place.F - step, place.F) if arriving else place.f
        part = self.rows.at[video, :, frame]
        return remote(part, part, self.send.at[hop, step], self.recv.at[hop, step], place.frame_peer(step))

    def each_frame(self, call):
        pl.loop(1, self.place.F)(call)

    def each_video(self, call):
        pl.loop(1, self.place.V)(call)

    def start(self, far=True):
        self.each_frame(lambda step: self.near_copy(step, False).start())
        self.each_video(lambda hop: self.far_copy(hop, False).start())

    def near(self):
        self.each_frame(lambda step: self.near_copy(step, True).wait_recv())

    def forward(self):
        @pl.loop(1, self.place.V)
        def _(hop):
            self.far_copy(hop, True).wait_recv()
            self.each_frame(lambda step: self.passed_copy(hop, step, False).start())

    def finish(self):
        @pl.loop(1, self.place.V)
        def _(hop):
            def passed(step):
                self.passed_copy(hop, step, True).wait_recv()
                self.passed_copy(hop, step, False).wait_send()

            self.each_frame(passed)
            self.far_copy(hop, False).wait_send()

        self.each_frame(lambda step: self.near_copy(step, False).wait_send())


def attn_fwd_kernel(
    frame_size, video_size, frames_here, videos_here,
    x_ref, x_hbm, gain1, shift1, in_bias1, out_bias1, w_in1, w_out_hbm, *rest,
):
    operands, rest = rest[:8], rest[8:]
    (
        q_hbm, k_hbm, v_hbm, normed_hbm, p_ref, inv_ref, mixed_ref, kept_ref, out_ref, cls_ref,
        q_ref, k_ref, v_ref, normed_ref, joined, w_out1, msg_rows, msg_wide, own, rows, wide, mixed_out, *rest,
    ) = rest
    kept, scratch, (send, recv, local, s_out) = rest[:8], rest[8:14], rest[14:]
    bias, gain, shift, in_bias, out_bias, w_msg, w_in, w_out = kept
    place = Place(frame_size, video_size)
    t = pl.program_id(0)
    i = lax.rem(t, videos_here)
    frames = videos_here * frames_here
    every = frames_here * ROWS
    gather = Gather(place, own, rows, send, recv)

    def loads():
        pairs = [(x_hbm.at[:, 0], own), (x_hbm.at[:, 0], rows.at[place.v, :, place.f]), (w_out_hbm, w_out1)]
        pairs += list(zip(operands, kept))
        return [pltpu.make_async_copy(source, target, local.at[at]) for at, (source, target) in enumerate(pairs)]

    def stores():
        pairs = ((q_ref, q_hbm), (k_ref, k_hbm), (v_ref, v_hbm), (normed_ref, normed_hbm))
        return [pltpu.make_async_copy(source, target, s_out.at[at]) for at, (source, target) in enumerate(pairs)]

    @pl.when(t == 0)
    def _():
        place.announce()
        for load in loads():
            load.start()

    @pl.when(t == min(1, videos_here - 1))
    def _():
        for load in loads()[:2]:
            load.wait()
        place.meet()
        gather.start()

    @pl.when(t < videos_here)
    def _():
        x = x_ref[0].astype(F32)
        first = i * frames_here
        for j in range(frames_here):
            joined[first + j, 0:PATCHES, :] = x[:, j, :]
            joined[first + j, PATCHES:ROWS, :] = jnp.zeros((ROWS - PATCHES, D), F32)
        here = pl.ds(first, frames_here)
        normed, _, _ = norm_fwd(joined[here].reshape(every, D), vec(gain1), vec(shift1))
        normed_ref[here] = normed.astype(BF).reshape(frames_here, ROWS, D)
        normed = normed_ref[here].reshape(every, D)
        pad = jnp.zeros((KEYS - ROWS, 128), BF)
        q = ((dims(normed, w_in1[:, :D], 1, 0) + vec(in_bias1)) * 0.125).astype(BF)
        k = dims(normed, w_in1[:, D : 2 * D], 1, 0).astype(BF)
        v = (dims(normed, w_in1[:, 2 * D :], 1, 0) + vec(in_bias1, 1)).astype(BF)
        for j in range(frames_here):
            part = slice(j * ROWS, j * ROWS + ROWS)
            for pair in range(PAIRS):
                sl = lanes(pair)
                q_ref[first + j, pair] = q[part, sl]
                k_ref[first + j, pair, 0:ROWS] = k[part, sl]
                k_ref[first + j, pair, ROWS:KEYS] = pad
                v_ref[first + j, pair, 0:ROWS] = v[part, sl]
                v_ref[first + j, pair, ROWS:KEYS] = pad

    def unpack(video):
        for n in range(videos_here):
            for f in range(frame_size):
                at = (n * frame_size + f) * frames_here
                wide[at : at + frames_here, :] = rows[video, n, f].astype(F32)

    @pl.when(t == videos_here)
    def _():
        gather.near()
        gather.forward()
        unpack(place.v)
        for load in loads()[2:]:
            load.wait()
        biases = (bias, gain, shift, in_bias, out_bias)
        msg_forward(wide[...].astype(BF), biases, w_msg, w_in, w_out, scratch, PAIRS)
        mixed_out[...] = scratch[5][...] + dims(scratch[3][...], w_out[...], 1, 0) + vec(out_bias)
        msg_rows[...] = jnp.zeros_like(msg_rows)
        for n in range(videos_here):
            for j in range(frames_here):
                c = n * frames_here + j
                row = mixed_out[pl.ds(n * FRAMES + place.f * frames_here + j, 1), :]
                out_ref[c] = row
                msg_rows[c : c + 1, :] = row
                joined[c, PATCHES : PATCHES + 1, :] = row
        normed, _, _ = norm_fwd(msg_rows[...], vec(gain1), vec(shift1))
        low = normed.astype(BF)
        msg_wide[:, :D] = low.astype(F32)
        msg_wide[:, D : 2 * D] = dims(low, w_in1[:, D : 2 * D], 1, 0)
        msg_wide[:, 2 * D :] = dims(low, w_in1[:, 2 * D :], 1, 0) + vec(in_bias1, 1)
        at = PATCHES - PATCHES % 16
        mine = lax.broadcasted_iota(jnp.int32, (16, 1), 0) == PATCHES % 16
        block = slice(at, at + 16)

        @pl.loop(0, frames)
        def _(c):
            row = msg_wide[pl.ds(c, 1), :]
            normed_ref[c, block, :] = jnp.where(mine, row[:, :D], normed_ref[c, block, :].astype(F32)).astype(BF)
            for pair in range(PAIRS):
                for target, lo in ((k_ref, D), (v_ref, 2 * D)):
                    part = row[:, lo + pair * 128 : lo + pair * 128 + 128]
                    target[c, pair, block, :] = jnp.where(mine, part, target[c, pair, block, :].astype(F32)).astype(BF)

        for store in stores():
            store.start()

    valid = lax.broadcasted_iota(jnp.int32, (1, KEYS - 128), 1) < JOINED - 128

    def mask(scores):
        return jnp.concatenate([scores[:, :128], jnp.where(valid, scores[:, 128:], -1e30)], axis=1)

    @pl.when(t >= videos_here)
    def _():
        first = i * frames_here

        @pl.loop(0, frames_here)
        def _(j):
            c = first + j
            for pair in range(PAIRS):

                def keep(head, p, pair=pair):
                    p_ref[j, pair, :, head * KEYS : head * KEYS + KEYS] = p

                out, inv = pair_fwd(q_ref[c, pair], k_ref[c, pair], v_ref[c, pair], mask, keep)
                inv_ref[j, pair] = inv
                mixed_ref[j, :, lanes(pair)] = out.astype(BF)

        attended = dims(mixed_ref[...].reshape(every, D), w_out1[...], 1, 0) + vec(out_bias1)
        kept_ref[...] = joined[pl.ds(first, frames_here)] + attended.reshape(frames_here, ROWS, D)

    @pl.when(t == 2 * videos_here - 1)
    def _():
        gather.finish()
        count = videos_here * FRAMES
        for video in range(video_size):
            unpack(video)
            cls_ref[video * count : video * count + count, :] = wide[...].astype(BF)
        for store in stores():
            store.wait()


def fc_parts(x, w, V):
    size, width = FF // UNITS // V, FF // UNITS
    return jnp.concatenate([x[:, q * width + w * size : q * width + w * size + size] for q in range(UNITS)], axis=1)


def proj_parts(x, w, V):
    size = D // V
    return jnp.concatenate([x[:, q * D + w * size : q * D + w * size + size] for q in range(4)], axis=1)


MLP_PARTS = (fc_parts, proj_parts)


def in_pieces(group, w, V):
    size, out = 3 * D // V, []
    for kind in range(3):
        first = kind * D + group * HALF
        lo, hi = max(first, w * size), min(first + HALF, w * size + size)
        if hi > lo:
            out.append((kind * HALF + lo - first, hi - lo, lo - w * size))
    return out


def in_width(V):
    return max(sum(piece[1] for piece in in_pieces(g, w, V)) for g in range(2) for w in range(V))


def attn_parts(group):
    def parts(x, w, V):
        pieces = [x[:, at : at + count] for at, count, _ in in_pieces(group, w, V)]
        short = in_width(V) - sum(piece.shape[1] for piece in pieces)
        if short:
            pieces.append(jnp.zeros((x.shape[0], short), F32))
        if group == 0:
            size = D // V
            pieces.append(x[:, 3 * HALF + w * size : 3 * HALF + w * size + size])
        return jnp.concatenate(pieces, axis=1) if len(pieces) > 1 else pieces[0]

    return parts


class Scatter:
    def __init__(self, place, step, acc, recv0, recv_bits, send3, recv3, result, sems, first=0):
        self.place, self.step, self.acc, self.first = place, step, acc, first
        self.recv0, self.recv_bits, self.send3, self.recv3, self.result = recv0, recv_bits, send3, recv3, result
        self.sems = sems
        self.n_bits = len(place.bits) - 1

    def other_core(self):
        return {"frame": self.place.f + 1 - 2 * self.place.core}

    def exchange0(self, unit, source):
        return remote(source, self.recv0.at[unit - self.first], self.sems["send0"].at[unit], self.sems["recv0"].at[unit], self.other_core())

    def order(self, core, stage):
        return stage if core == 0 else self.n_bits - 1 - stage

    def blocks(self, stage, flip):
        place, n = self.place, self.n_bits
        free = n - 1 - stage
        out = []
        for i in range(1 << free):
            both = []
            for core in range(2):
                done = [self.order(core, s) for s in range(stage)]
                now = self.order(core, stage)
                rest = [bit for bit in range(n) if bit not in done and bit != now]
                at = 0
                for bit in done:
                    at = at + place.bits[bit + 1] * (1 << bit)
                own = place.bits[now + 1]
                at = at + ((1 - own) if flip else own) * (1 << now)
                for index, bit in enumerate(rest):
                    at = at + ((i >> index) & 1) * (1 << bit)
                both.append(at)
            out.append((1 - place.core) * both[0] + place.core * both[1])
        return out

    def partner(self, stage):
        place = self.place
        moves = []
        for core in range(2):
            bit = self.order(core, stage) + 1
            moves.append((1 - 2 * place.bits[bit]) * (1 << bit))
        return {"frame": place.f + (1 - place.core) * moves[0] + place.core * moves[1]}

    def exchange(self, unit, stage, i, block):
        sems = self.sems
        return remote(
            self.acc(unit, block), self.recv_bits[stage].at[unit - self.first, i],
            sems["send_bits"].at[unit, stage, i], sems["recv_bits"].at[unit, stage, i], self.partner(stage),
        )

    def add(self, unit, block, came):
        target = self.acc(unit, block)
        target[...] = target[...] + came

    def stage(self, unit, stage):
        if stage == 0:
            self.exchange0(unit, self.recv0.at[unit - self.first]).wait_recv()
            came = lambda position, block: self.recv0[unit - self.first, block]
        else:
            for i in range(1 << (self.n_bits - stage)):
                self.exchange(unit, stage - 1, i, 0).wait_recv()
            came = lambda position, block: self.recv_bits[stage - 1][unit - self.first, position]
        if stage == self.n_bits:
            block = self.own_block()
            self.add(unit, block, came(0, block))
            return
        sending, staying = self.blocks(stage, True), self.blocks(stage, False)
        where = self.positions(stage)
        for i, block in enumerate(sending):
            self.add(unit, block, came(where[1][i], block))
            self.exchange(unit, stage, i, block).start()
        for i, block in enumerate(staying):
            self.add(unit, block, came(where[0][i], block))

    def positions(self, stage):
        place, n = self.place, self.n_bits
        if stage == 0:
            return [[None] * (1 << (n - 1))] * 2
        out = [[], []]
        for flip in range(2):
            for i in range(1 << (n - 1 - stage)):
                both = []
                for core in range(2):
                    done = [self.order(core, s) for s in range(stage)]
                    now = self.order(core, stage)
                    rest_before = [bit for bit in range(n) if bit not in done]
                    rest = [bit for bit in rest_before if bit != now]
                    own = place.bits[now + 1]
                    at = 0
                    for index, bit in enumerate(rest_before):
                        if bit == now:
                            at = at + ((1 - own) if flip else own) * (1 << index)
                        else:
                            at = at + ((i >> rest.index(bit)) & 1) * (1 << index)
                    both.append(at)
                out[flip].append((1 - place.core) * both[0] + place.core * both[1])
        return out

    def own_block(self):
        return lax.div(self.place.f, 2)

    def across(self, unit, hop):
        place, sems = self.place, self.sems
        to = lax.rem(place.v + hop, place.V)
        return remote(
            self.send3.at[unit, to], self.recv3.at[unit, hop],
            sems["send3"].at[unit, hop], sems["recv3"].at[unit, hop], place.video_peer(hop),
        )

    def middle(self, unit):
        for stage in range(1, self.n_bits):
            self.stage(unit, stage)

    def land(self, unit):
        self.stage(unit, self.n_bits)
        return self.acc(unit, self.own_block())

    def send_video(self, unit, parts, value):
        value = value.astype(F32)
        for w in range(self.place.V):
            self.send3[unit, w] = parts(value, w, self.place.V).astype(BF)
        pl.loop(1, self.place.V)(lambda hop: self.across(unit, hop).start())

    def finish(self, unit):
        self.result[unit] = self.send3[unit, self.place.v].astype(F32)

        @pl.loop(1, self.place.V)
        def _(hop):
            self.across(unit, hop).wait_recv()
            self.result[unit] += self.recv3[unit, hop].astype(F32)

    def drain(self, unit, source):
        self.exchange0(unit, source).wait_send()
        for stage in range(self.n_bits):
            for i in range(1 << (self.n_bits - 1 - stage)):
                self.exchange(unit, stage, i, 0).wait_send()

    def drain_video(self, unit):
        pl.loop(1, self.place.V)(lambda hop: self.across(unit, hop).wait_send())


class Totals:
    def __init__(self, place, which, own, near, middle, far, result, sems):
        self.place, self.which, self.own, self.near_buf, self.middle = place, which, own, near, middle
        self.far_buf, self.result, self.sems = far, result, sems

    def near(self, step):
        sems = self.sems
        return remote(
            self.own, self.near_buf.at[self.which, step], sems["vec_send"].at[self.which, 0, step],
            sems["vec_recv"].at[self.which, 0, step], self.place.frame_peer(step),
        )

    def far(self, hop):
        sems = self.sems
        return remote(
            self.middle.at[self.which], self.far_buf.at[self.which, hop], sems["vec_send"].at[self.which, 1, hop],
            sems["vec_recv"].at[self.which, 1, hop], self.place.video_peer(hop),
        )

    def start(self):
        pl.loop(1, self.place.F)(lambda step: self.near(step).start())

    def forward(self):
        self.middle[self.which] = self.own[...]

        @pl.loop(1, self.place.F)
        def _(step):
            self.near(step).wait_recv()
            self.middle[self.which] += self.near_buf[self.which, step]

        pl.loop(1, self.place.V)(lambda hop: self.far(hop).start())

    def finish(self):
        self.result[self.which] = self.middle[self.which]

        @pl.loop(1, self.place.V)
        def _(hop):
            self.far(hop).wait_recv()
            self.result[self.which] += self.far_buf[self.which, hop]
            self.far(hop).wait_send()

        pl.loop(1, self.place.F)(lambda step: self.near(step).wait_send())


def mlp_kernel(
    frame_size, video_size, videos_here, frames_here,
    kept_hbm, cot_hbm, gain, shift, fc_bias, proj_bias, fc_hbm, proj_hbm,
    out_hbm, grad_hbm, done_ref, mid_ref, raw_hbm, sums,
    kept_ref, cot_ref, grad_ref, wide, normed2, cot2, act, grad_h, out_acc, grad_acc, bias_rows, bias_sums, fc_buf, proj_buf, fc_all,
    grads, recv0, recv_a, recv_b, recv_c, send3, recv3,
    s_rows, s_load, s_raw, s_send0, s_recv0, s_sendb, s_recvb, s_send3, s_recv3,
):
    chunk = pl.program_id(0)
    frames = videos_here * frames_here
    place = Place(frame_size, video_size)
    step = D // frame_size // UNITS
    wide_step = 4 * step
    width = FF // UNITS
    sems = dict(send0=s_send0, recv0=s_recv0, send_bits=s_sendb, recv_bits=s_recvb, send3=s_send3, recv3=s_recv3)
    scatter = Scatter(
        place, step, lambda unit, block: grads.at[unit, 0, block], recv0, [recv_a, recv_b, recv_c], send3, recv3, done_ref, sems
    )
    sliced = wide_step % 128 == 0

    def rows_of(b, count=1):
        return pl.ds(pl.multiple_of(b * count * ROWS, ROWS), count * ROWS)

    def loads(c):
        slot = lax.rem(c, 2)
        out = []
        for f in range(frame_size):
            at = pl.multiple_of((f * UNITS + c) * wide_step, wide_step)
            to = slice(f * wide_step, f * wide_step + wide_step)
            out.append(pltpu.make_async_copy(proj_hbm.at[pl.ds(at, wide_step)], proj_buf.at[slot, to], s_load.at[slot, 0, f]))
            if sliced:
                out.append(pltpu.make_async_copy(fc_hbm.at[:, pl.ds(at, wide_step)], fc_buf.at[slot, :, to], s_load.at[slot, 1, f]))
        return out

    def row_loads(i):
        part = pl.ds(i * frames_here, frames_here)
        return [
            pltpu.make_async_copy(kept_hbm.at[part], kept_ref.at[part], s_rows.at[0, i]),
            pltpu.make_async_copy(cot_hbm.at[i], cot_ref.at[i], s_rows.at[1, i]),
        ]

    def row_stores(i):
        part = pl.ds(i * frames_here, frames_here)
        return [
            pltpu.make_async_copy(grad_ref.at[part], grad_hbm.at[part], s_rows.at[0, i]),
            pltpu.make_async_copy(cot_ref.at[i], out_hbm.at[i], s_rows.at[1, i]),
        ]

    def load_all():
        return pltpu.make_async_copy(fc_hbm, fc_all, s_load.at[0, 1, 0])

    @pl.when(chunk == 0)
    def _():
        place.announce()
        for n in range(videos_here):
            for load in row_loads(n):
                load.start()
        for load in loads(chunk):
            load.start()
        if not sliced:
            load_all().start()
        sums[...] = jnp.zeros_like(sums)
        bias_sums[...] = jnp.zeros_like(bias_sums)
        wide[:, PATCHES:ROWS, :] = jnp.zeros((frames_here, ROWS - PATCHES, D), F32)
        bias = fc_bias[...].astype(F32).reshape(1, FF)
        for c in range(UNITS):
            for f in range(frame_size):
                at = (f * UNITS + c) * wide_step
                bias_rows[c : c + 1, f * wide_step : f * wide_step + wide_step] = bias[:, at : at + wide_step]

        @pl.loop(0, videos_here)
        def _(i):
            for load in row_loads(i):
                load.wait()
            cot = cot_ref[i].astype(F32)
            for j in range(frames_here):
                wide[j, 0:PATCHES, :] = cot[:, j, :]
            for j in range(frames_here):
                b = i * frames_here + j
                cot_j = wide[j]
                cot2[rows_of(b), :] = cot_j.astype(BF)
                sums[6:7, :] += column_sum(cot_j)
                normed, _, _ = norm_fwd(kept_ref[b], vec(gain), vec(shift))
                normed2[rows_of(b), :] = normed.astype(BF)
                out_acc[rows_of(b), :] = kept_ref[b] + vec(proj_bias)
                grad_acc[rows_of(b), :] = jnp.zeros((ROWS, D), F32)

        if not sliced:
            load_all().wait()

    for load in loads(chunk):
        load.wait()

    @pl.when(chunk < UNITS - 1)
    def _():
        for load in loads(chunk + 1):
            load.start()

    slot = lax.rem(chunk, 2)
    if not sliced:
        for c in range(UNITS):

            @pl.when(chunk == c)
            def _(c=c):
                for f in range(frame_size):
                    at = (f * UNITS + c) * wide_step
                    fc_buf[slot, :, f * wide_step : f * wide_step + wide_step] = fc_all[:, at : at + wide_step]

    fc, proj = fc_buf.at[slot], proj_buf.at[slot]
    bias = bias_rows[pl.ds(chunk, 1), :]
    per_tile = 2 if frames % 2 == 0 else 1
    tiles = frames // per_tile

    def due(c, t, now, call):
        pl.when(jnp.logical_and(chunk == c, now == min(t, tiles - 1)))(call)

    def both(call, first):
        return lambda: pl.loop(first, first + 2)(call)

    def video():
        for unit in range(2):
            scatter.send_video(unit, MLP_PARTS[unit % 2], scatter.land(unit)[...])

    @pl.loop(0, tiles)
    def _(t):
        due(0, 2, t, place.meet)
        due(1, 1, t, both(lambda unit: scatter.stage(unit, 0), 0))
        due(2, 0, t, both(scatter.middle, 0))
        due(2, 1, t, both(lambda unit: scatter.stage(unit, 0), 2))
        due(2, 2, t, video)
        rows = rows_of(t, per_tile)
        hidden = dims(normed2[rows, :], fc[...], 1, 0) + bias
        grad_a = dims(cot2[rows, :], proj[...], 1, 1)
        gate = 0.5 * jnp.tanh(0.851 * hidden) + 0.5
        active = hidden * gate
        grad = (grad_a * (gate + 1.702 * active * (1.0 - gate))).astype(BF)
        active = active.astype(BF)
        act[rows, :] = active
        grad_h[rows, :] = grad
        bias_sums[pl.ds(chunk, 1), :] += column_sum(grad.astype(F32))
        out_acc[rows, :] += dims(active, proj[...], 1, 0)
        grad_acc[rows, :] += dims(grad, fc[...], 1, 1)

    unit = 2 * chunk

    def weight_grads(m):
        size = width // 2
        count = frame_size // 4
        value = dims(act[:, pl.ds(pl.multiple_of(m * size, size), size)], cot2[...], 0, 0).astype(BF)
        value = value.reshape(count, 2, 4, step, D)
        for core in range(2):
            for q in range(4):
                grads[
                    unit + 1, lax.rem(core + place.core, 2), pl.ds(m * count, count), :, q * D : q * D + D
                ] = value[:, core, q]
        size = D // 2
        value = dims(normed2[:, pl.ds(pl.multiple_of(m * size, size), size)], grad_h[...], 0, 0).astype(BF)
        value = value.reshape(count, 2, UNITS, step, width)
        for core in range(2):
            for q in range(UNITS):
                grads[
                    unit, lax.rem(core + place.core, 2), pl.ds(m * count, count), :, q * width : q * width + width
                ] = value[:, core, q]

    pl.loop(0, 2)(weight_grads)

    def raw():
        return pltpu.make_async_copy(grads.at[pl.ds(4, 2)], raw_hbm, s_raw.at[0])

    def source(unit):
        return grads.at[unit, 1]

    @pl.when(chunk == 0)
    def _():
        pl.loop(0, 2)(lambda unit: scatter.exchange0(unit, source(unit)).start())

    @pl.when(chunk == 1)
    def _():
        pl.loop(2, 4)(lambda unit: scatter.exchange0(unit, source(unit)).start())

    @pl.when(chunk == 2)
    def _():
        raw().start()
        both(scatter.middle, 2)()
        both(scatter.finish, 0)()
        for c in range(UNITS):
            for f in range(frame_size):
                at = (f * UNITS + c) * wide_step
                row, column = 2 + at // D, at % D
                sums[row : row + 1, column : column + wide_step] = bias_sums[
                    c : c + 1, f * wide_step : f * wide_step + wide_step
                ]

        @pl.loop(0, videos_here)
        def _(i):
            outs = [out_acc[rows_of(i * frames_here + j), :][:PATCHES] for j in range(frames_here)]
            cot_ref[i] = jnp.stack(outs, axis=1).astype(BF)
            every = frames_here * ROWS
            here = pl.ds(i * frames_here, frames_here)
            rows = rows_of(i, frames_here)
            _, unit, inv = norm_fwd(kept_ref[here].reshape(every, D), vec(gain), vec(shift))
            grad = grad_acc[rows, :]
            sums[0:1, :] += column_sum(grad * unit)
            sums[1:2, :] += column_sum(grad)
            grad = norm_back(grad, unit, inv, vec(gain)) + cot2[rows, :].astype(F32)
            grad_ref[here] = grad.reshape(frames_here, ROWS, D)
            for store in row_stores(i):
                store.start()

        @pl.loop(0, 2)
        def _(unit):
            mid_ref[unit] = scatter.land(2 + unit)[...]
            scatter.drain_video(unit)

        pl.loop(0, 4)(lambda unit: scatter.drain(unit, source(unit)))
        raw().wait()
        for n in range(videos_here):
            for store in row_stores(n):
                store.wait()


def attn_back_kernel(
    frame_size, video_size, videos_here, frames_here,
    x_hbm, normed_hbm, w_in_hbm, gk_hbm, mixed_hbm, msg_ref, gain, shift, w_out, mlp_sums, mid_ref, raw_hbm, cls_ref, *rest,
):
    msg_operands, rest = rest[:8], rest[8:]
    (
        q_ref, k_ref, v_ref, p_ref, inv_ref,
        tg_ref, reduced_ref, near_ref, far_ref, totals_ref, msg_ref_out, in_ref_out, out_ref_out, msg_sums, grad_cls,
        x_ref, normed_ref, w_in, gk_ref, mixed_ref, joined, staged, gqkv_all, gk_all, sums, gm_grads, gm_wide, gm_own, gm_rows, gm_all, wide, cls_grads,
        acc_mlp, *rest,
    ) = rest
    last_buffers, rest = rest[:6], rest[6:]
    (acc_near, *near_buffers), rest = rest[:7], rest[7:]
    (acc_far, *far_buffers), rest = rest[:7], rest[7:]
    (vec_near, vec_mid, vec_far), rest = rest[:3], rest[3:]
    msg_kept, (msg_gqkv, msg_mixed), msg_state, rest = list(rest[:7]), rest[7:9], rest[9:15], rest[15:]
    msg_kept.insert(6, gqkv_all.at[0:D])
    (s_rows, s_late, s_msg, s_local, s_staged, s_vsend, s_vrecv, s_gsend, s_grecv), rest = rest[:9], rest[9:]
    names = ("send0", "recv0", "send_bits", "recv_bits", "send3", "recv3")
    last_sems, near_sems, far_sems = (dict(zip(names, rest[6 * i : 6 * i + 6])) for i in range(3))
    frames = videos_here * frames_here
    steps = 2 * frames
    t = pl.program_id(0)
    side, b = lax.div(t, frames), lax.rem(t, frames)
    place = Place(frame_size, video_size)
    step = D // frame_size // UNITS
    total = frames * ROWS
    each_mid, each_last, each_attn = pl.loop(0, 2), pl.loop(2, 4), pl.loop(0, UNITS)

    def scatter(acc, buffers, result, sems, first=0):
        recv0, recv_a, recv_b, recv_c, send3, recv3 = buffers
        return Scatter(place, step, acc, recv0, [recv_a, recv_b, recv_c], send3, recv3, result, sems, first)

    lasts = scatter(lambda unit, block: acc_mlp.at[unit - 2, block], last_buffers, reduced_ref, last_sems, first=2)
    near = scatter(lambda unit, block: acc_near.at[0, unit, block], near_buffers, near_ref, near_sems)
    far = scatter(lambda unit, block: acc_far.at[0, unit, block], far_buffers, far_ref, far_sems)
    vec_sems = dict(vec_send=s_vsend, vec_recv=s_vrecv)
    early = Totals(place, 0, mlp_sums, vec_near, vec_mid, vec_far, totals_ref, vec_sems)
    late = Totals(place, 1, sums, vec_near, vec_mid, vec_far, totals_ref, vec_sems)
    gather = Gather(place, gm_own, gm_rows, s_gsend, s_grecv)

    def last_source(unit):
        return raw_hbm.at[unit - 2, 1]

    def local(unit):
        return pltpu.make_async_copy(raw_hbm.at[unit - 2, 0], acc_mlp.at[unit - 2], s_local.at[unit - 2])

    def msg_loads():
        return [pltpu.make_async_copy(a, b, s_msg.at[i]) for i, (a, b) in enumerate(zip(msg_operands, msg_kept))]

    def row_loads(c):
        return [
            pltpu.make_async_copy(gk_hbm.at[c], gk_ref.at[c], s_rows.at[0, c]),
            pltpu.make_async_copy(mixed_hbm.at[c], mixed_ref.at[c], s_rows.at[1, c]),
        ]

    def late_loads():
        out = [
            pltpu.make_async_copy(x_hbm, x_ref, s_late.at[0]), pltpu.make_async_copy(normed_hbm, normed_ref, s_late.at[1]),
        ]
        for half_at in range(2):
            for kind in range(3):
                source = w_in_hbm.at[:, kind * D + half_at * HALF : kind * D + half_at * HALF + HALF]
                at = (half_at * 3 + kind) * HALF
                out.append(pltpu.make_async_copy(source, w_in.at[:, at : at + HALF], s_late.at[2 + half_at * 3 + kind]))
        return out

    def due(at, call):
        pl.when(t == min(at, steps - 1))(call)

    def begin():
        place.announce()

        @pl.loop(0, frames)
        def _(c):
            for load in row_loads(c):
                load.start()

        sums[...] = jnp.zeros_like(sums)
        each_last(lambda unit: local(unit).start())
        for load in late_loads():
            load.start()
        for at, load in enumerate(msg_loads()):
            if at != 6:
                load.start()

    def begin_far():
        place.meet()
        each_last(lambda unit: lasts.exchange0(unit, last_source(unit)).start())
        early.start()
        for unit in range(2):
            lasts.send_video(unit, MLP_PARTS[unit], mid_ref[unit])

    def open_lasts():
        @each_last
        def _(unit):
            local(unit).wait()
            lasts.stage(unit, 0)

    def land_lasts():
        for unit in (2, 3):
            lasts.send_video(unit, MLP_PARTS[unit % 2], lasts.land(unit)[...])

    def land(scatter, group):
        @each_attn
        def _(unit):
            scatter.send_video(unit, attn_parts(group), scatter.land(unit)[...])

    due(0, begin)
    rows = pl.ds(pl.multiple_of(b * ROWS, ROWS), ROWS)
    side_lanes = pl.ds(pl.multiple_of(side * HALF, HALF), HALF)

    @pl.when(side == 0)
    def _():
        for load in row_loads(b):
            load.wait()
        gk_low = gk_ref[b].astype(BF)
        gk_all[b] = gk_low
        sums[0:1, :] += column_sum(gk_low.astype(F32))

    grad_mixed = dims(gk_all[b], w_out[side_lanes, :], 1, 1)
    for pair in range(PAIRS // 2):
        grads = pair_back(
            q_ref[0, pair], k_ref[0, pair], v_ref[0, pair], grad_mixed[:, lanes(pair)],
            mixed_ref[b, :, pl.ds(pl.multiple_of(side * HALF + pair * 128, 128), 128)], inv_ref[0, pair],
            lambda head, pair=pair: p_ref[0, pair, :, head * KEYS : head * KEYS + KEYS],
        )
        for kind in range(3):
            at = pl.ds(pl.multiple_of((side * 3 + kind) * HALF + pair * 128, 128), 128)
            gqkv_all[rows, at] = grads[kind][:ROWS].astype(BF)
    due(0, begin_far)
    due(1, open_lasts)
    due(3, lambda: each_mid(lasts.finish))
    due(4, early.forward)
    due(5, lambda: each_last(lasts.middle))
    due(7, land_lasts)
    due(frames + 1, lambda: each_attn(lambda unit: near.stage(unit, 0)))
    for row, kind in ((1, 0), (2, 2)):
        part = gqkv_all[rows, pl.ds(pl.multiple_of((side * 3 + kind) * HALF, HALF), HALF)]
        sums[row : row + 1, side_lanes] += column_sum(part.astype(F32))

    def attn_unit(m, target, left, right, lo):
        size, width = D // 2, right.shape[1]
        value = dims(left[:, :, pl.ds(pl.multiple_of(m * size, size), size)].reshape(total, size), right, 0, 0).astype(BF)
        count = frame_size // 4
        value = value.reshape(count, 2, UNITS, step, width)
        for u in range(UNITS):
            for core in range(2):
                target[lax.rem(core + place.core, 2), u, pl.ds(m * count, count), :, lo : lo + width] = value[:, core, u]

    def attn_units(group, target, scatter):
        @pl.loop(0, 2)
        def _(m):
            attn_unit(m, target, normed_ref, gqkv_all[0:total, group * 3 * HALF : (group + 1) * 3 * HALF], 0)
            if group == 0:
                attn_unit(m, target, mixed_ref, gk_all[...].reshape(total, D), 3 * HALF)

        each_attn(lambda unit: scatter.exchange0(unit, target.at[1, unit]).start())

    @pl.when(t == frames - 1)
    def _():
        for load in late_loads():
            load.wait()
        attn_units(0, acc_near, near)

    @pl.when(t == steps - 1)
    def _():
        at = JOINED - 1 - (JOINED - 1) % 16
        gm_grads[...] = jnp.zeros_like(gm_grads)
        for c in range(frames):
            piece = gqkv_all[c * ROWS + at : c * ROWS + at + 16, :].astype(F32)
            gm_grads[c : c + 1, :] = piece[PATCHES - at : PATCHES - at + 1]
            joined[0, c : c + 1, :] = msg_ref[c]
        _, unit, inv = norm_fwd(joined[0, 0:frames, :], vec(gain), vec(shift))
        grad = dims(gm_grads[...].astype(BF), w_in[...], 1, 1)[0:frames]
        gm_wide[0:frames, :] = norm_back(grad, unit, inv, vec(gain))
        for i in range(videos_here):
            gm_own[i] = gm_wide[i * frames_here : i * frames_here + frames_here, :].astype(BF)
            gm_rows[place.v, i, place.f] = gm_own[i]
        gather.start()
        each_attn(near.middle)
        attn_units(1, acc_far, far)
        each_last(lasts.finish)
        early.finish()
        gather.near()
        gather.forward()

        def put(i, j):
            return pltpu.make_async_copy(staged.at[j], tg_ref.at[i, :, j], s_staged.at[j])

        def norm_frames(lo, hi):
            @pl.loop(lo, hi)
            def _(i):
                @pl.when(i > 0)
                def _():
                    for j in range(frames_here):
                        put(i - 1, j).wait()

                x = x_ref[i].astype(F32)
                first = i * frames_here
                for j in range(frames_here):
                    joined[j, 0:PATCHES, :] = x[:, j, :]
                    joined[j, PATCHES:ROWS, :] = jnp.zeros((ROWS - PATCHES, D), F32)
                    joined[j, PATCHES : PATCHES + 1, :] = msg_ref[first + j]
                every = frames_here * ROWS
                rows = pl.ds(pl.multiple_of(first * ROWS, ROWS), every)
                grad = dims(gqkv_all[rows, :], w_in[...], 1, 1)
                _, unit, inv = norm_fwd(joined[...].reshape(every, D), vec(gain), vec(shift))
                sums[3:4, :] += column_sum(grad * unit)
                sums[4:5, :] += column_sum(grad)
                back = gk_ref[pl.ds(first, frames_here)].reshape(every, D) + norm_back(grad, unit, inv, vec(gain))
                for j in range(frames_here):
                    staged[j] = back[j * ROWS : j * ROWS + PATCHES]
                    put(i, j).start()

        norm_frames(0, 1)
        each_attn(lambda unit: far.stage(unit, 0))
        land(near, 0)
        norm_frames(1, videos_here)
        msg_loads()[6].start()
        late.start()
        each_attn(far.middle)
        each_attn(near.finish)
        for load in msg_loads():
            load.wait()
        for ref in (msg_sums, msg_ref_out, in_ref_out, out_ref_out):
            ref[...] = jnp.zeros_like(ref)
        count = videos_here * FRAMES

        def between():
            land(far, 1)
            late.forward()
            gather.finish()
            for video in range(video_size):
                for i in range(videos_here):
                    for f in range(frame_size):
                        at_row = (i * frame_size + f) * frames_here
                        wide[at_row : at_row + frames_here, :] = gm_rows[video, i, f].astype(F32)
                gm_all[video * count : video * count + count, :] = wide[...].astype(BF)

        def after():
            pass

        blocks = video_size * count // BLOCK
        if blocks > 1:
            between()
            after()

        @pl.loop(0, blocks)
        def _(block):
            at = pl.ds(pl.multiple_of(block * BLOCK, BLOCK), BLOCK)
            msg_back_block(
                place, cls_ref[at, :], gm_all.at[at], msg_kept, msg_ref_out, in_ref_out, out_ref_out, msg_sums, cls_grads.at[at],
                msg_state, msg_gqkv, msg_mixed, *((between, after) if blocks == 1 else (lambda: None,) * 2),
            )

        for i in range(videos_here):
            for j in range(frames_here):
                row = (place.v * videos_here + i) * FRAMES + place.f * frames_here + j
                grad_cls[i * frames_here + j] = cls_grads[pl.ds(row, 1), :]
        for j in range(frames_here):
            put(videos_here - 1, j).wait()
        late.finish()
        each_attn(far.finish)
        each_last(lambda unit: lasts.drain(unit, last_source(unit)))
        pl.loop(0, 4)(lasts.drain_video)

        @each_attn
        def _(unit):
            for scatter, target in ((near, acc_near), (far, acc_far)):
                scatter.drain(unit, target.at[1, unit])
                scatter.drain_video(unit)


def msg_back_block(place, cls, gm_ref, kept, acc_msg, acc_in, acc_out, sums, cls_grad, scratch, gqkv, grad_mixed, between, after):
    bias, gain, shift, in_bias, out_bias, w_msg, w_in, w_out = kept
    qkv, probs, invs, mixed, normed, _ = scratch
    own_rows = D // place.F
    padded = acc_msg.shape[0]

    def own_columns(x):
        return pltpu.roll(x.astype(F32), lax.rem(D - place.f * own_rows, D), 1)[:, :padded].astype(BF)

    unit, inv_std = msg_forward(cls, (bias, gain, shift, in_bias, out_bias), w_msg, w_in, w_out, scratch, PAIRS)
    between()
    gm = gm_ref[...]
    acc_out[...] += dims(own_columns(mixed[...]), gm, 0, 0)
    sums[5:6, :] += column_sum(gm.astype(F32))
    grad_mixed[...] = dims(gm, w_out[...], 1, 1)

    @pl.loop(0, PAIRS, unroll=PAIRS)
    def _(pair):
        at = pair_lanes(pair)
        grads = pair_back(
            qkv[:, at], qkv[:, pair_lanes(pair, 1)], qkv[:, pair_lanes(pair, 2)], grad_mixed[:, at],
            mixed[:, at], invs[:, at], lambda head: probs[2 * pair + head],
        )
        for kind in range(3):
            gqkv[:, pair_lanes(pair, kind)] = grads[kind].astype(BF)

    after()
    own_normed = own_columns(normed[...])
    grad = None
    for kind in range(3):
        columns = slice(kind * D, kind * D + D)
        part = gqkv[:, columns]
        acc_in[:, columns] += dims(own_normed, part, 0, 0)
        if kind != 1:
            row = 3 + kind // 2
            sums[row : row + 1, :] += column_sum(part.astype(F32))
        term = dims(part, w_in[:, columns], 1, 1)
        grad = term if grad is None else grad + term
    sums[1:2, :] += column_sum(grad * unit)
    sums[2:3, :] += column_sum(grad)
    grad_message = norm_back(grad, unit, inv_std, vec(gain)) + gm.astype(F32)
    grad_message = grad_message.astype(BF)
    acc_msg[...] += dims(own_columns(cls), grad_message, 0, 0)
    sums[0:1, :] += column_sum(grad_message.astype(F32))
    cls_grad[...] = dims(grad_message, w_msg[...], 1, 1)


def collect_kernel(
    frame_size, video_size, videos_here, frames_here,
    *rest,
):
    small, (tg_hbm, output_hbm, output, tokens_grad, *rest) = rest[:10], rest[10:]
    collect(frame_size, video_size, videos_here, frames_here, small, tg_hbm, output_hbm, output, tokens_grad, *rest)


def collect(
    frame_size, video_size, videos_here, frames_here, small, tg_hbm, output_hbm, output, tokens_grad, msg_grad, in_grad, out_grad, *rest,
):
    (
        msg_bias_g, msg_gain_g, msg_shift_g, msg_in_bias_g, msg_out_bias_g, gain1_g, shift1_g,
        attn_in_g, attn_in_bias_g, attn_out_g, attn_out_bias_g, gain2_g, shift2_g, fc_g, fc_bias_g, proj_g, proj_bias_g,
        tg, out, sem, s_small, *kept,
    ) = rest
    f, v = lax.axis_index("frame"), lax.axis_index("video")
    own_rows = D // frame_size

    def load(i):
        return pltpu.make_async_copy(tg_hbm.at[i], tg.at[i], sem.at[0, i])

    def store(i):
        return pltpu.make_async_copy(tg.at[i], tokens_grad.at[i], sem.at[0, i])

    def load_out(i):
        return pltpu.make_async_copy(output_hbm.at[i], out.at[i], sem.at[1, i])

    def store_out(i):
        return pltpu.make_async_copy(out.at[i], output.at[i], sem.at[1, i])

    for i in range(videos_here):
        load(i).start()
        load_out(i).start()
    smalls = [pltpu.make_async_copy(a, b, s_small.at[at]) for at, (a, b) in enumerate(zip(small, kept))]
    for copy in smalls:
        copy.start()
    for copy in smalls:
        copy.wait()
    done, reduced, near, far, totals, acc_msg, acc_in, acc_out, sums, grad_cls = kept
    for i in range(videos_here):
        load(i).wait()
        added = [grad_cls[i * frames_here + j] for j in range(frames_here)]
        tg[i, 0] = tg[i, 0] + jnp.concatenate(added, axis=0)
        store(i).start()
        load_out(i).wait()
        store_out(i).start()

    def own_matrix(target, x):
        size = x.shape[1] // video_size
        target[...] = pltpu.roll(x[:own_rows], lax.rem(x.shape[1] - v * size, x.shape[1]), 1)[:, :size]

    own_matrix(msg_grad, acc_msg[...])
    own_matrix(in_grad, acc_in[...])
    own_matrix(out_grad, acc_out[...])

    def own_vector(target, ref, first, count):
        size = count * D // frame_size
        per_row = frame_size // count
        row = first + lax.div(f, per_row)
        x = ref[pl.ds(row, 1), :]
        x = pltpu.roll(jnp.broadcast_to(x, (8, D)), lax.rem(D - lax.rem(f, per_row) * size, D), 1)
        target[...] = x[0:1, :size].reshape(size)

    mlp_sums, attn_sums = totals.at[0], totals.at[1]
    for target, ref, first, count in (
        (msg_bias_g, sums, 0, 1), (msg_gain_g, sums, 1, 1), (msg_shift_g, sums, 2, 1), (msg_in_bias_g, sums, 3, 2),
        (msg_out_bias_g, sums, 5, 1), (gain1_g, attn_sums, 3, 1), (shift1_g, attn_sums, 4, 1),
        (attn_in_bias_g, attn_sums, 1, 2), (attn_out_bias_g, attn_sums, 0, 1), (gain2_g, mlp_sums, 0, 1),
        (shift2_g, mlp_sums, 1, 1), (fc_bias_g, mlp_sums, 2, 4), (proj_bias_g, mlp_sums, 6, 1),
    ):
        own_vector(target, ref, first, count)
    step = own_rows // UNITS
    columns = D // video_size
    wide_step = 4 * step
    part = FF // UNITS // video_size
    fc = [done[0], reduced[0], reduced[2]]
    for c in range(UNITS):
        for q in range(UNITS):
            for g in range(frame_size // video_size):
                from_at = q * part + g * wide_step
                to = (g * UNITS + c) * wide_step
                fc_g[q * step : q * step + step, to : to + wide_step] = fc[c][:, from_at : from_at + wide_step]
    for u in range(UNITS):
        rows = slice(u * step, u * step + step)
        attn_out_g[rows, :] = near[u][:, in_width(video_size) :]
        for w in range(video_size):

            @pl.when(v == w)
            def _(rows=rows, u=u, w=w):
                for group, parts in enumerate((near, far)):
                    at = 0
                    for _, count, to in in_pieces(group, w, video_size):
                        attn_in_g[rows, to : to + count] = parts[u][:, at : at + count]
                        at += count

    proj = [done[1], reduced[1], reduced[3]]
    proj = [x[:, q * columns : q * columns + columns] for x in proj for q in range(4)]
    proj_g[...] = jnp.concatenate(proj, axis=0).T
    for i in range(videos_here):
        store(i).wait()
        store_out(i).wait()


def shaped(shape, dtype):
    return jax.ShapeDtypeStruct(shape, dtype)


def whole(array):
    shape = array.shape
    return pl.BlockSpec(shape, lambda *_: (0,) * len(shape), pipeline_mode=pl.Buffered(1))


def wholes(*arrays):
    return [whole(array) for array in arrays]


def in_hbm():
    return pl.BlockSpec(memory_space=pl.ANY)


def in_vmem():
    return pl.BlockSpec(memory_space=pltpu.VMEM)


def per_step(count, shape):
    return pl.BlockSpec((count,) + shape, lambda b: (b,) + (0,) * len(shape))


def params(mib, **more):
    return pltpu.CompilerParams(vmem_limit_bytes=mib * MIB, **more)


def on_device(frame_size, video_size, *args):
    (
        tokens, cotangent, msg_weight, msg_bias, msg_norm_gain, msg_norm_shift, msg_in_weight,
        msg_in_bias, msg_out_weight, msg_out_bias, norm1_gain, norm1_shift, attn_in_weight,
        attn_in_bias, attn_out_weight, attn_out_bias, norm2_gain, norm2_shift, fc_weight, fc_bias,
        proj_weight, proj_bias,
    ) = args
    videos_here, frames_here = tokens.shape[:2]
    frames = videos_here * frames_here
    msgs = videos_here * video_size * FRAMES
    group = videos_here * FRAMES
    total = frames * ROWS
    F, V = frame_size, video_size
    step = D // F // UNITS
    n_bits = int(math.log2(F)) - 1
    x = tokens.transpose(0, 2, 1, 3)
    cot = cotangent.transpose(0, 2, 1, 3)
    msg_vectors = (msg_bias, msg_norm_gain, msg_norm_shift, msg_in_bias, msg_out_bias)
    DMA = pltpu.SemaphoreType.DMA

    msg_arrays = (*msg_vectors, msg_weight, msg_in_weight, msg_out_weight)
    kv_shape = (frames, PAIRS, KEYS, 128)

    def second(shape):
        zeros = (0,) * len(shape)
        return pl.BlockSpec((frames_here,) + shape, lambda t: (jnp.maximum(t - videos_here, 0),) + zeros)

    block_shapes = [(PAIRS, ROWS, 2 * KEYS), (PAIRS, ROWS, 128), (ROWS, D), (ROWS, D)]
    fwd_outs = [
        shaped((frames, PAIRS, ROWS, 128), BF), shaped(kv_shape, BF), shaped(kv_shape, BF), shaped((frames, ROWS, D), BF),
        shaped((frames,) + block_shapes[0], BF), shaped((frames,) + block_shapes[1], F32),
        shaped((frames,) + block_shapes[2], BF), shaped((frames,) + block_shapes[3], F32),
        shaped((frames, 1, D), F32), shaped((msgs, D), BF),
    ]
    q, k, v, normed, p, inv, mixed, kept, msg_out, cls = pl.pallas_call(
        functools.partial(attn_fwd_kernel, F, V, frames_here, videos_here),
        grid=(2 * videos_here,),
        in_specs=[
            pl.BlockSpec((1, PATCHES, frames_here, D), lambda t: (jnp.minimum(t, videos_here - 1), 0, 0, 0)), in_hbm(),
        ]
        + wholes(norm1_gain, norm1_shift, attn_in_bias, attn_out_bias, attn_in_weight) + [in_hbm()] * 9,
        out_specs=[in_hbm()] * 4 + [second(shape) for shape in block_shapes] + wholes(*fwd_outs[8:]),
        out_shape=fwd_outs,
        scratch_shapes=[pltpu.VMEM(out.shape, BF) for out in fwd_outs[:4]]
        + [
            pltpu.VMEM((frames, ROWS, D), F32), pltpu.VMEM((D, D), BF),
            pltpu.VMEM((16, D), F32), pltpu.VMEM((16, 3 * D), F32),
            pltpu.VMEM((videos_here, frames_here, D), BF),
            pltpu.VMEM((V, videos_here, F, frames_here, D), BF),
            pltpu.VMEM((group, D), F32), pltpu.VMEM((group, D), F32),
        ]
        + [pltpu.VMEM(a.shape, BF) for a in msg_arrays]
        + msg_scratch(group) + [DMA((V, F + V)), DMA((V, F + V)), DMA((11,)), DMA((4,))],
        compiler_params=params(63, collective_id=1, has_side_effects=True),
        name="attn_fwd",
    )(x, x, norm1_gain, norm1_shift, attn_in_bias, attn_out_bias, attn_in_weight, attn_out_weight, *msg_arrays)

    def bit_buffers(units, width=FF):
        return [
            pltpu.VMEM((units, max(1, F >> (2 + i)), step, width), BF) if i < n_bits else pltpu.VMEM((1, 1, 16, 128), BF)
            for i in range(3)
        ]

    def exchange_sems(units):
        return [DMA((units,)), DMA((units,)), DMA((units, n_bits, F // 4)), DMA((units, n_bits, F // 4)), DMA((units, V)), DMA((units, V))]

    def unit_buffers(count, units):
        return [pltpu.VMEM((count,) + shape, BF) for shape in units]

    block_shape = (F // 2, step, FF)
    part_shape = (V, step, FF // V)
    width = FF // UNITS
    mlp_outs = [
        shaped(x.shape, BF), shaped(kept.shape, F32), shaped((2, step, FF // V), F32), shaped((2, step, FF), BF),
        shaped((2, 2) + block_shape, BF), shaped((8, D), F32),
    ]
    output, grad_kept, done, mid, raw, mlp_sums = pl.pallas_call(
        functools.partial(mlp_kernel, F, V, videos_here, frames_here),
        grid=(UNITS,),
        in_specs=[in_hbm()] * 2 + wholes(norm2_gain, norm2_shift, fc_bias, proj_bias) + [in_hbm()] * 2,
        out_specs=[in_hbm()] * 2 + wholes(*mlp_outs[2:4]) + [in_hbm()] + wholes(mlp_outs[5]),
        out_shape=mlp_outs,
        scratch_shapes=[
            pltpu.VMEM(kept.shape, F32), pltpu.VMEM(x.shape, BF), pltpu.VMEM(kept.shape, F32),
            pltpu.VMEM((frames_here, ROWS, D), F32),
            pltpu.VMEM((total, D), BF), pltpu.VMEM((total, D), BF), pltpu.VMEM((total, width), BF), pltpu.VMEM((total, width), BF),
            pltpu.VMEM((total, D), F32), pltpu.VMEM((total, D), F32),
            pltpu.VMEM((UNITS, width), F32), pltpu.VMEM((UNITS, width), F32),
            pltpu.VMEM((2, D, width), BF), pltpu.VMEM((2, width, D), BF),
            pltpu.VMEM((D, FF) if 4 * step % 128 else (16, 128), BF),
            pltpu.VMEM((2 * UNITS, 2) + block_shape, BF), pltpu.VMEM((4,) + block_shape, BF),
        ]
        + bit_buffers(4) + unit_buffers(2, [part_shape] * 2)
        + [DMA((2, videos_here)), DMA((2, 2, F)), DMA((1,))] + exchange_sems(4),
        compiler_params=params(63, collective_id=2, has_side_effects=True),
        name="mlp",
    )(kept, cot, norm2_gain, norm2_shift, fc_bias, proj_bias, fc_weight, proj_weight)

    rows_own, columns = D // F, D // V
    padded = -(-rows_own // 128) * 128
    widths = (3 * HALF + D, 3 * HALF)
    part_widths = (in_width(V) + columns, in_width(V))
    back_outs = [
        shaped(x.shape, F32), shaped((4, step, FF // V), F32), shaped((UNITS, step, part_widths[0]), F32),
        shaped((UNITS, step, part_widths[1]), F32), shaped((2, 8, D), F32),
        shaped((padded, D), F32), shaped((padded, 3 * D), F32), shaped((padded, D), F32), shaped((8, D), F32),
        shaped((frames, 1, D), F32),
    ]
    def group_buffers(width, part_width):
        block = (F // 2, step, width)
        return [pltpu.VMEM((2, UNITS) + block, BF), pltpu.VMEM((UNITS,) + block, BF)] + bit_buffers(UNITS, width) + [
            pltpu.VMEM((UNITS, V, step, part_width), BF)
        ] * 2

    def by_pairs(shape):
        return pl.BlockSpec((1, PAIRS // 2) + shape, lambda t: (lax.rem(t, frames), lax.div(t, frames), 0, 0))

    tg, reduced, near, far, totals, acc_msg, acc_in, acc_out, msg_sums, grad_cls = pl.pallas_call(
        functools.partial(attn_back_kernel, F, V, videos_here, frames_here),
        grid=(2 * frames,),
        in_specs=[in_hbm()] * 5
        + wholes(msg_out, norm1_gain, norm1_shift, attn_out_weight, mlp_sums, mid)
        + [in_hbm()] + wholes(cls) + [in_hbm()] * 8
        + [by_pairs(shape) for shape in ((ROWS, 128), (KEYS, 128), (KEYS, 128), (ROWS, 2 * KEYS), (ROWS, 128))],
        out_specs=[in_hbm()] + wholes(*back_outs[1:]),
        out_shape=back_outs,
        scratch_shapes=[
            pltpu.VMEM(x.shape, BF), pltpu.VMEM(normed.shape, BF), pltpu.VMEM((D, 3 * D), BF),
            pltpu.VMEM(grad_kept.shape, F32), pltpu.VMEM(mixed.shape, BF),
            pltpu.VMEM((frames_here, ROWS, D), F32), pltpu.VMEM((frames_here, PATCHES, D), F32),
            pltpu.VMEM((max(total, D), 3 * D), BF), pltpu.VMEM((frames, ROWS, D), BF), pltpu.VMEM((8, D), F32), pltpu.VMEM((16, 3 * D), F32), pltpu.VMEM((8, D), F32),
            pltpu.VMEM((videos_here, frames_here, D), BF), pltpu.VMEM((V, videos_here, F, frames_here, D), BF),
            pltpu.VMEM((msgs, D), BF), pltpu.VMEM((group, D), F32), pltpu.VMEM((msgs, D), F32),
            pltpu.VMEM((2,) + block_shape, BF), pltpu.VMEM((2,) + block_shape, BF),
        ]
        + bit_buffers(2) + unit_buffers(4, [part_shape] * 2)
        + group_buffers(widths[0], part_widths[0]) + group_buffers(widths[1], part_widths[1])
        + [pltpu.VMEM((2, F, 8, D), F32), pltpu.VMEM((2, 8, D), F32), pltpu.VMEM((2, V, 8, D), F32)]
        + [pltpu.VMEM(a.shape, BF) for a in msg_arrays if a is not msg_in_weight]
        + [pltpu.VMEM((BLOCK, 3 * D), BF), pltpu.VMEM((BLOCK, D), F32)] + msg_scratch(BLOCK)
        + [DMA((2, frames)), DMA((8,)), DMA((8,)), DMA((2,)), DMA((frames_here,))]
        + [DMA((2, 2, max(F, V))), DMA((2, 2, max(F, V))), DMA((V, F + V)), DMA((V, F + V))]
        + exchange_sems(4) + exchange_sems(UNITS) + exchange_sems(UNITS),
        compiler_params=params(63, collective_id=3, has_side_effects=True),
        name="attn_back",
    )(
        x, normed, attn_in_weight, grad_kept, mixed, msg_out, norm1_gain, norm1_shift, attn_out_weight, mlp_sums, mid, raw, cls,
        *msg_arrays, q, k, v, p, inv,
    )

    out_shapes = [
        (rows_own, columns), (rows_own, 3 * columns), (rows_own, columns),
        (rows_own,), (rows_own,), (rows_own,), (2 * rows_own,), (rows_own,), (rows_own,), (rows_own,),
        (rows_own, 3 * columns), (2 * rows_own,), (rows_own, columns), (rows_own,), (rows_own,), (rows_own,),
        (rows_own, 4 * columns), (4 * rows_own,), (columns, 4 * rows_own), (rows_own,),
    ]
    out_shapes = [shaped(shape, F32) for shape in out_shapes]
    (
        output, tokens_grad, msg_grad, msg_in_grad, msg_out_grad,
        msg_bias_g, msg_gain_g, msg_shift_g, msg_in_bias_g, msg_out_bias_g, gain1_g, shift1_g,
        attn_in_g, attn_in_bias_g, attn_out_g, attn_out_bias_g, gain2_g, shift2_g, fc_g, fc_bias_g, proj_g, proj_bias_g,
    ) = pl.pallas_call(
        functools.partial(collect_kernel, F, V, videos_here, frames_here),
        grid=(1,),
        in_specs=[in_hbm()] * 12,
        out_specs=[in_hbm()] * 2 + wholes(*out_shapes),
        out_shape=[shaped(x.shape, BF), shaped(x.shape, F32)] + out_shapes,
        scratch_shapes=[pltpu.VMEM(x.shape, F32), pltpu.VMEM(x.shape, BF), DMA((2, videos_here)), DMA((10,))]
        + [pltpu.VMEM(a.shape, F32) for a in (done, reduced, near, far, totals, acc_msg, acc_in, acc_out, msg_sums, grad_cls)],
        compiler_params=params(63),
        name="collect",
    )(done, reduced, near, far, totals, acc_msg, acc_in, acc_out, msg_sums, grad_cls, tg, output)

    return (
        output.transpose(0, 2, 1, 3), tokens_grad.transpose(0, 2, 1, 3),
        msg_grad, msg_bias_g, msg_gain_g, msg_shift_g, msg_in_grad, msg_in_bias_g, msg_out_grad, msg_out_bias_g,
        gain1_g, shift1_g, attn_in_g, attn_in_bias_g, attn_out_g, attn_out_bias_g,
        gain2_g, shift2_g, fc_g, fc_bias_g, proj_g.T, proj_bias_g,
    )


def solution(mesh):
    rows = P("video", "frame", None, None)
    matrix, vector = P("frame", "video"), P("frame")
    out_specs = (
        rows, rows,
        matrix, vector, vector, vector, matrix, vector, matrix, vector,
        vector, vector, matrix, vector, matrix, vector,
        vector, vector, matrix, vector, matrix, vector,
    )
    return jax.shard_map(
        functools.partial(on_device, mesh.shape["frame"], mesh.shape["video"]),
        mesh=mesh, in_specs=(rows, rows) + (P(),) * 20, out_specs=out_specs, check_vma=False,
    )
```

```python
import functools
import math

import jax
import jax.numpy as jnp
from jax import lax
from jax.experimental import pallas as pl
from jax.experimental.pallas import tpu as pltpu
from jax.sharding import PartitionSpec as P

D = 768
HEADS = 12
PAIRS = 6
FF = 3072
PATCHES = 197
JOINED = 198
ROWS = 208
KEYS = 256
HALF = D // 2
FRAMES = 16
BLOCK = 192
UNITS = 3
BF = jnp.bfloat16
F32 = jnp.float32
MIB = 1 << 20
MESH = pl.DeviceIdType.MESH


def vec(ref, at=0):
    return ref[...].astype(F32).reshape(1, ref.shape[0])[:, at * D : at * D + D]


def dims(a, b, ca, cb):
    return lax.dot_general(a, b, (((ca,), (cb,)), ((), ())), preferred_element_type=F32)


def column_sum(x):
    return jnp.sum(x, axis=0, keepdims=True)


def norm_fwd(x, gain, shift):
    centre = x - jnp.mean(x, axis=-1, keepdims=True)
    inv = lax.rsqrt(jnp.mean(centre * centre, axis=-1, keepdims=True) + 1e-05)
    unit = centre * inv
    return unit * gain + shift, unit, inv


def norm_back(grad, unit, inv, gain):
    scaled = grad * gain
    return inv * (
        scaled
        - jnp.mean(scaled, axis=-1, keepdims=True)
        - unit * jnp.mean(scaled * unit, axis=-1, keepdims=True)
    )


def low_half():
    return lax.broadcasted_iota(jnp.int32, (1, 128), 1) < 64


def half(low, head, value, other):
    return jnp.where(low, value, other) if head == 0 else jnp.where(low, other, value)


def pair_fwd(q, k, v, mask_scores, keep):
    low = low_half()
    sums = []
    for head in range(2):
        scores = mask_scores(dims(q, half(low, head, k, jnp.zeros_like(k)), 1, 1))
        top = jnp.max(scores, axis=1, keepdims=True)
        probs = jnp.exp(scores - top).astype(BF)
        keep(head, probs)
        sums.append(dims(probs, half(low, head, v, jnp.ones_like(v)), 1, 0))
    inv = 1.0 / pltpu.roll(jnp.where(low, sums[1], sums[0]), 64, 1)
    return jnp.where(low, sums[0], sums[1]) * inv, inv


def pair_back(q, k, v, grad, mixed, inv, probs):
    low = low_half()
    scaled = grad * inv
    scaled_low = scaled.astype(BF)
    minus = -pltpu.roll(mixed.astype(F32) * scaled, 64, 1)
    totals = None
    for head in range(2):
        p = probs(head)
        centred = dims(half(low, head, scaled, minus).astype(BF), half(low, head, v, jnp.ones_like(v)), 1, 1)
        grad_s = (p.astype(F32) * centred).astype(BF)
        terms = (
            dims(grad_s, half(low, head, k, jnp.zeros_like(k)), 1, 0),
            dims(grad_s, half(low, head, q, jnp.zeros_like(q)), 0, 0),
            dims(p, half(low, head, scaled_low, jnp.zeros_like(scaled_low)), 0, 0),
        )
        totals = terms if totals is None else tuple(a + b for a, b in zip(totals, terms))
    return totals[0] * 0.125, totals[1], totals[2]


def lanes(pair):
    return slice(pair * 128, pair * 128 + 128)


def msg_mask(rows):
    row = lax.broadcasted_iota(jnp.int32, (rows, rows), 0) // FRAMES
    col = lax.broadcasted_iota(jnp.int32, (rows, rows), 1) // FRAMES
    same = row == col
    return lambda scores: jnp.where(same, scores, -1e30)


def msg_scratch(rows):
    return [
        pltpu.VMEM((rows, 3 * D), BF), pltpu.VMEM((HEADS, rows, rows), BF), pltpu.VMEM((rows, D), F32), pltpu.VMEM((rows, D), BF),
        pltpu.VMEM((rows, D), BF), pltpu.VMEM((rows, D), F32),
    ]


def pair_lanes(pair, kind=0):
    return pl.ds(pl.multiple_of(kind * D + pair * 128, 128), 128)


def msg_forward(cls, biases, w_msg, w_in, w_out, scratch, unroll):
    bias, gain, shift, in_bias, _ = biases
    qkv, probs, invs, mixed, normed_low, message = scratch
    message[...] = dims(cls, w_msg[...], 1, 0) + vec(bias)
    normed, unit, inv_std = norm_fwd(message[...], vec(gain), vec(shift))
    normed_low[...] = normed.astype(BF)

    def project(kind, bias, scale):
        columns = slice(kind * D, kind * D + D)
        qkv[:, columns] = ((dims(normed_low[...], w_in[:, columns], 1, 0) + bias) * scale).astype(BF)

    project(0, vec(in_bias), 0.125)
    project(1, 0.0, 1.0)
    project(2, vec(in_bias, 1), 1.0)
    mask = msg_mask(cls.shape[0])

    @pl.loop(0, PAIRS, unroll=unroll)
    def _(pair):
        def keep(head, p):
            probs[2 * pair + head] = p

        out, inv = pair_fwd(qkv[:, pair_lanes(pair)], qkv[:, pair_lanes(pair, 1)], qkv[:, pair_lanes(pair, 2)], mask, keep)
        mixed[:, pair_lanes(pair)] = out.astype(BF)
        invs[:, pair_lanes(pair)] = inv

    return unit, inv_std


class Place:
    def __init__(self, frame_size, video_size):
        self.F, self.V = frame_size, video_size
        self.f, self.v = lax.axis_index("frame"), lax.axis_index("video")
        self.core = lax.rem(self.f, 2)
        self.bits = [lax.rem(lax.div(self.f, 1 << i), 2) for i in range(int(math.log2(frame_size)))]

    def frame_peer(self, step):
        return {"frame": lax.rem(self.f + step, self.F)}

    def video_peer(self, step):
        return {"video": lax.rem(self.v + step, self.V)}

    def greet(self):
        self.announce()
        self.meet()

    def announce(self):
        barrier = pltpu.get_barrier_semaphore()

        @pl.loop(1, self.F)
        def _(step):
            pl.semaphore_signal(barrier, inc=1, device_id=self.frame_peer(step), device_id_type=MESH)

        @pl.loop(1, self.V)
        def _(step):
            pl.semaphore_signal(barrier, inc=1, device_id=self.video_peer(step), device_id_type=MESH)

    def meet(self):
        pl.semaphore_wait(pltpu.get_barrier_semaphore(), self.F + self.V - 2)


def remote(src, dst, send, recv, peer):
    return pltpu.make_async_remote_copy(
        src_ref=src, dst_ref=dst, send_sem=send, recv_sem=recv, device_id=peer, device_id_type=MESH
    )


class Gather:
    def __init__(self, place, own, rows, send, recv):
        self.place, self.own, self.rows, self.send, self.recv = place, own, rows, send, recv

    def near_copy(self, step, arriving):
        place = self.place
        frame = lax.rem(place.f + place.F - step, place.F) if arriving else place.f
        return remote(
            self.own, self.rows.at[place.v, :, frame], self.send.at[0, step], self.recv.at[0, step], place.frame_peer(step)
        )

    def far_copy(self, hop, arriving):
        place = self.place
        video = lax.rem(place.v + place.V - hop, place.V) if arriving else place.v
        slot = place.F - 1 + hop
        return remote(
            self.own, self.rows.at[video, :, place.f], self.send.at[0, slot], self.recv.at[0, slot], place.video_peer(hop)
        )

    def passed_copy(self, hop, step, arriving):
        place = self.place
        video = lax.rem(place.v + place.V - hop, place.V)
        frame = lax.rem(place.f + place.F - step, place.F) if arriving else place.f
        part = self.rows.at[video, :, frame]
        return remote(part, part, self.send.at[hop, step], self.recv.at[hop, step], place.frame_peer(step))

    def each_frame(self, call):
        pl.loop(1, self.place.F)(call)

    def each_video(self, call):
        pl.loop(1, self.place.V)(call)

    def start(self, far=True):
        self.each_frame(lambda step: self.near_copy(step, False).start())
        self.each_video(lambda hop: self.far_copy(hop, False).start())

    def near(self):
        self.each_frame(lambda step: self.near_copy(step, True).wait_recv())

    def forward(self):
        @pl.loop(1, self.place.V)
        def _(hop):
            self.far_copy(hop, True).wait_recv()
            self.each_frame(lambda step: self.passed_copy(hop, step, False).start())

    def finish(self):
        @pl.loop(1, self.place.V)
        def _(hop):
            def passed(step):
                self.passed_copy(hop, step, True).wait_recv()
                self.passed_copy(hop, step, False).wait_send()

            self.each_frame(passed)
            self.far_copy(hop, False).wait_send()

        self.each_frame(lambda step: self.near_copy(step, False).wait_send())


def attn_fwd_kernel(
    frame_size, video_size, frames_here, videos_here,
    x_ref, x_hbm, gain1, shift1, in_bias1, out_bias1, w_in1, w_out_hbm, *rest,
):
    operands, rest = rest[:8], rest[8:]
    (
        q_hbm, k_hbm, v_hbm, normed_hbm, p_ref, inv_ref, mixed_ref, kept_ref, out_ref, cls_ref,
        q_ref, k_ref, v_ref, normed_ref, joined, w_out1, msg_rows, msg_wide, own, rows, wide, mixed_out, *rest,
    ) = rest
    kept, scratch, (send, recv, local, s_out) = rest[:8], rest[8:14], rest[14:]
    bias, gain, shift, in_bias, out_bias, w_msg, w_in, w_out = kept
    place = Place(frame_size, video_size)
    t = pl.program_id(0)
    i = lax.rem(t, videos_here)
    frames = videos_here * frames_here
    every = frames_here * ROWS
    gather = Gather(place, own, rows, send, recv)

    def loads():
        pairs = [(x_hbm.at[:, 0], own), (x_hbm.at[:, 0], rows.at[place.v, :, place.f]), (w_out_hbm, w_out1)]
        pairs += list(zip(operands, kept))
        return [pltpu.make_async_copy(source, target, local.at[at]) for at, (source, target) in enumerate(pairs)]

    def stores():
        pairs = ((q_ref, q_hbm), (k_ref, k_hbm), (v_ref, v_hbm), (normed_ref, normed_hbm))
        return [pltpu.make_async_copy(source, target, s_out.at[at]) for at, (source, target) in enumerate(pairs)]

    @pl.when(t == 0)
    def _():
        place.announce()
        for load in loads():
            load.start()

    @pl.when(t == min(1, videos_here - 1))
    def _():
        for load in loads()[:2]:
            load.wait()
        place.meet()
        gather.start()

    @pl.when(t < videos_here)
    def _():
        x = x_ref[0].astype(F32)
        first = i * frames_here
        for j in range(frames_here):
            joined[first + j, 0:PATCHES, :] = x[:, j, :]
            joined[first + j, PATCHES:ROWS, :] = jnp.zeros((ROWS - PATCHES, D), F32)
        here = pl.ds(first, frames_here)
        normed, _, _ = norm_fwd(joined[here].reshape(every, D), vec(gain1), vec(shift1))
        normed_ref[here] = normed.astype(BF).reshape(frames_here, ROWS, D)
        normed = normed_ref[here].reshape(every, D)
        pad = jnp.zeros((KEYS - ROWS, 128), BF)
        qkv = dims(normed, w_in1[...], 1, 0)
        q = ((qkv[:, :D] + vec(in_bias1)) * 0.125).astype(BF)
        k = qkv[:, D : 2 * D].astype(BF)
        v = (qkv[:, 2 * D :] + vec(in_bias1, 1)).astype(BF)
        for j in range(frames_here):
            part = slice(j * ROWS, j * ROWS + ROWS)
            for pair in range(PAIRS):
                sl = lanes(pair)
                q_ref[first + j, pair] = q[part, sl]
                k_ref[first + j, pair, 0:ROWS] = k[part, sl]
                k_ref[first + j, pair, ROWS:KEYS] = pad
                v_ref[first + j, pair, 0:ROWS] = v[part, sl]
                v_ref[first + j, pair, ROWS:KEYS] = pad

    def unpack(video):
        for n in range(videos_here):
            for f in range(frame_size):
                at = (n * frame_size + f) * frames_here
                wide[at : at + frames_here, :] = rows[video, n, f].astype(F32)

    @pl.when(t == videos_here)
    def _():
        gather.near()
        gather.forward()
        unpack(place.v)
        for load in loads()[2:]:
            load.wait()
        biases = (bias, gain, shift, in_bias, out_bias)
        msg_forward(wide[...].astype(BF), biases, w_msg, w_in, w_out, scratch, PAIRS)
        mixed_out[...] = scratch[5][...] + dims(scratch[3][...], w_out[...], 1, 0) + vec(out_bias)
        msg_rows[...] = jnp.zeros_like(msg_rows)
        for n in range(videos_here):
            for j in range(frames_here):
                c = n * frames_here + j
                row = mixed_out[pl.ds(n * FRAMES + place.f * frames_here + j, 1), :]
                out_ref[c] = row
                msg_rows[c : c + 1, :] = row
                joined[c, PATCHES : PATCHES + 1, :] = row
        normed, _, _ = norm_fwd(msg_rows[...], vec(gain1), vec(shift1))
        low = normed.astype(BF)
        msg_wide[:, :D] = low.astype(F32)
        msg_wide[:, D : 2 * D] = dims(low, w_in1[:, D : 2 * D], 1, 0)
        msg_wide[:, 2 * D :] = dims(low, w_in1[:, 2 * D :], 1, 0) + vec(in_bias1, 1)
        at = PATCHES - PATCHES % 16
        mine = lax.broadcasted_iota(jnp.int32, (16, 1), 0) == PATCHES % 16
        block = slice(at, at + 16)

        @pl.loop(0, frames)
        def _(c):
            row = msg_wide[pl.ds(c, 1), :]
            normed_ref[c, block, :] = jnp.where(mine, row[:, :D], normed_ref[c, block, :].astype(F32)).astype(BF)
            for pair in range(PAIRS):
                for target, lo in ((k_ref, D), (v_ref, 2 * D)):
                    part = row[:, lo + pair * 128 : lo + pair * 128 + 128]
                    target[c, pair, block, :] = jnp.where(mine, part, target[c, pair, block, :].astype(F32)).astype(BF)

        for store in stores():
            store.start()

    valid = lax.broadcasted_iota(jnp.int32, (1, KEYS - 128), 1) < JOINED - 128

    def mask(scores):
        return jnp.concatenate([scores[:, :128], jnp.where(valid, scores[:, 128:], -1e30)], axis=1)

    @pl.when(t >= videos_here)
    def _():
        first = i * frames_here

        @pl.loop(0, frames_here)
        def _(j):
            c = first + j
            for pair in range(PAIRS):

                def keep(head, p, pair=pair):
                    p_ref[j, pair, :, head * KEYS : head * KEYS + KEYS] = p

                out, inv = pair_fwd(q_ref[c, pair], k_ref[c, pair], v_ref[c, pair], mask, keep)
                inv_ref[j, pair] = inv
                mixed_ref[j, :, lanes(pair)] = out.astype(BF)

        attended = dims(mixed_ref[...].reshape(every, D), w_out1[...], 1, 0) + vec(out_bias1)
        kept_ref[...] = joined[pl.ds(first, frames_here)] + attended.reshape(frames_here, ROWS, D)

    @pl.when(t == 2 * videos_here - 1)
    def _():
        gather.finish()
        count = videos_here * FRAMES
        for video in range(video_size):
            unpack(video)
            cls_ref[video * count : video * count + count, :] = wide[...].astype(BF)
        for store in stores():
            store.wait()


def fc_parts(x, w, V):
    size, width = FF // UNITS // V, FF // UNITS
    return jnp.concatenate([x[:, q * width + w * size : q * width + w * size + size] for q in range(UNITS)], axis=1)


def proj_parts(x, w, V):
    size = D // V
    return jnp.concatenate([x[:, q * D + w * size : q * D + w * size + size] for q in range(4)], axis=1)


MLP_PARTS = (fc_parts, proj_parts)


def in_pieces(group, w, V):
    size, out = 3 * D // V, []
    for kind in range(3):
        first = kind * D + group * HALF
        lo, hi = max(first, w * size), min(first + HALF, w * size + size)
        if hi > lo:
            out.append((kind * HALF + lo - first, hi - lo, lo - w * size))
    return out


def in_width(V):
    return max(sum(piece[1] for piece in in_pieces(g, w, V)) for g in range(2) for w in range(V))


def attn_parts(group):
    def parts(x, w, V):
        pieces = [x[:, at : at + count] for at, count, _ in in_pieces(group, w, V)]
        short = in_width(V) - sum(piece.shape[1] for piece in pieces)
        if short:
            pieces.append(jnp.zeros((x.shape[0], short), F32))
        if group == 0:
            size = D // V
            pieces.append(x[:, 3 * HALF + w * size : 3 * HALF + w * size + size])
        return jnp.concatenate(pieces, axis=1) if len(pieces) > 1 else pieces[0]

    return parts


class Scatter:
    def __init__(self, place, step, acc, recv0, recv_bits, send3, recv3, result, sems, first=0):
        self.place, self.step, self.acc, self.first = place, step, acc, first
        self.recv0, self.recv_bits, self.send3, self.recv3, self.result = recv0, recv_bits, send3, recv3, result
        self.sems = sems
        self.n_bits = len(place.bits) - 1

    def other_core(self):
        return {"frame": self.place.f + 1 - 2 * self.place.core}

    def exchange0(self, unit, source):
        return remote(source, self.recv0.at[unit - self.first], self.sems["send0"].at[unit], self.sems["recv0"].at[unit], self.other_core())

    def order(self, core, stage):
        return stage if core == 0 else self.n_bits - 1 - stage

    def blocks(self, stage, flip):
        place, n = self.place, self.n_bits
        free = n - 1 - stage
        out = []
        for i in range(1 << free):
            both = []
            for core in range(2):
                done = [self.order(core, s) for s in range(stage)]
                now = self.order(core, stage)
                rest = [bit for bit in range(n) if bit not in done and bit != now]
                at = 0
                for bit in done:
                    at = at + place.bits[bit + 1] * (1 << bit)
                own = place.bits[now + 1]
                at = at + ((1 - own) if flip else own) * (1 << now)
                for index, bit in enumerate(rest):
                    at = at + ((i >> index) & 1) * (1 << bit)
                both.append(at)
            out.append((1 - place.core) * both[0] + place.core * both[1])
        return out

    def partner(self, stage):
        place = self.place
        moves = []
        for core in range(2):
            bit = self.order(core, stage) + 1
            moves.append((1 - 2 * place.bits[bit]) * (1 << bit))
        return {"frame": place.f + (1 - place.core) * moves[0] + place.core * moves[1]}

    def exchange(self, unit, stage, i, block):
        sems = self.sems
        return remote(
            self.acc(unit, block), self.recv_bits[stage].at[unit - self.first, i],
            sems["send_bits"].at[unit, stage, i], sems["recv_bits"].at[unit, stage, i], self.partner(stage),
        )

    def add(self, unit, block, came):
        target = self.acc(unit, block)
        target[...] = target[...] + came

    def stage(self, unit, stage):
        if stage == 0:
            self.exchange0(unit, self.recv0.at[unit - self.first]).wait_recv()
            came = lambda position, block: self.recv0[unit - self.first, block]
        else:
            for i in range(1 << (self.n_bits - stage)):
                self.exchange(unit, stage - 1, i, 0).wait_recv()
            came = lambda position, block: self.recv_bits[stage - 1][unit - self.first, position]
        if stage == self.n_bits:
            block = self.own_block()
            self.add(unit, block, came(0, block))
            return
        sending, staying = self.blocks(stage, True), self.blocks(stage, False)
        where = self.positions(stage)
        for i, block in enumerate(sending):
            self.add(unit, block, came(where[1][i], block))
            self.exchange(unit, stage, i, block).start()
        for i, block in enumerate(staying):
            self.add(unit, block, came(where[0][i], block))

    def positions(self, stage):
        place, n = self.place, self.n_bits
        if stage == 0:
            return [[None] * (1 << (n - 1))] * 2
        out = [[], []]
        for flip in range(2):
            for i in range(1 << (n - 1 - stage)):
                both = []
                for core in range(2):
                    done = [self.order(core, s) for s in range(stage)]
                    now = self.order(core, stage)
                    rest_before = [bit for bit in range(n) if bit not in done]
                    rest = [bit for bit in rest_before if bit != now]
                    own = place.bits[now + 1]
                    at = 0
                    for index, bit in enumerate(rest_before):
                        if bit == now:
                            at = at + ((1 - own) if flip else own) * (1 << index)
                        else:
                            at = at + ((i >> rest.index(bit)) & 1) * (1 << index)
                    both.append(at)
                out[flip].append((1 - place.core) * both[0] + place.core * both[1])
        return out

    def own_block(self):
        return lax.div(self.place.f, 2)

    def across(self, unit, hop):
        place, sems = self.place, self.sems
        to = lax.rem(place.v + hop, place.V)
        return remote(
            self.send3.at[unit, to], self.recv3.at[unit, hop],
            sems["send3"].at[unit, hop], sems["recv3"].at[unit, hop], place.video_peer(hop),
        )

    def middle(self, unit):
        for stage in range(1, self.n_bits):
            self.stage(unit, stage)

    def land(self, unit):
        self.stage(unit, self.n_bits)
        return self.acc(unit, self.own_block())

    def send_video(self, unit, parts, value):
        value = value.astype(F32)
        for w in range(self.place.V):
            self.send3[unit, w] = parts(value, w, self.place.V).astype(BF)
        pl.loop(1, self.place.V)(lambda hop: self.across(unit, hop).start())

    def finish(self, unit):
        self.result[unit] = self.send3[unit, self.place.v].astype(F32)

        @pl.loop(1, self.place.V)
        def _(hop):
            self.across(unit, hop).wait_recv()
            self.result[unit] += self.recv3[unit, hop].astype(F32)

    def drain(self, unit, source):
        self.exchange0(unit, source).wait_send()
        for stage in range(self.n_bits):
            for i in range(1 << (self.n_bits - 1 - stage)):
                self.exchange(unit, stage, i, 0).wait_send()

    def drain_video(self, unit):
        pl.loop(1, self.place.V)(lambda hop: self.across(unit, hop).wait_send())


class Totals:
    def __init__(self, place, which, own, near, middle, far, result, sems):
        self.place, self.which, self.own, self.near_buf, self.middle = place, which, own, near, middle
        self.far_buf, self.result, self.sems = far, result, sems

    def near(self, step):
        sems = self.sems
        return remote(
            self.own, self.near_buf.at[self.which, step], sems["vec_send"].at[self.which, 0, step],
            sems["vec_recv"].at[self.which, 0, step], self.place.frame_peer(step),
        )

    def far(self, hop):
        sems = self.sems
        return remote(
            self.middle.at[self.which], self.far_buf.at[self.which, hop], sems["vec_send"].at[self.which, 1, hop],
            sems["vec_recv"].at[self.which, 1, hop], self.place.video_peer(hop),
        )

    def start(self):
        pl.loop(1, self.place.F)(lambda step: self.near(step).start())

    def forward(self):
        self.middle[self.which] = self.own[...]

        @pl.loop(1, self.place.F)
        def _(step):
            self.near(step).wait_recv()
            self.middle[self.which] += self.near_buf[self.which, step]

        pl.loop(1, self.place.V)(lambda hop: self.far(hop).start())

    def finish(self):
        self.result[self.which] = self.middle[self.which]

        @pl.loop(1, self.place.V)
        def _(hop):
            self.far(hop).wait_recv()
            self.result[self.which] += self.far_buf[self.which, hop]
            self.far(hop).wait_send()

        pl.loop(1, self.place.F)(lambda step: self.near(step).wait_send())


def mlp_kernel(
    frame_size, video_size, videos_here, frames_here,
    kept_hbm, cot_hbm, gain, shift, fc_bias, proj_bias, fc_hbm, proj_hbm,
    out_hbm, grad_hbm, done_ref, mid_ref, raw_hbm, sums,
    kept_ref, cot_ref, grad_ref, wide, normed2, cot2, act, grad_h, out_acc, grad_acc, bias_rows, bias_sums, fc_buf, proj_buf, fc_all,
    grads, recv0, recv_a, recv_b, recv_c, send3, recv3,
    s_rows, s_load, s_raw, s_send0, s_recv0, s_sendb, s_recvb, s_send3, s_recv3,
):
    chunk = pl.program_id(0)
    frames = videos_here * frames_here
    place = Place(frame_size, video_size)
    step = D // frame_size // UNITS
    wide_step = 4 * step
    width = FF // UNITS
    sems = dict(send0=s_send0, recv0=s_recv0, send_bits=s_sendb, recv_bits=s_recvb, send3=s_send3, recv3=s_recv3)
    scatter = Scatter(
        place, step, lambda unit, block: grads.at[unit, 0, block], recv0, [recv_a, recv_b, recv_c], send3, recv3, done_ref, sems
    )
    sliced = wide_step % 128 == 0

    def rows_of(b, count=1):
        return pl.ds(pl.multiple_of(b * count * ROWS, ROWS), count * ROWS)

    def loads(c):
        slot = lax.rem(c, 2)
        out = []
        for f in range(frame_size):
            at = pl.multiple_of((f * UNITS + c) * wide_step, wide_step)
            to = slice(f * wide_step, f * wide_step + wide_step)
            out.append(pltpu.make_async_copy(proj_hbm.at[pl.ds(at, wide_step)], proj_buf.at[slot, to], s_load.at[slot, 0, f]))
            if sliced:
                out.append(pltpu.make_async_copy(fc_hbm.at[:, pl.ds(at, wide_step)], fc_buf.at[slot, :, to], s_load.at[slot, 1, f]))
        return out

    def row_loads(i):
        part = pl.ds(i * frames_here, frames_here)
        return [
            pltpu.make_async_copy(kept_hbm.at[part], kept_ref.at[part], s_rows.at[0, i]),
            pltpu.make_async_copy(cot_hbm.at[i], cot_ref.at[i], s_rows.at[1, i]),
        ]

    def row_stores(i):
        part = pl.ds(i * frames_here, frames_here)
        return [
            pltpu.make_async_copy(grad_ref.at[part], grad_hbm.at[part], s_rows.at[0, i]),
            pltpu.make_async_copy(cot_ref.at[i], out_hbm.at[i], s_rows.at[1, i]),
        ]

    def load_all():
        return pltpu.make_async_copy(fc_hbm, fc_all, s_load.at[0, 1, 0])

    @pl.when(chunk == 0)
    def _():
        place.announce()
        for n in range(videos_here):
            for load in row_loads(n):
                load.start()
        for load in loads(chunk):
            load.start()
        if not sliced:
            load_all().start()
        sums[...] = jnp.zeros_like(sums)
        bias_sums[...] = jnp.zeros_like(bias_sums)
        wide[:, PATCHES:ROWS, :] = jnp.zeros((frames_here, ROWS - PATCHES, D), F32)
        bias = fc_bias[...].astype(F32).reshape(1, FF)
        for c in range(UNITS):
            for f in range(frame_size):
                at = (f * UNITS + c) * wide_step
                bias_rows[c : c + 1, f * wide_step : f * wide_step + wide_step] = bias[:, at : at + wide_step]

        @pl.loop(0, videos_here)
        def _(i):
            for load in row_loads(i):
                load.wait()
            cot = cot_ref[i].astype(F32)
            for j in range(frames_here):
                wide[j, 0:PATCHES, :] = cot[:, j, :]
            for j in range(frames_here):
                b = i * frames_here + j
                cot_j = wide[j]
                cot2[rows_of(b), :] = cot_j.astype(BF)
                sums[6:7, :] += column_sum(cot_j)
                normed, _, _ = norm_fwd(kept_ref[b], vec(gain), vec(shift))
                normed2[rows_of(b), :] = normed.astype(BF)
                out_acc[rows_of(b), :] = kept_ref[b] + vec(proj_bias)
                grad_acc[rows_of(b), :] = jnp.zeros((ROWS, D), F32)

        if not sliced:
            load_all().wait()

    for load in loads(chunk):
        load.wait()

    @pl.when(chunk < UNITS - 1)
    def _():
        for load in loads(chunk + 1):
            load.start()

    slot = lax.rem(chunk, 2)
    if not sliced:
        for c in range(UNITS):

            @pl.when(chunk == c)
            def _(c=c):
                for f in range(frame_size):
                    at = (f * UNITS + c) * wide_step
                    fc_buf[slot, :, f * wide_step : f * wide_step + wide_step] = fc_all[:, at : at + wide_step]

    fc, proj = fc_buf.at[slot], proj_buf.at[slot]
    bias = bias_rows[pl.ds(chunk, 1), :]
    per_tile = 2 if frames % 2 == 0 else 1
    tiles = frames // per_tile

    def due(c, t, now, call):
        pl.when(jnp.logical_and(chunk == c, now == min(t, tiles - 1)))(call)

    def both(call, first):
        return lambda: pl.loop(first, first + 2)(call)

    def video():
        for unit in range(2):
            scatter.send_video(unit, MLP_PARTS[unit % 2], scatter.land(unit)[...])

    @pl.loop(0, tiles)
    def _(t):
        due(0, 2, t, place.meet)
        due(1, 1, t, both(lambda unit: scatter.stage(unit, 0), 0))
        due(2, 0, t, both(scatter.middle, 0))
        due(2, 1, t, both(lambda unit: scatter.stage(unit, 0), 2))
        due(2, 2, t, video)
        rows = rows_of(t, per_tile)
        hidden = dims(normed2[rows, :], fc[...], 1, 0) + bias
        grad_a = dims(cot2[rows, :], proj[...], 1, 1)
        gate = 0.5 * jnp.tanh(0.851 * hidden) + 0.5
        active = hidden * gate
        grad = (grad_a * (gate + 1.702 * active * (1.0 - gate))).astype(BF)
        active = active.astype(BF)
        act[rows, :] = active
        grad_h[rows, :] = grad
        bias_sums[pl.ds(chunk, 1), :] += column_sum(grad.astype(F32))
        out_acc[rows, :] += dims(active, proj[...], 1, 0)
        grad_acc[rows, :] += dims(grad, fc[...], 1, 1)

    unit = 2 * chunk

    def weight_grads(m):
        size = width // 2
        count = frame_size // 4
        value = dims(act[:, pl.ds(pl.multiple_of(m * size, size), size)], cot2[...], 0, 0).astype(BF)
        value = value.reshape(count, 2, 4, step, D)
        for core in range(2):
            for q in range(4):
                grads[
                    unit + 1, lax.rem(core + place.core, 2), pl.ds(m * count, count), :, q * D : q * D + D
                ] = value[:, core, q]
        size = D // 2
        value = dims(normed2[:, pl.ds(pl.multiple_of(m * size, size), size)], grad_h[...], 0, 0).astype(BF)
        value = value.reshape(count, 2, UNITS, step, width)
        for core in range(2):
            for q in range(UNITS):
                grads[
                    unit, lax.rem(core + place.core, 2), pl.ds(m * count, count), :, q * width : q * width + width
                ] = value[:, core, q]

    pl.loop(0, 2)(weight_grads)

    def raw():
        return pltpu.make_async_copy(grads.at[pl.ds(4, 2)], raw_hbm, s_raw.at[0])

    def source(unit):
        return grads.at[unit, 1]

    @pl.when(chunk == 0)
    def _():
        pl.loop(0, 2)(lambda unit: scatter.exchange0(unit, source(unit)).start())

    @pl.when(chunk == 1)
    def _():
        pl.loop(2, 4)(lambda unit: scatter.exchange0(unit, source(unit)).start())

    @pl.when(chunk == 2)
    def _():
        raw().start()
        both(scatter.middle, 2)()
        both(scatter.finish, 0)()
        for c in range(UNITS):
            for f in range(frame_size):
                at = (f * UNITS + c) * wide_step
                row, column = 2 + at // D, at % D
                sums[row : row + 1, column : column + wide_step] = bias_sums[
                    c : c + 1, f * wide_step : f * wide_step + wide_step
                ]

        @pl.loop(0, videos_here)
        def _(i):
            outs = [out_acc[rows_of(i * frames_here + j), :][:PATCHES] for j in range(frames_here)]
            cot_ref[i] = jnp.stack(outs, axis=1).astype(BF)
            every = frames_here * ROWS
            here = pl.ds(i * frames_here, frames_here)
            rows = rows_of(i, frames_here)
            _, unit, inv = norm_fwd(kept_ref[here].reshape(every, D), vec(gain), vec(shift))
            grad = grad_acc[rows, :]
            sums[0:1, :] += column_sum(grad * unit)
            sums[1:2, :] += column_sum(grad)
            grad = norm_back(grad, unit, inv, vec(gain)) + cot2[rows, :].astype(F32)
            grad_ref[here] = grad.reshape(frames_here, ROWS, D)
            for store in row_stores(i):
                store.start()

        @pl.loop(0, 2)
        def _(unit):
            mid_ref[unit] = scatter.land(2 + unit)[...]
            scatter.drain_video(unit)

        pl.loop(0, 4)(lambda unit: scatter.drain(unit, source(unit)))
        raw().wait()
        for n in range(videos_here):
            for store in row_stores(n):
                store.wait()


def attn_back_kernel(
    frame_size, video_size, videos_here, frames_here,
    x_hbm, normed_hbm, w_in_hbm, gk_hbm, mixed_hbm, msg_ref, gain, shift, w_out, mlp_sums, mid_ref, raw_hbm, cls_ref, *rest,
):
    msg_operands, rest = rest[:8], rest[8:]
    (
        q_ref, k_ref, v_ref, p_ref, inv_ref,
        tg_ref, reduced_ref, near_ref, far_ref, totals_ref, msg_ref_out, in_ref_out, out_ref_out, msg_sums, grad_cls,
        x_ref, normed_ref, w_in, gk_ref, mixed_ref, joined, staged, gqkv_all, gk_all, sums, gm_grads, gm_wide, gm_own, gm_rows, gm_all, wide, cls_grads,
        acc_mlp, *rest,
    ) = rest
    last_buffers, rest = rest[:6], rest[6:]
    (acc_near, *near_buffers), rest = rest[:7], rest[7:]
    (acc_far, *far_buffers), rest = rest[:7], rest[7:]
    (vec_near, vec_mid, vec_far), rest = rest[:3], rest[3:]
    msg_kept, (msg_gqkv, msg_mixed), msg_state, rest = list(rest[:7]), rest[7:9], rest[9:15], rest[15:]
    msg_kept.insert(6, gqkv_all.at[0:D])
    (s_rows, s_late, s_msg, s_local, s_staged, s_vsend, s_vrecv, s_gsend, s_grecv), rest = rest[:9], rest[9:]
    names = ("send0", "recv0", "send_bits", "recv_bits", "send3", "recv3")
    last_sems, near_sems, far_sems = (dict(zip(names, rest[6 * i : 6 * i + 6])) for i in range(3))
    frames = videos_here * frames_here
    steps = 2 * frames
    t = pl.program_id(0)
    side, b = lax.div(t, frames), lax.rem(t, frames)
    place = Place(frame_size, video_size)
    step = D // frame_size // UNITS
    total = frames * ROWS
    each_mid, each_last, each_attn = pl.loop(0, 2), pl.loop(2, 4), pl.loop(0, UNITS)

    def scatter(acc, buffers, result, sems, first=0):
        recv0, recv_a, recv_b, recv_c, send3, recv3 = buffers
        return Scatter(place, step, acc, recv0, [recv_a, recv_b, recv_c], send3, recv3, result, sems, first)

    lasts = scatter(lambda unit, block: acc_mlp.at[unit - 2, block], last_buffers, reduced_ref, last_sems, first=2)
    near = scatter(lambda unit, block: acc_near.at[0, unit, block], near_buffers, near_ref, near_sems)
    far = scatter(lambda unit, block: acc_far.at[0, unit, block], far_buffers, far_ref, far_sems)
    vec_sems = dict(vec_send=s_vsend, vec_recv=s_vrecv)
    early = Totals(place, 0, mlp_sums, vec_near, vec_mid, vec_far, totals_ref, vec_sems)
    late = Totals(place, 1, sums, vec_near, vec_mid, vec_far, totals_ref, vec_sems)
    gather = Gather(place, gm_own, gm_rows, s_gsend, s_grecv)

    def last_source(unit):
        return raw_hbm.at[unit - 2, 1]

    def local(unit):
        return pltpu.make_async_copy(raw_hbm.at[unit - 2, 0], acc_mlp.at[unit - 2], s_local.at[unit - 2])

    def msg_loads():
        return [pltpu.make_async_copy(a, b, s_msg.at[i]) for i, (a, b) in enumerate(zip(msg_operands, msg_kept))]

    def row_loads(c):
        return [
            pltpu.make_async_copy(gk_hbm.at[c], gk_ref.at[c], s_rows.at[0, c]),
            pltpu.make_async_copy(mixed_hbm.at[c], mixed_ref.at[c], s_rows.at[1, c]),
        ]

    def late_loads():
        out = [
            pltpu.make_async_copy(x_hbm, x_ref, s_late.at[0]), pltpu.make_async_copy(normed_hbm, normed_ref, s_late.at[1]),
        ]
        for half_at in range(2):
            for kind in range(3):
                source = w_in_hbm.at[:, kind * D + half_at * HALF : kind * D + half_at * HALF + HALF]
                at = (half_at * 3 + kind) * HALF
                out.append(pltpu.make_async_copy(source, w_in.at[:, at : at + HALF], s_late.at[2 + half_at * 3 + kind]))
        return out

    def due(at, call):
        pl.when(t == min(at, steps - 1))(call)

    def begin():
        place.announce()

        @pl.loop(0, frames)
        def _(c):
            for load in row_loads(c):
                load.start()

        sums[...] = jnp.zeros_like(sums)
        each_last(lambda unit: local(unit).start())
        for load in late_loads():
            load.start()
        for at, load in enumerate(msg_loads()):
            if at != 6:
                load.start()

    def begin_far():
        place.meet()
        each_last(lambda unit: lasts.exchange0(unit, last_source(unit)).start())
        early.start()
        for unit in range(2):
            lasts.send_video(unit, MLP_PARTS[unit], mid_ref[unit])

    def open_lasts():
        @each_last
        def _(unit):
            local(unit).wait()
            lasts.stage(unit, 0)

    def land_lasts():
        for unit in (2, 3):
            lasts.send_video(unit, MLP_PARTS[unit % 2], lasts.land(unit)[...])

    def land(scatter, group):
        @each_attn
        def _(unit):
            scatter.send_video(unit, attn_parts(group), scatter.land(unit)[...])

    due(0, begin)
    rows = pl.ds(pl.multiple_of(b * ROWS, ROWS), ROWS)
    side_lanes = pl.ds(pl.multiple_of(side * HALF, HALF), HALF)

    @pl.when(side == 0)
    def _():
        for load in row_loads(b):
            load.wait()
        gk_low = gk_ref[b].astype(BF)
        gk_all[b] = gk_low
        sums[0:1, :] += column_sum(gk_low.astype(F32))

    grad_mixed = dims(gk_all[b], w_out[side_lanes, :], 1, 1)
    for pair in range(PAIRS // 2):
        grads = pair_back(
            q_ref[0, pair], k_ref[0, pair], v_ref[0, pair], grad_mixed[:, lanes(pair)],
            mixed_ref[b, :, pl.ds(pl.multiple_of(side * HALF + pair * 128, 128), 128)], inv_ref[0, pair],
            lambda head, pair=pair: p_ref[0, pair, :, head * KEYS : head * KEYS + KEYS],
        )
        for kind in range(3):
            at = pl.ds(pl.multiple_of((side * 3 + kind) * HALF + pair * 128, 128), 128)
            gqkv_all[rows, at] = grads[kind][:ROWS].astype(BF)
    due(0, begin_far)
    due(1, open_lasts)
    due(3, lambda: each_mid(lasts.finish))
    due(4, early.forward)
    due(5, lambda: each_last(lasts.middle))
    due(7, land_lasts)
    due(frames + 1, lambda: each_attn(lambda unit: near.stage(unit, 0)))
    for row, kind in ((1, 0), (2, 2)):
        part = gqkv_all[rows, pl.ds(pl.multiple_of((side * 3 + kind) * HALF, HALF), HALF)]
        sums[row : row + 1, side_lanes] += column_sum(part.astype(F32))

    def attn_unit(m, target, left, right, lo):
        size, width = D // 2, right.shape[1]
        value = dims(left[:, :, pl.ds(pl.multiple_of(m * size, size), size)].reshape(total, size), right, 0, 0).astype(BF)
        count = frame_size // 4
        value = value.reshape(count, 2, UNITS, step, width)
        for u in range(UNITS):
            for core in range(2):
                target[lax.rem(core + place.core, 2), u, pl.ds(m * count, count), :, lo : lo + width] = value[:, core, u]

    def attn_units(group, target, scatter):
        @pl.loop(0, 2)
        def _(m):
            attn_unit(m, target, normed_ref, gqkv_all[0:total, group * 3 * HALF : (group + 1) * 3 * HALF], 0)
            if group == 0:
                attn_unit(m, target, mixed_ref, gk_all[...].reshape(total, D), 3 * HALF)

        each_attn(lambda unit: scatter.exchange0(unit, target.at[1, unit]).start())

    @pl.when(t == frames - 1)
    def _():
        for load in late_loads():
            load.wait()
        attn_units(0, acc_near, near)

    @pl.when(t == steps - 1)
    def _():
        at = JOINED - 1 - (JOINED - 1) % 16
        gm_grads[...] = jnp.zeros_like(gm_grads)
        for c in range(frames):
            piece = gqkv_all[c * ROWS + at : c * ROWS + at + 16, :].astype(F32)
            gm_grads[c : c + 1, :] = piece[PATCHES - at : PATCHES - at + 1]
            joined[0, c : c + 1, :] = msg_ref[c]
        _, unit, inv = norm_fwd(joined[0, 0:frames, :], vec(gain), vec(shift))
        grad = dims(gm_grads[...].astype(BF), w_in[...], 1, 1)[0:frames]
        gm_wide[0:frames, :] = norm_back(grad, unit, inv, vec(gain))
        for i in range(videos_here):
            gm_own[i] = gm_wide[i * frames_here : i * frames_here + frames_here, :].astype(BF)
            gm_rows[place.v, i, place.f] = gm_own[i]
        gather.start()
        each_attn(near.middle)
        attn_units(1, acc_far, far)
        each_last(lasts.finish)
        early.finish()
        gather.near()
        gather.forward()

        def put(i, j):
            return pltpu.make_async_copy(staged.at[j], tg_ref.at[i, :, j], s_staged.at[j])

        def norm_frames(lo, hi):
            @pl.loop(lo, hi)
            def _(i):
                @pl.when(i > 0)
                def _():
                    for j in range(frames_here):
                        put(i - 1, j).wait()

                x = x_ref[i].astype(F32)
                first = i * frames_here
                for j in range(frames_here):
                    joined[j, 0:PATCHES, :] = x[:, j, :]
                    joined[j, PATCHES:ROWS, :] = jnp.zeros((ROWS - PATCHES, D), F32)
                    joined[j, PATCHES : PATCHES + 1, :] = msg_ref[first + j]
                every = frames_here * ROWS
                rows = pl.ds(pl.multiple_of(first * ROWS, ROWS), every)
                grad = dims(gqkv_all[rows, :], w_in[...], 1, 1)
                _, unit, inv = norm_fwd(joined[...].reshape(every, D), vec(gain), vec(shift))
                sums[3:4, :] += column_sum(grad * unit)
                sums[4:5, :] += column_sum(grad)
                back = gk_ref[pl.ds(first, frames_here)].reshape(every, D) + norm_back(grad, unit, inv, vec(gain))
                for j in range(frames_here):
                    staged[j] = back[j * ROWS : j * ROWS + PATCHES]
                    put(i, j).start()

        norm_frames(0, 1)
        each_attn(lambda unit: far.stage(unit, 0))
        land(near, 0)
        norm_frames(1, videos_here)
        msg_loads()[6].start()
        late.start()
        each_attn(far.middle)
        each_attn(near.finish)
        for load in msg_loads():
            load.wait()
        for ref in (msg_sums, msg_ref_out, in_ref_out, out_ref_out):
            ref[...] = jnp.zeros_like(ref)
        count = videos_here * FRAMES

        def between():
            land(far, 1)
            late.forward()
            gather.finish()
            for video in range(video_size):
                for i in range(videos_here):
                    for f in range(frame_size):
                        at_row = (i * frame_size + f) * frames_here
                        wide[at_row : at_row + frames_here, :] = gm_rows[video, i, f].astype(F32)
                gm_all[video * count : video * count + count, :] = wide[...].astype(BF)

        def after():
            pass

        blocks = video_size * count // BLOCK
        if blocks > 1:
            between()
            after()

        @pl.loop(0, blocks)
        def _(block):
            at = pl.ds(pl.multiple_of(block * BLOCK, BLOCK), BLOCK)
            msg_back_block(
                place, cls_ref[at, :], gm_all.at[at], msg_kept, msg_ref_out, in_ref_out, out_ref_out, msg_sums, cls_grads.at[at],
                msg_state, msg_gqkv, msg_mixed, *((between, after) if blocks == 1 else (lambda: None,) * 2),
            )

        for i in range(videos_here):
            for j in range(frames_here):
                row = (place.v * videos_here + i) * FRAMES + place.f * frames_here + j
                grad_cls[i * frames_here + j] = cls_grads[pl.ds(row, 1), :]
        for j in range(frames_here):
            put(videos_here - 1, j).wait()
        late.finish()
        each_attn(far.finish)
        each_last(lambda unit: lasts.drain(unit, last_source(unit)))
        pl.loop(0, 4)(lasts.drain_video)

        @each_attn
        def _(unit):
            for scatter, target in ((near, acc_near), (far, acc_far)):
                scatter.drain(unit, target.at[1, unit])
                scatter.drain_video(unit)


def msg_back_block(place, cls, gm_ref, kept, acc_msg, acc_in, acc_out, sums, cls_grad, scratch, gqkv, grad_mixed, between, after):
    bias, gain, shift, in_bias, out_bias, w_msg, w_in, w_out = kept
    qkv, probs, invs, mixed, normed, _ = scratch
    own_rows = D // place.F
    padded = acc_msg.shape[0]

    def own_columns(x):
        return pltpu.roll(x.astype(F32), lax.rem(D - place.f * own_rows, D), 1)[:, :padded].astype(BF)

    unit, inv_std = msg_forward(cls, (bias, gain, shift, in_bias, out_bias), w_msg, w_in, w_out, scratch, PAIRS)
    between()
    gm = gm_ref[...]
    acc_out[...] += dims(own_columns(mixed[...]), gm, 0, 0)
    sums[5:6, :] += column_sum(gm.astype(F32))
    grad_mixed[...] = dims(gm, w_out[...], 1, 1)

    @pl.loop(0, PAIRS, unroll=PAIRS)
    def _(pair):
        at = pair_lanes(pair)
        grads = pair_back(
            qkv[:, at], qkv[:, pair_lanes(pair, 1)], qkv[:, pair_lanes(pair, 2)], grad_mixed[:, at],
            mixed[:, at], invs[:, at], lambda head: probs[2 * pair + head],
        )
        for kind in range(3):
            gqkv[:, pair_lanes(pair, kind)] = grads[kind].astype(BF)

    after()
    own_normed = own_columns(normed[...])
    grad = None
    for kind in range(3):
        columns = slice(kind * D, kind * D + D)
        part = gqkv[:, columns]
        acc_in[:, columns] += dims(own_normed, part, 0, 0)
        if kind != 1:
            row = 3 + kind // 2
            sums[row : row + 1, :] += column_sum(part.astype(F32))
        term = dims(part, w_in[:, columns], 1, 1)
        grad = term if grad is None else grad + term
    sums[1:2, :] += column_sum(grad * unit)
    sums[2:3, :] += column_sum(grad)
    grad_message = norm_back(grad, unit, inv_std, vec(gain)) + gm.astype(F32)
    grad_message = grad_message.astype(BF)
    acc_msg[...] += dims(own_columns(cls), grad_message, 0, 0)
    sums[0:1, :] += column_sum(grad_message.astype(F32))
    cls_grad[...] = dims(grad_message, w_msg[...], 1, 1)


def collect_kernel(
    frame_size, video_size, videos_here, frames_here,
    *rest,
):
    small, (tg_hbm, output_hbm, output, tokens_grad, *rest) = rest[:10], rest[10:]
    collect(frame_size, video_size, videos_here, frames_here, small, tg_hbm, output_hbm, output, tokens_grad, *rest)


def collect(
    frame_size, video_size, videos_here, frames_here, small, tg_hbm, output_hbm, output, tokens_grad, msg_grad, in_grad, out_grad, *rest,
):
    (
        msg_bias_g, msg_gain_g, msg_shift_g, msg_in_bias_g, msg_out_bias_g, gain1_g, shift1_g,
        attn_in_g, attn_in_bias_g, attn_out_g, attn_out_bias_g, gain2_g, shift2_g, fc_g, fc_bias_g, proj_g, proj_bias_g,
        tg, out, sem, s_small, *kept,
    ) = rest
    f, v = lax.axis_index("frame"), lax.axis_index("video")
    own_rows = D // frame_size

    def load(i):
        return pltpu.make_async_copy(tg_hbm.at[i], tg.at[i], sem.at[0, i])

    def store(i):
        return pltpu.make_async_copy(tg.at[i], tokens_grad.at[i], sem.at[0, i])

    def load_out(i):
        return pltpu.make_async_copy(output_hbm.at[i], out.at[i], sem.at[1, i])

    def store_out(i):
        return pltpu.make_async_copy(out.at[i], output.at[i], sem.at[1, i])

    for i in range(videos_here):
        load(i).start()
        load_out(i).start()
    smalls = [pltpu.make_async_copy(a, b, s_small.at[at]) for at, (a, b) in enumerate(zip(small, kept))]
    for copy in smalls:
        copy.start()
    for copy in smalls:
        copy.wait()
    done, reduced, near, far, totals, acc_msg, acc_in, acc_out, sums, grad_cls = kept
    for i in range(videos_here):
        load(i).wait()
        added = [grad_cls[i * frames_here + j] for j in range(frames_here)]
        tg[i, 0] = tg[i, 0] + jnp.concatenate(added, axis=0)
        store(i).start()
        load_out(i).wait()
        store_out(i).start()

    def own_matrix(target, x):
        size = x.shape[1] // video_size
        target[...] = pltpu.roll(x[:own_rows], lax.rem(x.shape[1] - v * size, x.shape[1]), 1)[:, :size]

    own_matrix(msg_grad, acc_msg[...])
    own_matrix(in_grad, acc_in[...])
    own_matrix(out_grad, acc_out[...])

    def own_vector(target, ref, first, count):
        size = count * D // frame_size
        per_row = frame_size // count
        row = first + lax.div(f, per_row)
        x = ref[pl.ds(row, 1), :]
        x = pltpu.roll(jnp.broadcast_to(x, (8, D)), lax.rem(D - lax.rem(f, per_row) * size, D), 1)
        target[...] = x[0:1, :size].reshape(size)

    mlp_sums, attn_sums = totals.at[0], totals.at[1]
    for target, ref, first, count in (
        (msg_bias_g, sums, 0, 1), (msg_gain_g, sums, 1, 1), (msg_shift_g, sums, 2, 1), (msg_in_bias_g, sums, 3, 2),
        (msg_out_bias_g, sums, 5, 1), (gain1_g, attn_sums, 3, 1), (shift1_g, attn_sums, 4, 1),
        (attn_in_bias_g, attn_sums, 1, 2), (attn_out_bias_g, attn_sums, 0, 1), (gain2_g, mlp_sums, 0, 1),
        (shift2_g, mlp_sums, 1, 1), (fc_bias_g, mlp_sums, 2, 4), (proj_bias_g, mlp_sums, 6, 1),
    ):
        own_vector(target, ref, first, count)
    step = own_rows // UNITS
    columns = D // video_size
    wide_step = 4 * step
    part = FF // UNITS // video_size
    fc = [done[0], reduced[0], reduced[2]]
    for c in range(UNITS):
        for q in range(UNITS):
            for g in range(frame_size // video_size):
                from_at = q * part + g * wide_step
                to = (g * UNITS + c) * wide_step
                fc_g[q * step : q * step + step, to : to + wide_step] = fc[c][:, from_at : from_at + wide_step]
    for u in range(UNITS):
        rows = slice(u * step, u * step + step)
        attn_out_g[rows, :] = near[u][:, in_width(video_size) :]
        for w in range(video_size):

            @pl.when(v == w)
            def _(rows=rows, u=u, w=w):
                for group, parts in enumerate((near, far)):
                    at = 0
                    for _, count, to in in_pieces(group, w, video_size):
                        attn_in_g[rows, to : to + count] = parts[u][:, at : at + count]
                        at += count

    proj = [done[1], reduced[1], reduced[3]]
    proj = [x[:, q * columns : q * columns + columns] for x in proj for q in range(4)]
    proj_g[...] = jnp.concatenate(proj, axis=0).T
    for i in range(videos_here):
        store(i).wait()
        store_out(i).wait()


def shaped(shape, dtype):
    return jax.ShapeDtypeStruct(shape, dtype)


def whole(array):
    shape = array.shape
    return pl.BlockSpec(shape, lambda *_: (0,) * len(shape), pipeline_mode=pl.Buffered(1))


def wholes(*arrays):
    return [whole(array) for array in arrays]


def in_hbm():
    return pl.BlockSpec(memory_space=pl.ANY)


def in_vmem():
    return pl.BlockSpec(memory_space=pltpu.VMEM)


def per_step(count, shape):
    return pl.BlockSpec((count,) + shape, lambda b: (b,) + (0,) * len(shape))


def params(mib, **more):
    return pltpu.CompilerParams(vmem_limit_bytes=mib * MIB, **more)


def on_device(frame_size, video_size, *args):
    (
        tokens, cotangent, msg_weight, msg_bias, msg_norm_gain, msg_norm_shift, msg_in_weight,
        msg_in_bias, msg_out_weight, msg_out_bias, norm1_gain, norm1_shift, attn_in_weight,
        attn_in_bias, attn_out_weight, attn_out_bias, norm2_gain, norm2_shift, fc_weight, fc_bias,
        proj_weight, proj_bias,
    ) = args
    videos_here, frames_here = tokens.shape[:2]
    frames = videos_here * frames_here
    msgs = videos_here * video_size * FRAMES
    group = videos_here * FRAMES
    total = frames * ROWS
    F, V = frame_size, video_size
    step = D // F // UNITS
    n_bits = int(math.log2(F)) - 1
    x = tokens.transpose(0, 2, 1, 3)
    cot = cotangent.transpose(0, 2, 1, 3)
    msg_vectors = (msg_bias, msg_norm_gain, msg_norm_shift, msg_in_bias, msg_out_bias)
    DMA = pltpu.SemaphoreType.DMA

    msg_arrays = (*msg_vectors, msg_weight, msg_in_weight, msg_out_weight)
    kv_shape = (frames, PAIRS, KEYS, 128)

    def second(shape):
        zeros = (0,) * len(shape)
        return pl.BlockSpec((frames_here,) + shape, lambda t: (jnp.maximum(t - videos_here, 0),) + zeros)

    block_shapes = [(PAIRS, ROWS, 2 * KEYS), (PAIRS, ROWS, 128), (ROWS, D), (ROWS, D)]
    fwd_outs = [
        shaped((frames, PAIRS, ROWS, 128), BF), shaped(kv_shape, BF), shaped(kv_shape, BF), shaped((frames, ROWS, D), BF),
        shaped((frames,) + block_shapes[0], BF), shaped((frames,) + block_shapes[1], F32),
        shaped((frames,) + block_shapes[2], BF), shaped((frames,) + block_shapes[3], F32),
        shaped((frames, 1, D), F32), shaped((msgs, D), BF),
    ]
    q, k, v, normed, p, inv, mixed, kept, msg_out, cls = pl.pallas_call(
        functools.partial(attn_fwd_kernel, F, V, frames_here, videos_here),
        grid=(2 * videos_here,),
        in_specs=[
            pl.BlockSpec((1, PATCHES, frames_here, D), lambda t: (jnp.minimum(t, videos_here - 1), 0, 0, 0)), in_hbm(),
        ]
        + wholes(norm1_gain, norm1_shift, attn_in_bias, attn_out_bias, attn_in_weight) + [in_hbm()] * 9,
        out_specs=[in_hbm()] * 4 + [second(shape) for shape in block_shapes] + wholes(*fwd_outs[8:]),
        out_shape=fwd_outs,
        scratch_shapes=[pltpu.VMEM(out.shape, BF) for out in fwd_outs[:4]]
        + [
            pltpu.VMEM((frames, ROWS, D), F32), pltpu.VMEM((D, D), BF),
            pltpu.VMEM((16, D), F32), pltpu.VMEM((16, 3 * D), F32),
            pltpu.VMEM((videos_here, frames_here, D), BF),
            pltpu.VMEM((V, videos_here, F, frames_here, D), BF),
            pltpu.VMEM((group, D), F32), pltpu.VMEM((group, D), F32),
        ]
        + [pltpu.VMEM(a.shape, BF) for a in msg_arrays]
        + msg_scratch(group) + [DMA((V, F + V)), DMA((V, F + V)), DMA((11,)), DMA((4,))],
        compiler_params=params(63, collective_id=1, has_side_effects=True),
        name="attn_fwd",
    )(x, x, norm1_gain, norm1_shift, attn_in_bias, attn_out_bias, attn_in_weight, attn_out_weight, *msg_arrays)

    def bit_buffers(units, width=FF):
        return [
            pltpu.VMEM((units, max(1, F >> (2 + i)), step, width), BF) if i < n_bits else pltpu.VMEM((1, 1, 16, 128), BF)
            for i in range(3)
        ]

    def exchange_sems(units):
        return [DMA((units,)), DMA((units,)), DMA((units, n_bits, F // 4)), DMA((units, n_bits, F // 4)), DMA((units, V)), DMA((units, V))]

    def unit_buffers(count, units):
        return [pltpu.VMEM((count,) + shape, BF) for shape in units]

    block_shape = (F // 2, step, FF)
    part_shape = (V, step, FF // V)
    width = FF // UNITS
    mlp_outs = [
        shaped(x.shape, BF), shaped(kept.shape, F32), shaped((2, step, FF // V), F32), shaped((2, step, FF), BF),
        shaped((2, 2) + block_shape, BF), shaped((8, D), F32),
    ]
    output, grad_kept, done, mid, raw, mlp_sums = pl.pallas_call(
        functools.partial(mlp_kernel, F, V, videos_here, frames_here),
        grid=(UNITS,),
        in_specs=[in_hbm()] * 2 + wholes(norm2_gain, norm2_shift, fc_bias, proj_bias) + [in_hbm()] * 2,
        out_specs=[in_hbm()] * 2 + wholes(*mlp_outs[2:4]) + [in_hbm()] + wholes(mlp_outs[5]),
        out_shape=mlp_outs,
        scratch_shapes=[
            pltpu.VMEM(kept.shape, F32), pltpu.VMEM(x.shape, BF), pltpu.VMEM(kept.shape, F32),
            pltpu.VMEM((frames_here, ROWS, D), F32),
            pltpu.VMEM((total, D), BF), pltpu.VMEM((total, D), BF), pltpu.VMEM((total, width), BF), pltpu.VMEM((total, width), BF),
            pltpu.VMEM((total, D), F32), pltpu.VMEM((total, D), F32),
            pltpu.VMEM((UNITS, width), F32), pltpu.VMEM((UNITS, width), F32),
            pltpu.VMEM((2, D, width), BF), pltpu.VMEM((2, width, D), BF),
            pltpu.VMEM((D, FF) if 4 * step % 128 else (16, 128), BF),
            pltpu.VMEM((2 * UNITS, 2) + block_shape, BF), pltpu.VMEM((4,) + block_shape, BF),
        ]
        + bit_buffers(4) + unit_buffers(2, [part_shape] * 2)
        + [DMA((2, videos_here)), DMA((2, 2, F)), DMA((1,))] + exchange_sems(4),
        compiler_params=params(63, collective_id=2, has_side_effects=True),
        name="mlp",
    )(kept, cot, norm2_gain, norm2_shift, fc_bias, proj_bias, fc_weight, proj_weight)

    rows_own, columns = D // F, D // V
    padded = -(-rows_own // 128) * 128
    widths = (3 * HALF + D, 3 * HALF)
    part_widths = (in_width(V) + columns, in_width(V))
    back_outs = [
        shaped(x.shape, F32), shaped((4, step, FF // V), F32), shaped((UNITS, step, part_widths[0]), F32),
        shaped((UNITS, step, part_widths[1]), F32), shaped((2, 8, D), F32),
        shaped((padded, D), F32), shaped((padded, 3 * D), F32), shaped((padded, D), F32), shaped((8, D), F32),
        shaped((frames, 1, D), F32),
    ]
    def group_buffers(width, part_width):
        block = (F // 2, step, width)
        return [pltpu.VMEM((2, UNITS) + block, BF), pltpu.VMEM((UNITS,) + block, BF)] + bit_buffers(UNITS, width) + [
            pltpu.VMEM((UNITS, V, step, part_width), BF)
        ] * 2

    def by_pairs(shape):
        return pl.BlockSpec((1, PAIRS // 2) + shape, lambda t: (lax.rem(t, frames), lax.div(t, frames), 0, 0))

    tg, reduced, near, far, totals, acc_msg, acc_in, acc_out, msg_sums, grad_cls = pl.pallas_call(
        functools.partial(attn_back_kernel, F, V, videos_here, frames_here),
        grid=(2 * frames,),
        in_specs=[in_hbm()] * 5
        + wholes(msg_out, norm1_gain, norm1_shift, attn_out_weight, mlp_sums, mid)
        + [in_hbm()] + wholes(cls) + [in_hbm()] * 8
        + [by_pairs(shape) for shape in ((ROWS, 128), (KEYS, 128), (KEYS, 128), (ROWS, 2 * KEYS), (ROWS, 128))],
        out_specs=[in_hbm()] + wholes(*back_outs[1:]),
        out_shape=back_outs,
        scratch_shapes=[
            pltpu.VMEM(x.shape, BF), pltpu.VMEM(normed.shape, BF), pltpu.VMEM((D, 3 * D), BF),
            pltpu.VMEM(grad_kept.shape, F32), pltpu.VMEM(mixed.shape, BF),
            pltpu.VMEM((frames_here, ROWS, D), F32), pltpu.VMEM((frames_here, PATCHES, D), F32),
            pltpu.VMEM((max(total, D), 3 * D), BF), pltpu.VMEM((frames, ROWS, D), BF), pltpu.VMEM((8, D), F32), pltpu.VMEM((16, 3 * D), F32), pltpu.VMEM((8, D), F32),
            pltpu.VMEM((videos_here, frames_here, D), BF), pltpu.VMEM((V, videos_here, F, frames_here, D), BF),
            pltpu.VMEM((msgs, D), BF), pltpu.VMEM((group, D), F32), pltpu.VMEM((msgs, D), F32),
            pltpu.VMEM((2,) + block_shape, BF), pltpu.VMEM((2,) + block_shape, BF),
        ]
        + bit_buffers(2) + unit_buffers(4, [part_shape] * 2)
        + group_buffers(widths[0], part_widths[0]) + group_buffers(widths[1], part_widths[1])
        + [pltpu.VMEM((2, F, 8, D), F32), pltpu.VMEM((2, 8, D), F32), pltpu.VMEM((2, V, 8, D), F32)]
        + [pltpu.VMEM(a.shape, BF) for a in msg_arrays if a is not msg_in_weight]
        + [pltpu.VMEM((BLOCK, 3 * D), BF), pltpu.VMEM((BLOCK, D), F32)] + msg_scratch(BLOCK)
        + [DMA((2, frames)), DMA((8,)), DMA((8,)), DMA((2,)), DMA((frames_here,))]
        + [DMA((2, 2, max(F, V))), DMA((2, 2, max(F, V))), DMA((V, F + V)), DMA((V, F + V))]
        + exchange_sems(4) + exchange_sems(UNITS) + exchange_sems(UNITS),
        compiler_params=params(63, collective_id=3, has_side_effects=True),
        name="attn_back",
    )(
        x, normed, attn_in_weight, grad_kept, mixed, msg_out, norm1_gain, norm1_shift, attn_out_weight, mlp_sums, mid, raw, cls,
        *msg_arrays, q, k, v, p, inv,
    )

    out_shapes = [
        (rows_own, columns), (rows_own, 3 * columns), (rows_own, columns),
        (rows_own,), (rows_own,), (rows_own,), (2 * rows_own,), (rows_own,), (rows_own,), (rows_own,),
        (rows_own, 3 * columns), (2 * rows_own,), (rows_own, columns), (rows_own,), (rows_own,), (rows_own,),
        (rows_own, 4 * columns), (4 * rows_own,), (columns, 4 * rows_own), (rows_own,),
    ]
    out_shapes = [shaped(shape, F32) for shape in out_shapes]
    (
        output, tokens_grad, msg_grad, msg_in_grad, msg_out_grad,
        msg_bias_g, msg_gain_g, msg_shift_g, msg_in_bias_g, msg_out_bias_g, gain1_g, shift1_g,
        attn_in_g, attn_in_bias_g, attn_out_g, attn_out_bias_g, gain2_g, shift2_g, fc_g, fc_bias_g, proj_g, proj_bias_g,
    ) = pl.pallas_call(
        functools.partial(collect_kernel, F, V, videos_here, frames_here),
        grid=(1,),
        in_specs=[in_hbm()] * 12,
        out_specs=[in_hbm()] * 2 + wholes(*out_shapes),
        out_shape=[shaped(x.shape, BF), shaped(x.shape, F32)] + out_shapes,
        scratch_shapes=[pltpu.VMEM(x.shape, F32), pltpu.VMEM(x.shape, BF), DMA((2, videos_here)), DMA((10,))]
        + [pltpu.VMEM(a.shape, F32) for a in (done, reduced, near, far, totals, acc_msg, acc_in, acc_out, msg_sums, grad_cls)],
        compiler_params=params(63),
        name="collect",
    )(done, reduced, near, far, totals, acc_msg, acc_in, acc_out, msg_sums, grad_cls, tg, output)

    return (
        output.transpose(0, 2, 1, 3), tokens_grad.transpose(0, 2, 1, 3),
        msg_grad, msg_bias_g, msg_gain_g, msg_shift_g, msg_in_grad, msg_in_bias_g, msg_out_grad, msg_out_bias_g,
        gain1_g, shift1_g, attn_in_g, attn_in_bias_g, attn_out_g, attn_out_bias_g,
        gain2_g, shift2_g, fc_g, fc_bias_g, proj_g.T, proj_bias_g,
    )


def solution(mesh):
    rows = P("video", "frame", None, None)
    matrix, vector = P("frame", "video"), P("frame")
    out_specs = (
        rows, rows,
        matrix, vector, vector, vector, matrix, vector, matrix, vector,
        vector, vector, matrix, vector, matrix, vector,
        vector, vector, matrix, vector, matrix, vector,
    )
    return jax.shard_map(
        functools.partial(on_device, mesh.shape["frame"], mesh.shape["video"]),
        mesh=mesh, in_specs=(rows, rows) + (P(),) * 20, out_specs=out_specs, check_vma=False,
    )
```
